32 devices in a mesh: rep: 2 (over x), wide: 16 (over z, y, core).
Axes of the slice: x: 2, y: 2, z: 4, core: 2. Of those that a mesh axis runs over, the one named last changes fastest.
Arguments:
- prompt_hidden: bfloat16 [4096, 8192], P(('rep', 'wide')), parts along dimension 0, may hold values from -6 to 6
- resident_latent: bfloat16 [64, 1024, 256], P(('rep', 'wide')), parts along dimension 0, may hold values from -6 to 6
- row_target: int32 [4096], P(('rep', 'wide')), parts along dimension 0, may hold values from 0 to 31, as said below
- row_offset: int32 [4096], P(('rep', 'wide')), parts along dimension 0, may hold values from 0 to 1023, as said below
- context_len: int32 [64], P(('rep', 'wide')), parts along dimension 0, may hold values from 1 to 1024, as said below
- draft_hidden: bfloat16 [64, 4, 8192], P(('rep', 'wide')), parts along dimension 0, may hold values from -6 to 6
- draft_query_heads: bfloat16 [64, 4, 8192], P(('rep', 'wide')), parts along dimension 0, may hold values from -60 to 60
- down_weight: bfloat16 [8192, 256], P('wide'), may hold values from -0.0625 to 0.0625
- key_up_weight: bfloat16 [256, 1024], replicated, may hold values from -0.375 to 0.375
- value_up_weight: bfloat16 [256, 1024], replicated, may hold values from -0.375 to 0.375
Outputs:
- attended: bfloat16 [64, 4, 8192], P(('rep', 'wide')), parts along dimension 0
The draws below stay inside these ranges and needn't reach their ends.
There are 2 independent parts, one for each index of `rep`. The reference program is written for one: setup_inputs(seed, part) draws one part's arguments, and reference() takes and returns one part's arrays. A program takes and returns all parts, laid end to end along the dimension named above; an argument that names none is the same for every part. Nothing has to cross between parts.
Inputs may be any that keep to these rules, and one draw needn't show every extreme that they name: row_target // 2 is the device that decodes the request; the rows held by one device name any one such device at most 16 times and some device exactly 16 times. `row_offset`: the rows of one request take distinct positions that, after its resident rows, fill positions up to context_len of that request exactly: a request with k prompt rows has its resident rows at positions below context_len - k. `context_len`: at least the number of prompt rows of the request.
All inputs are finite; a program needn't handle non-finite values.
Results may differ from the reference program's by a relative error of at most 0.0062.
Values may be sent and summed in bfloat16 or wider, within the bound.
No kernel may reach another device: no remote copies, remote signals or barrier semaphores. Data moves between devices by JAX's collectives and lax.ppermute only.
A program may use at most 128 MiB of HBM per device.

```python
import math
import jax
import jax.numpy as jnp
from jax import lax

D = 8192
QUERY_HEADS = 64
KEY_VALUE_HEADS = 8
HEAD_SIZE = 128
LATENT_RANK = 256
CTX = 1024
DRAFT_TOKENS = 4
ROWS = 128
BATCH_REQUESTS = 2
MOST = 16
TOTAL_ROWS = 2048
REQUESTS = 32
N_WIDE = 16


def plan_rows(key):
    wide_size = N_WIDE
    subkeys = jax.random.split(key, 6)
    hot_device = jax.random.randint(subkeys[0], (wide_size,), 0, wide_size)
    rotation = jax.random.randint(subkeys[1], (wide_size,), 0, wide_size - 1)
    slot_index = jnp.arange(ROWS, dtype=jnp.int32)
    others = (hot_device[:, None] + 1 + (slot_index[None, :] + rotation[:, None]) % (wide_size - 1)) % wide_size
    device = jnp.where(slot_index[None, :] < MOST, hot_device[:, None], others)
    shuffle = jax.vmap(lambda sub_key: jax.random.permutation(sub_key, ROWS))(jax.random.split(subkeys[2], wide_size))
    device = jnp.take_along_axis(device, shuffle, axis=1)
    member = jax.random.randint(subkeys[3], (wide_size, ROWS), 0, BATCH_REQUESTS)
    target = (device * BATCH_REQUESTS + member).reshape(-1).astype(jnp.int32)
    request_count = wide_size * BATCH_REQUESTS
    arrived = jax.ops.segment_sum(jnp.ones_like(target), target, request_count)
    spare_rows = jax.random.randint(subkeys[4], (request_count,), 0, CTX - wide_size * MOST + 1)
    keep_flag = jax.random.randint(subkeys[5], (request_count,), 0, 2)
    spare_rows = (spare_rows * keep_flag).at[0].set(0)
    length = (CTX - spare_rows).astype(jnp.int32)
    ordering = jnp.argsort(target, stable=True)
    ordered = target[ordering]
    group_start = jnp.searchsorted(ordered, ordered, side='left').astype(jnp.int32)
    rank_sorted = jnp.arange(target.shape[0], dtype=jnp.int32) - group_start
    rank_rows = jnp.zeros_like(target).at[ordering].set(rank_sorted)
    offset = ((length - arrived)[target] + rank_rows).astype(jnp.int32)
    return (target, offset, length)


def draw_row_target(key, part):
    return plan_rows(key)[0]


def draw_row_offset(key, part):
    return plan_rows(key)[1]


def draw_context_len(key, part):
    return plan_rows(key)[2]


def draw_draft_query_heads(key, part):
    key = jax.random.fold_in(key, 11)
    base_draw = jax.random.normal(key, (N_WIDE * BATCH_REQUESTS, DRAFT_TOKENS, QUERY_HEADS * HEAD_SIZE), jnp.float32)
    return jnp.clip(base_draw * 2.0, -12.0, 12.0).astype(jnp.bfloat16)


def block_scale(stream_key, extent, pieces, smallest, largest):
    def one(dim, blocks):
        heights = jax.random.uniform(jax.random.fold_in(jax.random.fold_in(stream_key, 6), dim), (blocks,), jnp.float32, smallest / len(pieces), largest / len(pieces))
        return jnp.repeat(jnp.exp(heights), extent[dim] // blocks).reshape((-1,) + (1,) * (len(extent) - dim - 1))

    gain = one(*pieces[0])
    for cut in pieces[1:]:
        gain = gain * one(*cut)
    return gain


def gaussian(own_key, shape, scale, limit, cuts=(), held_as=jnp.bfloat16):
    gain = block_scale(own_key, shape, cuts, -0.22, 0.18) if cuts else 1.0
    values = jax.random.normal(own_key, shape, jnp.float32) * scale * gain
    return jnp.minimum(jnp.maximum(values, -limit), limit).astype(held_as)


def setup_inputs(seed: int = 0, part: int = 0) -> dict:
    seeds = jax.random.split(jax.random.key(seed), 11)
    own_keys = jax.random.split(jax.random.fold_in(seeds[10], part), 11)
    prompt_hidden = gaussian(own_keys[0], (TOTAL_ROWS, D), 1.0, 6.0, ((0, 16),))
    resident_latent = gaussian(own_keys[1], (REQUESTS, CTX, LATENT_RANK), 1.0, 6.0, ((0, 16),))
    row_target = draw_row_target(jax.random.fold_in(jax.random.fold_in(seeds[10], part), 71), part)
    row_offset = draw_row_offset(jax.random.fold_in(jax.random.fold_in(seeds[10], part), 71), part)
    context_len = draw_context_len(jax.random.fold_in(jax.random.fold_in(seeds[10], part), 71), part)
    draft_hidden = gaussian(own_keys[5], (REQUESTS, DRAFT_TOKENS, D), 1.0, 6.0, ((0, 16),))
    draft_query_heads = draw_draft_query_heads(jax.random.fold_in(jax.random.fold_in(seeds[10], part), 71), part)
    down_weight = gaussian(seeds[7], (D, LATENT_RANK), D ** -0.5, 0.0625, ((0, 16),))
    key_up_weight = gaussian(seeds[8], (LATENT_RANK, KEY_VALUE_HEADS * HEAD_SIZE), LATENT_RANK ** -0.5, 0.375)
    value_up_weight = gaussian(seeds[9], (LATENT_RANK, KEY_VALUE_HEADS * HEAD_SIZE), LATENT_RANK ** -0.5, 0.375)
    return dict(prompt_hidden=prompt_hidden, resident_latent=resident_latent, row_target=row_target, row_offset=row_offset, context_len=context_len, draft_hidden=draft_hidden, draft_query_heads=draft_query_heads, down_weight=down_weight, key_up_weight=key_up_weight, value_up_weight=value_up_weight)


def softmax_parts(cache_scores, draft_scores, context_len):
    span_rows = cache_scores.shape[-1]
    draft_count = draft_scores.shape[-1]
    visible = jnp.arange(span_rows, dtype=jnp.int32)[None, :] < context_len[:, None]
    cache_scores = jnp.where(visible[:, None, None, None, :], cache_scores, -jnp.inf)
    causal = jnp.arange(draft_count)[None, :] <= jnp.arange(draft_count)[:, None]
    draft_scores = jnp.where(causal[None, :, None, None, :], draft_scores, -jnp.inf)
    peak_score = jnp.maximum(lax.optimization_barrier(jnp.max(cache_scores, -1, keepdims=True)), lax.optimization_barrier(jnp.max(draft_scores, -1, keepdims=True)))
    cache_exp = jnp.exp(cache_scores - peak_score)
    draft_exp = jnp.exp(draft_scores - peak_score)
    denominator = lax.optimization_barrier(jnp.sum(cache_exp, -1, keepdims=True)) + lax.optimization_barrier(jnp.sum(draft_exp, -1, keepdims=True))
    return (cache_exp / denominator, draft_exp / denominator)

def attend_block(latent_cache, draft_latent, draft_query_heads, context_len, key_up_weight, value_up_weight):
    high = lax.Precision.HIGHEST
    key_value_width = KEY_VALUE_HEADS * HEAD_SIZE
    up_both = jnp.concatenate([key_up_weight, value_up_weight], 1)
    draft_lookup_table = jnp.dot(draft_latent, up_both, preferred_element_type=jnp.float32)
    draft_key_rows = draft_lookup_table[:, :key_value_width].reshape(BATCH_REQUESTS, DRAFT_TOKENS, KEY_VALUE_HEADS, HEAD_SIZE)
    draft_value_rows = draft_lookup_table[:, key_value_width:].reshape(BATCH_REQUESTS, DRAFT_TOKENS, KEY_VALUE_HEADS, HEAD_SIZE)
    query_float = draft_query_heads.astype(jnp.float32).reshape(BATCH_REQUESTS, DRAFT_TOKENS, KEY_VALUE_HEADS, QUERY_HEADS // KEY_VALUE_HEADS, HEAD_SIZE)
    score_scale = 1.0 / math.sqrt(HEAD_SIZE)
    key_up_weight3 = key_up_weight.astype(jnp.float32).reshape(LATENT_RANK, KEY_VALUE_HEADS, HEAD_SIZE)
    value_up_weight3 = value_up_weight.astype(jnp.float32).reshape(LATENT_RANK, KEY_VALUE_HEADS, HEAD_SIZE)
    turned = jnp.einsum('bikgd,lkd->bikgl', query_float, key_up_weight3, precision=high)
    cache_f = latent_cache.astype(jnp.float32)
    cache_scores = jnp.einsum('bikgl,bpl->bikgp', turned, cache_f, precision=high) * score_scale
    draft_scores = jnp.einsum('bikgd,bjkd->bikgj', query_float, draft_key_rows, precision=high) * score_scale
    cache_weights, draft_weights = softmax_parts(cache_scores, draft_scores, context_len)
    mixed_latent = jnp.einsum('bikgp,bpl->bikgl', cache_weights, cache_f, precision=high)
    result = jnp.einsum('bikgl,lkd->bikgd', mixed_latent, value_up_weight3, precision=high)
    result = result + jnp.einsum('bikgj,bjkd->bikgd', draft_weights, draft_value_rows, precision=high)
    return result.reshape(BATCH_REQUESTS, DRAFT_TOKENS, QUERY_HEADS * HEAD_SIZE).astype(jnp.bfloat16)

def reference(prompt_hidden, resident_latent, row_target, row_offset, context_len, draft_hidden, draft_query_heads, down_weight, key_up_weight, value_up_weight):
    latent = jnp.dot(prompt_hidden, down_weight, preferred_element_type=jnp.float32).astype(jnp.bfloat16)
    draft_flat = draft_hidden.reshape(N_WIDE * BATCH_REQUESTS * DRAFT_TOKENS, D)
    draft_latent = jnp.dot(draft_flat, down_weight, preferred_element_type=jnp.float32).astype(jnp.bfloat16)
    land_index = (row_target.astype(jnp.int32) * CTX + row_offset.astype(jnp.int32)).astype(jnp.int32)
    latent_cache = resident_latent.reshape(N_WIDE * BATCH_REQUESTS * CTX, LATENT_RANK).at[land_index].set(latent)
    latent_cache = latent_cache.reshape(N_WIDE, BATCH_REQUESTS, CTX, LATENT_RANK)
    blocks = (latent_cache, draft_latent.reshape(N_WIDE, BATCH_REQUESTS * DRAFT_TOKENS, LATENT_RANK), draft_query_heads.reshape(N_WIDE, BATCH_REQUESTS, DRAFT_TOKENS, QUERY_HEADS * HEAD_SIZE), context_len.reshape(N_WIDE, BATCH_REQUESTS))
    attended = lax.map(lambda parts: attend_block(parts[0], parts[1], parts[2], parts[3], key_up_weight, value_up_weight), blocks)
    return attended.reshape(N_WIDE * BATCH_REQUESTS, DRAFT_TOKENS, QUERY_HEADS * HEAD_SIZE)
```

```python
import math

import jax
import jax.numpy as jnp
from jax import lax
from jax.experimental import pallas as pl
from jax.experimental.pallas import tpu as pltpu
from jax.sharding import PartitionSpec as P

QUERY_HEADS = 64
HEAD_SIZE = 128
FAR = -1e30
NT = (((1,), (1,)), ((), ()))
VMEM_BYTES = 40 * 1024 * 1024


def split_rows(x):
    top = x.astype(jnp.bfloat16)
    rest = (x - top.astype(jnp.float32)).astype(jnp.bfloat16)
    return jnp.concatenate([top, rest], 0)


def join_rows(x):
    half = x.shape[0] // 2
    return x[:half] + x[half:]


def held_kernel(draft_count, limit_ref, query_ref, key_up_ref, cache_ref, turned_ref, peak_ref, total_ref, mixed_ref):
    slot_count, span_rows, _ = cache_ref.shape
    tile = query_ref.shape[0]
    heads_kv = key_up_ref.shape[1] // HEAD_SIZE
    group_size = QUERY_HEADS // heads_kv
    rows = group_size * tile
    scale = math.log2(math.e) / math.sqrt(HEAD_SIZE)

    def head(k, carry):
        pieces = []
        for g in range(group_size):
            lanes = pl.ds(pl.multiple_of((k * group_size + g) * HEAD_SIZE, HEAD_SIZE), HEAD_SIZE)
            pieces.append(query_ref[:, lanes].astype(jnp.float32))
        query = jnp.concatenate(pieces, 0).astype(jnp.bfloat16)
        lanes = pl.ds(pl.multiple_of(k * HEAD_SIZE, HEAD_SIZE), HEAD_SIZE)
        turned = lax.dot_general(query, key_up_ref[:, lanes], NT, preferred_element_type=jnp.float32)
        both = split_rows(turned * scale)
        turned_ref[k] = both
        slot = lax.broadcasted_iota(jnp.int32, (rows, 1), 0) % tile // draft_count
        scores = jnp.full((rows, span_rows), FAR, jnp.float32)
        column = lax.broadcasted_iota(jnp.int32, (rows, span_rows), 1)
        for b in range(slot_count):
            one = join_rows(lax.dot_general(both, cache_ref[b], NT, preferred_element_type=jnp.float32))
            scores = jnp.where((slot == b) & (column < limit_ref[b]), one, scores)
        peak = jnp.max(scores, 1, keepdims=True)
        weights = jnp.exp2(scores - peak)
        peak_ref[k] = peak
        total_ref[k] = jnp.sum(weights, 1, keepdims=True)
        parted = split_rows(weights)
        mixed = jnp.zeros((rows, cache_ref.shape[2]), jnp.float32)
        for b in range(slot_count):
            one = join_rows(jnp.dot(parted, cache_ref[b], preferred_element_type=jnp.float32))
            mixed = jnp.where(slot == b, one, mixed)
        mixed_ref[k] = mixed
        return carry

    lax.fori_loop(0, heads_kv, head, 0)


def down_kernel(place_ref, prompt_ref, draft_ref, weight_ref, outgoing_ref, draft_latent_ref, sum_ref):
    step = pl.program_id(0)

    @pl.when(step == 0)
    def _():
        sum_ref[...] = jnp.zeros_like(sum_ref)

    rows = jnp.concatenate([prompt_ref[...], draft_ref[...]], 0)
    sum_ref[...] += jnp.dot(rows, weight_ref[...], preferred_element_type=jnp.float32)

    @pl.when(step == pl.num_programs(0) - 1)
    def _():
        count = prompt_ref.shape[0]
        latent = sum_ref[:count, :].astype(jnp.bfloat16)
        draft_latent_ref[...] = sum_ref[count:, :].astype(jnp.bfloat16)
        spot = lax.broadcasted_iota(jnp.int32, (outgoing_ref.shape[0], count), 0)
        chosen = jnp.where(spot == place_ref[...], 1.0, 0.0).astype(jnp.bfloat16)
        outgoing_ref[...] = jnp.dot(chosen, latent, preferred_element_type=jnp.float32).astype(jnp.bfloat16)


def late_kernel(
    column_slot_ref, incoming_ref, draft_latent_ref, turned_ref, peak_ref, total_ref, mixed_ref, value_up_ref,
    out_ref, rows_ref,
):
    slot_count, draft_count, _ = out_ref.shape
    tile = slot_count * draft_count
    heads_kv = peak_ref.shape[0]
    rows = peak_ref.shape[1]
    group_size = rows // tile
    arrived = incoming_ref.shape[0]
    drafts = draft_latent_ref.shape[0]
    span = rows_ref.shape[0]
    rows_ref[:arrived, :] = incoming_ref[...]
    rows_ref[arrived : arrived + drafts, :] = draft_latent_ref[...]
    rows_ref[arrived + drafts :, :] = jnp.zeros((span - arrived - drafts, rows_ref.shape[1]), jnp.bfloat16)
    place = lax.broadcasted_iota(jnp.int32, (rows, 1), 0) % tile
    arrived_seen = place // draft_count == column_slot_ref[...]
    column = lax.broadcasted_iota(jnp.int32, (rows, span - arrived), 1)
    draft_seen = (
        (column < tile) & (column // draft_count == place // draft_count) & (column % draft_count <= place % draft_count)
    )
    for k in range(heads_kv):
        scores = join_rows(lax.dot_general(turned_ref[k], rows_ref[...], NT, preferred_element_type=jnp.float32))
        scores = jnp.concatenate(
            [
                jnp.where(arrived_seen, scores[:, :arrived], FAR),
                jnp.where(draft_seen, scores[:, arrived:], FAR),
            ],
            1,
        )
        peak = jnp.maximum(jnp.max(scores, 1, keepdims=True), peak_ref[k])
        weights = jnp.exp2(scores - peak)
        fade = jnp.exp2(peak_ref[k] - peak)
        total = total_ref[k] * fade + jnp.sum(weights, 1, keepdims=True)
        mixed = join_rows(jnp.dot(split_rows(weights), rows_ref[...], preferred_element_type=jnp.float32))
        mixed = (mixed_ref[k] * fade + mixed) / total
        value_up = value_up_ref[:, k * HEAD_SIZE : (k + 1) * HEAD_SIZE]
        result = join_rows(jnp.dot(split_rows(mixed), value_up, preferred_element_type=jnp.float32))
        wide = jnp.concatenate([result[g * tile : (g + 1) * tile] for g in range(group_size)], 1)
        lanes = slice(k * group_size * HEAD_SIZE, (k + 1) * group_size * HEAD_SIZE)
        for b in range(slot_count):
            out_ref[b, :, lanes] = wide[b * draft_count : (b + 1) * draft_count].astype(jnp.bfloat16)


def local(
    prompt_hidden,
    resident_latent,
    row_target,
    row_offset,
    context_len,
    draft_hidden,
    draft_query_heads,
    down_weight,
    key_up_weight,
    value_up_weight,
):
    wide_size = lax.axis_size("wide")
    row_count, model_width = prompt_hidden.shape
    slot_count, span_rows, latent_width = resident_latent.shape
    draft_count = draft_hidden.shape[1]
    heads_kv = key_up_weight.shape[1] // HEAD_SIZE
    group_size = QUERY_HEADS // heads_kv
    tile = slot_count * draft_count
    head_rows = group_size * tile
    most_rows = 2 * ((row_count + wide_size - 1) // wide_size)
    params = pltpu.CompilerParams(vmem_limit_bytes=VMEM_BYTES)
    whole = pl.BlockSpec(memory_space=pltpu.VMEM)

    weight = lax.all_gather(down_weight, "wide", axis=0, tiled=True)

    index = jnp.arange(row_count, dtype=jnp.int32)
    same = (row_target[:, None] == row_target[None, :]) & (index[None, :] < index[:, None])
    rank = jnp.sum(same.astype(jnp.int32), 1)
    front = row_target % slot_count == 0
    place = row_target // slot_count * most_rows + jnp.where(front, rank, most_rows - 1 - rank)
    request = jnp.arange(wide_size * slot_count, dtype=jnp.int32)
    counts = jnp.sum((row_target[None, :] == request[:, None]).astype(jnp.int32), 1)
    counts = lax.all_to_all(counts.reshape(wide_size, slot_count), "wide", split_axis=0, concat_axis=0, tiled=True)
    limit = context_len - jnp.sum(counts, 0)
    spot = jnp.arange(most_rows, dtype=jnp.int32)[None, :]
    column_slot = jnp.where(
        spot < counts[:, 0:1], 0, jnp.where(spot >= most_rows - counts[:, 1:2], 1, -1)
    ).reshape(1, wide_size * most_rows)

    query = draft_query_heads.reshape(tile, QUERY_HEADS * HEAD_SIZE)
    f32 = jnp.float32
    turned, peak, total, mixed = pl.pallas_call(
        lambda *refs: held_kernel(draft_count, *refs),
        out_shape=[
            jax.ShapeDtypeStruct((heads_kv, 2 * head_rows, latent_width), jnp.bfloat16),
            jax.ShapeDtypeStruct((heads_kv, head_rows, 1), f32),
            jax.ShapeDtypeStruct((heads_kv, head_rows, 1), f32),
            jax.ShapeDtypeStruct((heads_kv, head_rows, latent_width), f32),
        ],
        in_specs=[pl.BlockSpec(memory_space=pltpu.SMEM), whole, whole, whole],
        out_specs=[whole] * 4,
        compiler_params=params,
        cost_estimate=pl.CostEstimate(flops=2**32, bytes_accessed=2**22, transcendentals=2**19),
        name="held_rows",
    )(limit, query, key_up_weight, resident_latent)

    draft_flat = jnp.pad(draft_hidden.reshape(tile, model_width), ((0, 16 - tile), (0, 0)))
    steps = 8
    depth = model_width // steps
    outgoing, draft_latent = pl.pallas_call(
        down_kernel,
        grid=(steps,),
        out_shape=[
            jax.ShapeDtypeStruct((wide_size * most_rows, latent_width), jnp.bfloat16),
            jax.ShapeDtypeStruct((16, latent_width), jnp.bfloat16),
        ],
        in_specs=[
            pl.BlockSpec((1, row_count), lambda i: (0, 0)),
            pl.BlockSpec((row_count, depth), lambda i: (0, i)),
            pl.BlockSpec((16, depth), lambda i: (0, i)),
            pl.BlockSpec((depth, latent_width), lambda i: (i, 0)),
        ],
        out_specs=[
            pl.BlockSpec((wide_size * most_rows, latent_width), lambda i: (0, 0)),
            pl.BlockSpec((16, latent_width), lambda i: (0, 0)),
        ],
        scratch_shapes=[pltpu.VMEM((row_count + 16, latent_width), f32)],
        compiler_params=params,
        name="down_rows",
    )(place.reshape(1, row_count), prompt_hidden, draft_flat, weight)

    incoming = lax.all_to_all(
        outgoing.reshape(wide_size, most_rows, latent_width), "wide", split_axis=0, concat_axis=0, tiled=True
    ).reshape(wide_size * most_rows, latent_width)

    span = (wide_size * most_rows + 16 + 127) // 128 * 128
    return pl.pallas_call(
        late_kernel,
        out_shape=jax.ShapeDtypeStruct((slot_count, draft_count, QUERY_HEADS * HEAD_SIZE), jnp.bfloat16),
        in_specs=[whole] * 8,
        out_specs=whole,
        scratch_shapes=[pltpu.VMEM((span, latent_width), jnp.bfloat16)],
        compiler_params=params,
        name="late_rows",
    )(column_slot, incoming, draft_latent, turned, peak, total, mixed, value_up_weight)


def solution(mesh):
    placed = (
        P(("rep", "wide"), None),
        P(("rep", "wide"), None, None),
        P(("rep", "wide")),
        P(("rep", "wide")),
        P(("rep", "wide")),
        P(("rep", "wide"), None, None),
        P(("rep", "wide"), None, None),
        P("wide", None),
        P(),
        P(),
    )
    return jax.shard_map(
        local, mesh=mesh, in_specs=placed, out_specs=P(("rep", "wide"), None, None), check_vma=False
    )
```

```python
import functools
import math

import jax
import jax.numpy as jnp
from jax import lax
from jax.experimental import pallas as pl
from jax.experimental.pallas import tpu as pltpu
from jax.sharding import PartitionSpec as P

QUERY_HEADS = 64
HEAD_SIZE = 128
FAR = -1e30
NT = (((1,), (1,)), ((), ()))
HELD_PARTS = 4
VMEM_BYTES = 40 * 1024 * 1024


def split_rows(x):
    top = x.astype(jnp.bfloat16)
    rest = (x - top.astype(jnp.float32)).astype(jnp.bfloat16)
    return jnp.concatenate([top, rest], 0)


def join_rows(x):
    half = x.shape[0] // 2
    return x[:half] + x[half:]


def held_kernel(first, draft_count, limit_ref, query_ref, key_up_ref, cache_ref, turned_ref, peak_ref, total_ref, mixed_ref):
    slot_count, span_rows, _ = cache_ref.shape
    tile = query_ref.shape[0]
    heads_kv = key_up_ref.shape[1] // HEAD_SIZE
    group_size = QUERY_HEADS // heads_kv
    rows = group_size * tile
    scale = math.log2(math.e) / math.sqrt(HEAD_SIZE)

    def head(k, carry):
        pieces = []
        for g in range(group_size):
            lanes = pl.ds(pl.multiple_of(((first + k) * group_size + g) * HEAD_SIZE, HEAD_SIZE), HEAD_SIZE)
            pieces.append(query_ref[:, lanes].astype(jnp.float32))
        query = jnp.concatenate(pieces, 0).astype(jnp.bfloat16)
        lanes = pl.ds(pl.multiple_of((first + k) * HEAD_SIZE, HEAD_SIZE), HEAD_SIZE)
        turned = lax.dot_general(query, key_up_ref[:, lanes], NT, preferred_element_type=jnp.float32)
        both = split_rows(turned * scale)
        turned_ref[k] = both
        slot = lax.broadcasted_iota(jnp.int32, (rows, 1), 0) % tile // draft_count
        scores = jnp.full((rows, span_rows), FAR, jnp.float32)
        column = lax.broadcasted_iota(jnp.int32, (rows, span_rows), 1)
        for b in range(slot_count):
            one = join_rows(lax.dot_general(both, cache_ref[b], NT, preferred_element_type=jnp.float32))
            scores = jnp.where((slot == b) & (column < limit_ref[b]), one, scores)
        peak = jnp.max(scores, 1, keepdims=True)
        weights = jnp.exp2(scores - peak)
        peak_ref[k] = peak
        total_ref[k] = jnp.sum(weights, 1, keepdims=True)
        parted = split_rows(weights)
        mixed = jnp.zeros((rows, cache_ref.shape[2]), jnp.float32)
        for b in range(slot_count):
            one = join_rows(jnp.dot(parted, cache_ref[b], preferred_element_type=jnp.float32))
            mixed = jnp.where(slot == b, one, mixed)
        mixed_ref[k] = mixed
        return carry

    lax.fori_loop(0, turned_ref.shape[0], head, 0)


def down_kernel(starts_of, me_ref, place_ref, prompt_ref, draft_ref, *refs):
    starts = starts_of(me_ref[0])
    weight_refs, (outgoing_ref, draft_latent_ref) = refs[:-2], refs[-2:]
    count = prompt_ref.shape[0]
    total = jnp.zeros((count + draft_ref.shape[0], outgoing_ref.shape[1]), jnp.float32)
    for p, weight_ref in enumerate(weight_refs):
        depth = weight_ref.shape[0]
        lanes = pl.ds(pl.multiple_of(starts[p], HEAD_SIZE), depth)
        rows = jnp.concatenate([prompt_ref[:, lanes], draft_ref[:, lanes]], 0)
        total += jnp.dot(rows, weight_ref[...], preferred_element_type=jnp.float32)
    latent = total[:count].astype(jnp.bfloat16)
    draft_latent_ref[...] = total[count:].astype(jnp.bfloat16)
    spot = lax.broadcasted_iota(jnp.int32, (outgoing_ref.shape[0], count), 0)
    chosen = jnp.where(spot == place_ref[...], 1.0, 0.0).astype(jnp.bfloat16)
    outgoing_ref[...] = jnp.dot(chosen, latent, preferred_element_type=jnp.float32).astype(jnp.bfloat16)


def gather_pieces(shard, wide_size):
    rows = shard.shape[0]
    if wide_size != 16:
        return [lax.all_gather(shard, "wide", axis=0, tiled=True)], lambda me: [0]
    sizes = (wide_size // 4, 2, 2)

    def flat(spot):
        return (spot[0] * sizes[1] + spot[1]) * sizes[2] + spot[2]

    def spots():
        return [(z, y, c) for z in range(sizes[0]) for y in range(sizes[1]) for c in range(sizes[2])]

    def move(x, axis, step):
        pairs = []
        for spot in spots():
            to = list(spot)
            to[axis] = (to[axis] + step) % sizes[axis]
            pairs.append((flat(spot), flat(to)))
        return lax.ppermute(x, "wide", pairs)

    held = [((0, 0, 0), shard)]
    for axis in range(3):
        came = []
        for step in range(1, sizes[axis]):
            for trail, x in held:
                longer = list(trail)
                longer[axis] = step
                came.append((tuple(longer), move(x, axis, step)))
        held = held + came

    def starts_of(me):
        here = (me // (sizes[1] * sizes[2]), me // sizes[2] % sizes[1], me % sizes[2])
        return [
            flat([(here[a] - trail[a] + sizes[a]) % sizes[a] for a in range(3)]) * rows for trail, _ in held
        ]

    return [x for _, x in held], starts_of


def late_kernel(
    column_slot_ref, incoming_ref, draft_latent_ref, value_up_ref, *refs
):
    held_refs, (out_ref, rows_ref) = refs[:-2], refs[-2:]
    slot_count, draft_count, _ = out_ref.shape
    tile = slot_count * draft_count
    part_heads, rows, _ = held_refs[1].shape
    heads_kv = part_heads * HELD_PARTS
    group_size = rows // tile
    arrived = incoming_ref.shape[0]
    drafts = draft_latent_ref.shape[0]
    span = rows_ref.shape[0]
    rows_ref[:arrived, :] = incoming_ref[...]
    rows_ref[arrived : arrived + drafts, :] = draft_latent_ref[...]
    rows_ref[arrived + drafts :, :] = jnp.zeros((span - arrived - drafts, rows_ref.shape[1]), jnp.bfloat16)
    place = lax.broadcasted_iota(jnp.int32, (rows, 1), 0) % tile
    arrived_seen = place // draft_count == column_slot_ref[...]
    column = lax.broadcasted_iota(jnp.int32, (rows, span - arrived), 1)
    draft_seen = (
        (column < tile) & (column // draft_count == place // draft_count) & (column % draft_count <= place % draft_count)
    )
    for k in range(heads_kv):
        turned, held_peak, held_total, held_mixed = (
            ref[k % part_heads] for ref in held_refs[k // part_heads * 4 : k // part_heads * 4 + 4]
        )
        scores = join_rows(lax.dot_general(turned, rows_ref[...], NT, preferred_element_type=jnp.float32))
        scores = jnp.concatenate(
            [
                jnp.where(arrived_seen, scores[:, :arrived], FAR),
                jnp.where(draft_seen, scores[:, arrived:], FAR),
            ],
            1,
        )
        peak = jnp.maximum(jnp.max(scores, 1, keepdims=True), held_peak)
        weights = jnp.exp2(scores - peak)
        fade = jnp.exp2(held_peak - peak)
        total = held_total * fade + jnp.sum(weights, 1, keepdims=True)
        mixed = join_rows(jnp.dot(split_rows(weights), rows_ref[...], preferred_element_type=jnp.float32))
        mixed = (held_mixed * fade + mixed) / total
        value_up = value_up_ref[:, k * HEAD_SIZE : (k + 1) * HEAD_SIZE]
        result = join_rows(jnp.dot(split_rows(mixed), value_up, preferred_element_type=jnp.float32))
        wide = jnp.concatenate([result[g * tile : (g + 1) * tile] for g in range(group_size)], 1)
        lanes = slice(k * group_size * HEAD_SIZE, (k + 1) * group_size * HEAD_SIZE)
        for b in range(slot_count):
            out_ref[b, :, lanes] = wide[b * draft_count : (b + 1) * draft_count].astype(jnp.bfloat16)


def local(
    prompt_hidden,
    resident_latent,
    row_target,
    row_offset,
    context_len,
    draft_hidden,
    draft_query_heads,
    down_weight,
    key_up_weight,
    value_up_weight,
):
    wide_size = lax.axis_size("wide")
    row_count, model_width = prompt_hidden.shape
    slot_count, span_rows, latent_width = resident_latent.shape
    draft_count = draft_hidden.shape[1]
    heads_kv = key_up_weight.shape[1] // HEAD_SIZE
    group_size = QUERY_HEADS // heads_kv
    tile = slot_count * draft_count
    head_rows = group_size * tile
    most_rows = 2 * ((row_count + wide_size - 1) // wide_size)
    params = pltpu.CompilerParams(vmem_limit_bytes=VMEM_BYTES)
    whole = pl.BlockSpec(memory_space=pltpu.VMEM)

    pieces, starts_of = gather_pieces(down_weight, wide_size)

    index = jnp.arange(row_count, dtype=jnp.int32)
    same = (row_target[:, None] == row_target[None, :]) & (index[None, :] < index[:, None])
    rank = jnp.sum(same.astype(jnp.int32), 1)
    front = row_target % slot_count == 0
    place = row_target // slot_count * most_rows + jnp.where(front, rank, most_rows - 1 - rank)
    request = jnp.arange(wide_size * slot_count, dtype=jnp.int32)
    counts = jnp.sum((row_target[None, :] == request[:, None]).astype(jnp.int32), 1)
    counts = lax.all_to_all(counts.reshape(wide_size, slot_count), "wide", split_axis=0, concat_axis=0, tiled=True)
    limit = context_len - jnp.sum(counts, 0)
    spot = jnp.arange(most_rows, dtype=jnp.int32)[None, :]
    column_slot = jnp.where(
        spot < counts[:, 0:1], 0, jnp.where(spot >= most_rows - counts[:, 1:2], 1, -1)
    ).reshape(1, wide_size * most_rows)

    query = draft_query_heads.reshape(tile, QUERY_HEADS * HEAD_SIZE)
    f32 = jnp.float32
    part_heads = heads_kv // HELD_PARTS
    held = []
    for part in range(HELD_PARTS):
        held += pl.pallas_call(
            functools.partial(held_kernel, part * part_heads, draft_count),
            out_shape=[
                jax.ShapeDtypeStruct((part_heads, 2 * head_rows, latent_width), jnp.bfloat16),
                jax.ShapeDtypeStruct((part_heads, head_rows, 1), f32),
                jax.ShapeDtypeStruct((part_heads, head_rows, 1), f32),
                jax.ShapeDtypeStruct((part_heads, head_rows, latent_width), f32),
            ],
            in_specs=[pl.BlockSpec(memory_space=pltpu.SMEM), whole, whole, whole],
            out_specs=[whole] * 4,
            compiler_params=params,
            cost_estimate=pl.CostEstimate(flops=2**30, bytes_accessed=2**21, transcendentals=2**17),
            name="held_rows",
        )(limit, query, key_up_weight, resident_latent)

    draft_flat = jnp.pad(draft_hidden.reshape(tile, model_width), ((0, 16 - tile), (0, 0)))
    smem = pl.BlockSpec(memory_space=pltpu.SMEM)
    outgoing, draft_latent = pl.pallas_call(
        functools.partial(down_kernel, starts_of),
        out_shape=[
            jax.ShapeDtypeStruct((wide_size * most_rows, latent_width), jnp.bfloat16),
            jax.ShapeDtypeStruct((16, latent_width), jnp.bfloat16),
        ],
        in_specs=[smem] + [whole] * (3 + len(pieces)),
        out_specs=[whole] * 2,
        compiler_params=params,
        name="down_rows",
    )(lax.axis_index("wide").reshape(1), place.reshape(1, row_count), prompt_hidden, draft_flat, *pieces)

    incoming = lax.all_to_all(
        outgoing.reshape(wide_size, most_rows, latent_width), "wide", split_axis=0, concat_axis=0, tiled=True
    ).reshape(wide_size * most_rows, latent_width)

    span = (wide_size * most_rows + 16 + 127) // 128 * 128
    return pl.pallas_call(
        late_kernel,
        out_shape=jax.ShapeDtypeStruct((slot_count, draft_count, QUERY_HEADS * HEAD_SIZE), jnp.bfloat16),
        in_specs=[whole] * (4 + len(held)),
        out_specs=whole,
        scratch_shapes=[pltpu.VMEM((span, latent_width), jnp.bfloat16)],
        compiler_params=params,
        name="late_rows",
    )(column_slot, incoming, draft_latent, value_up_weight, *held)


def solution(mesh):
    placed = (
        P(("rep", "wide"), None),
        P(("rep", "wide"), None, None),
        P(("rep", "wide")),
        P(("rep", "wide")),
        P(("rep", "wide")),
        P(("rep", "wide"), None, None),
        P(("rep", "wide"), None, None),
        P("wide", None),
        P(),
        P(),
    )
    return jax.shard_map(
        local, mesh=mesh, in_specs=placed, out_specs=P(("rep", "wide"), None, None), check_vma=False
    )
```

```python
import functools
import math

import jax
import jax.numpy as jnp
from jax import lax
from jax.experimental import pallas as pl
from jax.experimental.pallas import tpu as pltpu
from jax.sharding import PartitionSpec as P

QUERY_HEADS = 64
HEAD_SIZE = 128
FAR = -1e30
NT = (((1,), (1,)), ((), ()))
WHOLE = pl.BlockSpec(memory_space=pltpu.VMEM)
SCALARS = pl.BlockSpec(memory_space=pltpu.SMEM)
UNREAD = pl.BlockSpec(memory_space=pl.ANY)


def params(mib):
    return pltpu.CompilerParams(vmem_limit_bytes=mib * 1024 * 1024)


def split_rows(x):
    top = x.astype(jnp.bfloat16)
    rest = (x - top.astype(jnp.float32)).astype(jnp.bfloat16)
    return jnp.concatenate([top, rest], 0)


def join_rows(x):
    half = x.shape[0] // 2
    return x[:half] + x[half:]


def held_kernel(
    limit_ref, query_ref, key_up_ref, cache_ref, turned_ref, peak_ref, total_ref, mixed_ref, float_ref, scores_ref
):
    slot_count, span_rows, _ = cache_ref.shape
    draft_count = query_ref.shape[1]
    heads_kv = key_up_ref.shape[1] // HEAD_SIZE
    group_size = QUERY_HEADS // heads_kv
    rows = group_size * draft_count
    scale = math.log2(math.e) / math.sqrt(HEAD_SIZE)
    step = 256
    for k in range(heads_kv):
        pieces = []
        for b in range(slot_count):
            for g in range(group_size):
                lane = (k * group_size + g) * HEAD_SIZE
                pieces.append(query_ref[b, :, lane : lane + HEAD_SIZE].astype(jnp.float32))
        query = jnp.concatenate(pieces, 0).astype(jnp.bfloat16)
        key_up = key_up_ref[:, k * HEAD_SIZE : (k + 1) * HEAD_SIZE]
        turned = lax.dot_general(query, key_up, NT, preferred_element_type=jnp.float32) * scale
        for b in range(slot_count):
            float_ref[b, k * rows : (k + 1) * rows, :] = turned[b * rows : (b + 1) * rows]
    for b in range(slot_count):
        turned_ref[b] = split_rows(float_ref[b])
        peak = None
        for c in range(0, span_rows, step):
            scores = join_rows(
                lax.dot_general(turned_ref[b], cache_ref[b, c : c + step], NT, preferred_element_type=jnp.float32)
            )
            column = lax.broadcasted_iota(jnp.int32, (1, step), 1) + c
            scores = jnp.where(column < limit_ref[b], scores, FAR)
            scores_ref[:, c : c + step] = scores
            top = jnp.max(scores, 1, keepdims=True)
            peak = top if peak is None else jnp.maximum(peak, top)
        peak_ref[b] = peak
        total = jnp.zeros_like(peak)
        mixed = jnp.zeros(mixed_ref.shape[1:], jnp.float32)
        for c in range(0, span_rows, step):
            weights = jnp.exp2(scores_ref[:, c : c + step] - peak)
            total += jnp.sum(weights, 1, keepdims=True)
            mixed += join_rows(
                jnp.dot(split_rows(weights), cache_ref[b, c : c + step], preferred_element_type=jnp.float32)
            )
        total_ref[b] = total
        mixed_ref[b] = mixed


def down_kernel(trails, starts_of, groups, first, me_ref, *refs):
    row_refs, refs = refs[: 2 * groups], refs[2 * groups :]
    sum_refs = None
    if not first:
        sum_refs, refs = refs[:groups], refs[groups:]
    piece_refs, out_refs = refs[: len(trails)], refs[-groups:]
    starts = starts_of(me_ref, trails)
    count = row_refs[0].shape[0]
    slot_count, draft_count, _ = row_refs[1].shape
    drafts = slot_count * draft_count
    total = None
    for start, piece_ref in zip(starts, piece_refs):
        depth = piece_ref.shape[0]
        lanes = pl.ds(pl.multiple_of(start, HEAD_SIZE), depth)
        stack = [
            row_refs[2 * n + 1][b, :, lanes].astype(jnp.float32) for n in range(groups) for b in range(slot_count)
        ]
        if groups * drafts < 16:
            stack.append(jnp.zeros((16 - groups * drafts, depth), jnp.float32))
        rows = [row_refs[2 * n][:, lanes] for n in range(groups)] + [jnp.concatenate(stack, 0).astype(jnp.bfloat16)]
        product = jnp.dot(jnp.concatenate(rows, 0), piece_ref[...], preferred_element_type=jnp.float32)
        total = product if total is None else total + product
    for n in range(groups):
        prompt_sum = total[n * count : (n + 1) * count]
        draft_sum = total[groups * count + n * drafts : groups * count + (n + 1) * drafts]
        if sum_refs is not None:
            prompt_sum += sum_refs[n][:count, :]
            draft_sum += sum_refs[n][count:, :]
        out_refs[n][:count, :] = prompt_sum
        out_refs[n][count:, :] = draft_sum


def place_kernel(parts, place_ref, *refs):
    sum_refs, (outgoing_ref, draft_latent_ref) = refs[:parts], refs[-2:]
    total = sum_refs[0][...]
    for ref in sum_refs[1:]:
        total += ref[...]
    latent = total.astype(jnp.bfloat16)
    count = place_ref.shape[1]
    draft_latent_ref[...] = total[count:].astype(jnp.bfloat16).astype(jnp.float32)
    spot = lax.broadcasted_iota(jnp.int32, (outgoing_ref.shape[0], count), 0)
    chosen = jnp.where(spot == place_ref[...], 1.0, 0.0).astype(jnp.bfloat16)
    outgoing_ref[...] = jnp.dot(chosen, latent[:count], preferred_element_type=jnp.float32).astype(jnp.bfloat16)


def late_kernel(
    column_slot_ref, incoming_ref, draft_latent_ref, turned_ref, peak_ref, total_ref, mixed_ref, value_up_ref,
    out_ref, rows_ref, parted_ref,
):
    slot_count, draft_count, _ = out_ref.shape
    tile = slot_count * draft_count
    heads_kv = value_up_ref.shape[1] // HEAD_SIZE
    group_size = QUERY_HEADS // heads_kv
    head_rows = group_size * draft_count
    rows = peak_ref.shape[1]
    arrived = incoming_ref.shape[0]
    span = rows_ref.shape[0]
    drafts = jnp.concatenate([draft_latent_ref[...], jnp.zeros((span - arrived - tile, rows_ref.shape[1]), jnp.float32)], 0)
    rows_ref[:arrived, :] = incoming_ref[...]
    rows_ref[arrived:, :] = drafts.astype(jnp.bfloat16)
    token = lax.broadcasted_iota(jnp.int32, (rows, 1), 0) % draft_count
    column = lax.broadcasted_iota(jnp.int32, (rows, span - arrived), 1)
    for b in range(slot_count):
        scores = join_rows(lax.dot_general(turned_ref[b], rows_ref[...], NT, preferred_element_type=jnp.float32))
        draft_seen = (column >= b * draft_count) & (column <= b * draft_count + token)
        scores = jnp.concatenate(
            [
                jnp.where(column_slot_ref[...] == b, scores[:, :arrived], FAR),
                jnp.where(draft_seen, scores[:, arrived:], FAR),
            ],
            1,
        )
        peak = jnp.maximum(jnp.max(scores, 1, keepdims=True), peak_ref[b])
        weights = jnp.exp2(scores - peak)
        fade = jnp.exp2(peak_ref[b] - peak)
        total = total_ref[b] * fade + jnp.sum(weights, 1, keepdims=True)
        mixed = join_rows(jnp.dot(split_rows(weights), rows_ref[...], preferred_element_type=jnp.float32))
        parted_ref[b] = split_rows((mixed_ref[b] * fade + mixed) / total)
    for k in range(heads_kv):
        part = []
        for b in range(slot_count):
            part.append(parted_ref[b, k * head_rows : (k + 1) * head_rows, :])
            part.append(parted_ref[b, rows + k * head_rows : rows + (k + 1) * head_rows, :])
        value_up = value_up_ref[:, k * HEAD_SIZE : (k + 1) * HEAD_SIZE]
        both = jnp.dot(jnp.concatenate(part, 0), value_up, preferred_element_type=jnp.float32)
        for b in range(slot_count):
            result = join_rows(both[b * 2 * head_rows : (b + 1) * 2 * head_rows])
            wide = jnp.concatenate(
                [result[g * draft_count : (g + 1) * draft_count] for g in range(group_size)], 1
            )
            out_ref[b, :, k * group_size * HEAD_SIZE : (k + 1) * group_size * HEAD_SIZE] = wide.astype(jnp.bfloat16)


def down_sums(prompt_hidden, draft_hidden, shard, wide_size):
    shard_rows, latent_width = shard.shape
    count = prompt_hidden.shape[0]
    slot_count, draft_count, _ = draft_hidden.shape
    sum_shape = jax.ShapeDtypeStruct((count + slot_count * draft_count, latent_width), jnp.float32)
    rep, wide = lax.axis_index("rep"), lax.axis_index("wide")
    me = jnp.stack([rep, wide])

    def call(stages, starts_of, groups, rows, tie=()):
        sums = []
        for n, stage in enumerate(stages):
            trails, pieces = [t for t, _ in stage], [x for _, x in stage]
            ties = tie if n == len(stages) - 1 else ()
            sums = pl.pallas_call(
                functools.partial(down_kernel, trails, starts_of, groups, n == 0),
                out_shape=[sum_shape] * groups,
                in_specs=[SCALARS] + [WHOLE] * (len(rows) + len(sums) + len(pieces)) + [UNREAD] * len(ties),
                out_specs=[WHOLE] * groups,
                compiler_params=params(16),
                cost_estimate=pl.CostEstimate(flops=2**28, bytes_accessed=2**20, transcendentals=0),
                name="down_rows",
            )(me, *rows, *sums, *pieces, *ties)
        return sums

    if wide_size != 16 or lax.axis_size("rep") != 2:
        whole = lax.all_gather(shard, "wide", axis=0, tiled=True)
        return lambda tie: call([[(0, whole)]], lambda me_ref, trails: trails, 1, [prompt_hidden, draft_hidden], tie)

    sizes = (2, wide_size // 4, 2, 2)
    spots = [(r, z, y, c) for r in range(2) for z in range(sizes[1]) for y in range(2) for c in range(2)]

    def flat(spot):
        return ((spot[0] * sizes[1] + spot[1]) * 2 + spot[2]) * 2 + spot[3]

    def move(x, axis, step=1):
        pairs = []
        for spot in spots:
            to = list(spot)
            to[axis] = (to[axis] + step) % sizes[axis]
            pairs.append((flat(spot), flat(to)))
        return lax.ppermute(x, ("rep", "wide"), pairs)

    half_rows = shard_rows // 2
    half = lax.dynamic_slice(shard, (rep * half_rows, 0), (half_rows, latent_width))
    z1, z3 = move(half, 1, 1), move(half, 1, -1)
    y0 = move(shard, 2)
    other_prompt, other_draft = move(prompt_hidden, 3), move(draft_hidden, 3)
    yz1, yz3, xz1, xz3 = move(z1, 2), move(z3, 2), move(z1, 0), move(z3, 0)
    z2 = move(z1, 1, 1)
    xz2, yz2 = move(z2, 0), move(z2, 2)
    xyz1, xyz3 = move(yz1, 0), move(yz3, 0)
    yxz2 = move(xz2, 2)

    def starts_of(me_ref, trails):
        rep, wide = me_ref[0], me_ref[1]
        z, y, c = wide // 4, wide // 2 % 2, wide % 2
        starts = []
        for x_step, z_step, y_step, is_half in trails:
            owner = ((z - z_step + sizes[1]) % sizes[1] * 2 + (y + y_step) % 2) * 2 + c
            starts.append(owner * shard_rows + (rep + x_step) % 2 * half_rows * is_half)
        return starts

    stages = [
        [((0, 0, 0, 0), shard), ((0, 0, 1, 0), y0), ((0, 1, 0, 1), z1), ((0, 3, 0, 1), z3)],
        [((0, 1, 1, 1), yz1), ((0, 3, 1, 1), yz3), ((1, 1, 0, 1), xz1), ((1, 3, 0, 1), xz3)],
        [((0, 2, 0, 1), z2), ((0, 2, 1, 1), yz2), ((1, 2, 0, 1), xz2), ((1, 2, 1, 1), yxz2)],
        [((1, 1, 1, 1), xyz1), ((1, 3, 1, 1), xyz3)],
    ]
    rows = [prompt_hidden, draft_hidden, other_prompt, other_draft]

    def finish(tie):
        mine, others = call(stages, starts_of, 2, rows, tie)
        return [mine, move(others, 3)]

    return finish


def local(
    prompt_hidden,
    resident_latent,
    row_target,
    row_offset,
    context_len,
    draft_hidden,
    draft_query_heads,
    down_weight,
    key_up_weight,
    value_up_weight,
):
    f32, bf16 = jnp.float32, jnp.bfloat16
    wide_size = lax.axis_size("wide")
    row_count = prompt_hidden.shape[0]
    slot_count, span_rows, latent_width = resident_latent.shape
    draft_count = draft_hidden.shape[1]
    tile = slot_count * draft_count
    rows = QUERY_HEADS * draft_count
    most_rows = 2 * ((row_count + wide_size - 1) // wide_size)
    arrived = wide_size * most_rows

    finish = down_sums(prompt_hidden, draft_hidden, down_weight, wide_size)

    index = jnp.arange(row_count, dtype=jnp.int32)
    same = (row_target[:, None] == row_target[None, :]) & (index[None, :] < index[:, None])
    rank = jnp.sum(same.astype(jnp.int32), 1)
    front = row_target % slot_count == 0
    place = row_target // slot_count * most_rows + jnp.where(front, rank, most_rows - 1 - rank)
    request = jnp.arange(wide_size * slot_count, dtype=jnp.int32)
    counts = jnp.sum((row_target[None, :] == request[:, None]).astype(jnp.int32), 1)
    counts = lax.all_to_all(counts.reshape(wide_size, slot_count), "wide", split_axis=0, concat_axis=0, tiled=True)
    limit = context_len - jnp.sum(counts, 0)
    spot = jnp.arange(most_rows, dtype=jnp.int32)[None, :]
    column_slot = jnp.where(
        spot < counts[:, 0:1], 0, jnp.where(spot >= most_rows - counts[:, 1:2], 1, -1)
    ).reshape(1, arrived)

    turned, peak, total, mixed = pl.pallas_call(
        held_kernel,
        out_shape=[
            jax.ShapeDtypeStruct((slot_count, 2 * rows, latent_width), bf16),
            jax.ShapeDtypeStruct((slot_count, rows, 1), f32),
            jax.ShapeDtypeStruct((slot_count, rows, 1), f32),
            jax.ShapeDtypeStruct((slot_count, rows, latent_width), f32),
        ],
        in_specs=[SCALARS, WHOLE, WHOLE, WHOLE],
        out_specs=[WHOLE] * 4,
        scratch_shapes=[pltpu.VMEM((slot_count, rows, latent_width), f32), pltpu.VMEM((rows, span_rows), f32)],
        compiler_params=params(24),
        cost_estimate=pl.CostEstimate(flops=2**31, bytes_accessed=2**22, transcendentals=2**19),
        name="held_rows",
    )(limit, draft_query_heads, key_up_weight, resident_latent)

    sums = finish((peak,))
    outgoing, draft_latent = pl.pallas_call(
        functools.partial(place_kernel, len(sums)),
        out_shape=[
            jax.ShapeDtypeStruct((arrived, latent_width), bf16),
            jax.ShapeDtypeStruct((tile, latent_width), f32),
        ],
        in_specs=[WHOLE] * (1 + len(sums)),
        out_specs=[WHOLE] * 2,
        compiler_params=params(16),
        name="place_rows",
    )(place.reshape(1, row_count), *sums)

    incoming = lax.all_to_all(
        outgoing.reshape(wide_size, most_rows, latent_width), "wide", split_axis=0, concat_axis=0, tiled=True
    ).reshape(arrived, latent_width)

    span = (arrived + tile + 127) // 128 * 128
    return pl.pallas_call(
        late_kernel,
        out_shape=jax.ShapeDtypeStruct((slot_count, draft_count, QUERY_HEADS * HEAD_SIZE), bf16),
        in_specs=[WHOLE] * 8,
        out_specs=WHOLE,
        scratch_shapes=[
            pltpu.VMEM((span, latent_width), bf16),
            pltpu.VMEM((slot_count, 2 * rows, latent_width), bf16),
        ],
        compiler_params=params(24),
        name="late_rows",
    )(column_slot, incoming, draft_latent, turned, peak, total, mixed, value_up_weight)


def solution(mesh):
    placed = (
        P(("rep", "wide"), None),
        P(("rep", "wide"), None, None),
        P(("rep", "wide")),
        P(("rep", "wide")),
        P(("rep", "wide")),
        P(("rep", "wide"), None, None),
        P(("rep", "wide"), None, None),
        P("wide", None),
        P(),
        P(),
    )
    return jax.shard_map(
        local, mesh=mesh, in_specs=placed, out_specs=P(("rep", "wide"), None, None), check_vma=False
    )
```

```python
import functools
import math

import jax
import jax.numpy as jnp
from jax import lax
from jax.experimental import pallas as pl
from jax.experimental.pallas import tpu as pltpu
from jax.sharding import PartitionSpec as P

QUERY_HEADS = 64
HEAD_SIZE = 128
FAR = -1e30
NT = (((1,), (1,)), ((), ()))
WHOLE = pl.BlockSpec(memory_space=pltpu.VMEM)
SCALARS = pl.BlockSpec(memory_space=pltpu.SMEM)
UNREAD = pl.BlockSpec(memory_space=pl.ANY)


def params(mib):
    return pltpu.CompilerParams(vmem_limit_bytes=mib * 1024 * 1024)


def split_rows(x):
    top = x.astype(jnp.bfloat16)
    rest = (x - top.astype(jnp.float32)).astype(jnp.bfloat16)
    return jnp.concatenate([top, rest], 0)


def join_rows(x):
    half = x.shape[0] // 2
    return x[:half] + x[half:]


def held_kernel(
    limit_ref, query_hbm, key_up_hbm, cache_hbm, turned_ref, peak_ref, total_ref, mixed_ref,
    query_ref, key_up_ref, cache_ref, float_ref, scores_ref, sems,
):
    copies = [
        pltpu.make_async_copy(source, target, sems.at[n])
        for n, (source, target) in enumerate(
            [(query_hbm, query_ref), (key_up_hbm, key_up_ref), (cache_hbm, cache_ref)]
        )
    ]
    for copy in copies:
        copy.start()
    slot_count, span_rows, _ = cache_ref.shape
    draft_count = query_ref.shape[1]
    heads_kv = key_up_ref.shape[1] // HEAD_SIZE
    group_size = QUERY_HEADS // heads_kv
    rows = group_size * draft_count
    scale = math.log2(math.e) / math.sqrt(HEAD_SIZE)
    step = 256
    copies[0].wait()
    copies[1].wait()
    for k in range(heads_kv):
        pieces = []
        for b in range(slot_count):
            for g in range(group_size):
                lane = (k * group_size + g) * HEAD_SIZE
                pieces.append(query_ref[b, :, lane : lane + HEAD_SIZE].astype(jnp.float32))
        query = jnp.concatenate(pieces, 0).astype(jnp.bfloat16)
        key_up = key_up_ref[:, k * HEAD_SIZE : (k + 1) * HEAD_SIZE]
        turned = lax.dot_general(query, key_up, NT, preferred_element_type=jnp.float32) * scale
        for b in range(slot_count):
            float_ref[b, k * rows : (k + 1) * rows, :] = turned[b * rows : (b + 1) * rows]
    copies[2].wait()
    for b in range(slot_count):
        turned_ref[b] = split_rows(float_ref[b])
        peak = None
        for c in range(0, span_rows, step):
            scores = join_rows(
                lax.dot_general(turned_ref[b], cache_ref[b, c : c + step], NT, preferred_element_type=jnp.float32)
            )
            column = lax.broadcasted_iota(jnp.int32, (1, step), 1) + c
            scores = jnp.where(column < limit_ref[b : b + 1, 0:1], scores, FAR)
            scores_ref[:, c : c + step] = scores
            top = jnp.max(scores, 1, keepdims=True)
            peak = top if peak is None else jnp.maximum(peak, top)
        peak_ref[b] = peak
        total = jnp.zeros_like(peak)
        mixed = jnp.zeros(mixed_ref.shape[1:], jnp.float32)
        for c in range(0, span_rows, step):
            weights = jnp.exp2(scores_ref[:, c : c + step] - peak)
            total += jnp.sum(weights, 1, keepdims=True)
            mixed += join_rows(
                jnp.dot(split_rows(weights), cache_ref[b, c : c + step], preferred_element_type=jnp.float32)
            )
        total_ref[b] = total
        mixed_ref[b] = mixed


def piece_sums(starts, spans, row_refs, refs):
    groups = len(row_refs) // 2
    slot_count, draft_count, _ = row_refs[1].shape
    drafts = groups * slot_count * draft_count
    total = None
    for start, (n, first, depth) in zip(starts, spans):
        lanes = pl.ds(pl.multiple_of(start, HEAD_SIZE), depth)
        stack = [ref[b, :, lanes].astype(jnp.float32) for ref in row_refs[1::2] for b in range(slot_count)]
        if drafts < 16:
            stack.append(jnp.zeros((16 - drafts, depth), jnp.float32))
        rows = [ref[:, lanes] for ref in row_refs[0::2]] + [jnp.concatenate(stack, 0).astype(jnp.bfloat16)]
        piece = refs[n][first : first + depth, :]
        product = jnp.dot(jnp.concatenate(rows, 0), piece, preferred_element_type=jnp.float32)
        total = product if total is None else total + product
    return total


def down_kernel(starts_of, spans, first, *refs):
    row_refs, refs, out_ref = refs[:4], refs[4:-1], refs[-1]
    total = piece_sums(starts_of(), spans, row_refs, refs)
    out_ref[...] = total if first else total + refs[-1][...]


def down_place_kernel(starts_of, spans, *refs):
    row_refs, refs, (keep_ref, send_ref) = refs[:4], refs[4:-2], refs[-2:]
    place_ref, sum_ref, refs = refs[0], refs[1], refs[2:]
    total = piece_sums(starts_of(), spans, row_refs, refs) + sum_ref[...]
    slots, width = keep_ref.shape[0] - 8, keep_ref.shape[1]
    count = place_ref.shape[1]
    parts = []
    left = total[:count]
    for _ in range(3):
        part = left.astype(jnp.bfloat16)
        parts.append(part)
        left = left - part.astype(jnp.float32)
    parts = jnp.concatenate(parts, 1)
    core = lax.axis_index("wide") % 2
    spot = lax.broadcasted_iota(jnp.int32, (slots, count), 0)
    for ref, target, draft in ((keep_ref, core, count), (send_ref, 1 - core, count + 8)):
        chosen = jnp.where(spot + target * slots == place_ref[...], 1.0, 0.0).astype(jnp.bfloat16)
        moved = jnp.dot(chosen, parts, preferred_element_type=jnp.float32)
        ref[:slots, :] = moved[:, :width] + moved[:, width : 2 * width] + moved[:, 2 * width :]
        ref[slots:, :] = total[draft : draft + 8]


def route_kernel(blocks, keep_ref, came_ref, draft_latent_ref, *refs):
    out_refs, float_ref = refs[:-1], refs[-1]
    float_ref[...] = keep_ref[...] + came_ref[...]
    slots = float_ref.shape[0] - 8
    draft_latent_ref[...] = float_ref[slots:, :].astype(jnp.bfloat16).astype(jnp.float32)
    size = slots // len(out_refs)
    for block, ref in zip(blocks(), out_refs):
        rows = pl.ds(pl.multiple_of(block * size, size), size)
        ref[...] = float_ref[rows, :].astype(jnp.bfloat16)


def start_kernel(most_rows, target_ref, other_ref, shard_hbm, place_ref, half_ref, full_ref, sems):
    half_rows, shard_rows = half_ref.shape[0] - 16, full_ref.shape[0] - 16
    mine = pl.ds(pl.multiple_of(lax.axis_index("rep") * half_rows, half_rows), half_rows)
    copies = [
        pltpu.make_async_copy(shard_hbm.at[mine], half_ref.at[:half_rows], sems.at[0]),
        pltpu.make_async_copy(shard_hbm, full_ref.at[:shard_rows], sems.at[1]),
    ]
    for copy in copies:
        copy.start()
    core = lax.axis_index("wide") % 2
    width, count = half_ref.shape[1], target_ref.shape[1]
    f32, bf16 = jnp.float32, jnp.bfloat16
    earlier = lax.broadcasted_iota(jnp.int32, (count, count), 0) < lax.broadcasted_iota(jnp.int32, (count, count), 1)
    earlier = jnp.where(earlier, 1.0, 0.0).astype(bf16)
    counts = []
    for n, (ref, owner) in enumerate(((target_ref, core), (other_ref, 1 - core))):
        target = ref[...]
        hit = jnp.where(lax.broadcasted_iota(jnp.int32, (width, count), 0) == target, 1.0, 0.0)
        counts.append(lax.dot_general(jnp.ones((16, count), bf16), hit.astype(bf16), NT, preferred_element_type=f32))
        before = jnp.dot(hit[:64].astype(bf16), earlier, preferred_element_type=f32)
        rank = jnp.sum(hit[:64] * before, 0, keepdims=True).astype(jnp.int32)
        spot = jnp.where(target % 2 == 0, rank, most_rows - 1 - rank)
        chip, side = target // 4, target // 2 % 2
        slots = place_ref.shape[1]
        place_ref[:, n * count : (n + 1) * count] = side * slots + (chip * 2 + owner) * most_rows + spot
    low = jnp.where(core == 0, counts[0], counts[1])
    high = jnp.where(core == 0, counts[1], counts[0])
    block = jnp.where(lax.broadcasted_iota(jnp.int32, (16, width), 0) == 0, low, high).astype(bf16)
    half_ref[half_rows:, :] = block
    full_ref[shard_rows:, :] = block
    for copy in copies:
        copy.wait()


def join_kernel(one_ref, two_ref, out_ref):
    rows = one_ref.shape[0]
    out_ref[:rows, :] = one_ref[...]
    out_ref[rows:, :] = two_ref[...]


def count_kernel(most_rows, spans, context_ref, *refs):
    refs, (limit_ref, column_slot_ref) = refs[:-2], refs[-2:]
    counts = jnp.concatenate([refs[n][first : first + 16, :].astype(jnp.float32)[:2] for n, first in spans], 0)
    lane = lax.broadcasted_iota(jnp.int32, counts.shape, 1)
    row = lax.broadcasted_iota(jnp.int32, counts.shape, 0)
    spread = []
    for b in range(2):
        number = jnp.sum(jnp.where(lane == lax.axis_index("wide") * 2 + b, counts, 0.0), 1, keepdims=True)
        limit = context_ref[b] - jnp.sum(number, 0, keepdims=True).astype(jnp.int32)
        limit_ref[b : b + 1, :] = jnp.broadcast_to(limit, (1, limit_ref.shape[1]))
        spread.append(jnp.sum(jnp.where(lane // most_rows == row, number, 0.0), 0, keepdims=True).astype(jnp.int32))
    spot = lax.broadcasted_iota(jnp.int32, column_slot_ref.shape, 1) % most_rows
    column_slot_ref[...] = jnp.where(spot < spread[0], 0, jnp.where(spot >= most_rows - spread[1], 1, -1))


def plain_down_kernel(place_ref, prompt_ref, draft_ref, weight_ref, outgoing_ref, draft_latent_ref):
    count, depth = prompt_ref.shape
    total = piece_sums([0], [(0, 0, depth)], [prompt_ref, draft_ref], [weight_ref])
    draft_latent_ref[...] = total[count : count + 8].astype(jnp.bfloat16).astype(jnp.float32)
    spot = lax.broadcasted_iota(jnp.int32, (outgoing_ref.shape[0], count), 0)
    chosen = jnp.where(spot == place_ref[...], 1.0, 0.0).astype(jnp.bfloat16)
    latent = total[:count].astype(jnp.bfloat16)
    outgoing_ref[...] = jnp.dot(chosen, latent, preferred_element_type=jnp.float32).astype(jnp.bfloat16)


def late_kernel(
    column_slot_ref, draft_latent_ref, turned_ref, peak_ref, total_ref, mixed_ref, value_up_ref, *refs
):
    incoming_refs, (out_ref, rows_ref, parted_ref) = refs[:-3], refs[-3:]
    slot_count, draft_count, _ = out_ref.shape
    tile = slot_count * draft_count
    heads_kv = value_up_ref.shape[1] // HEAD_SIZE
    group_size = QUERY_HEADS // heads_kv
    head_rows = group_size * draft_count
    rows = peak_ref.shape[1]
    block = incoming_refs[0].shape[0]
    arrived = block * len(incoming_refs)
    span = rows_ref.shape[0]
    drafts = jnp.concatenate([draft_latent_ref[...], jnp.zeros((span - arrived - tile, rows_ref.shape[1]), jnp.float32)], 0)
    for n, ref in enumerate(incoming_refs):
        rows_ref[n * block : (n + 1) * block, :] = ref[...]
    rows_ref[arrived:, :] = drafts.astype(jnp.bfloat16)
    token = lax.broadcasted_iota(jnp.int32, (rows, 1), 0) % draft_count
    column = lax.broadcasted_iota(jnp.int32, (rows, span - arrived), 1)
    for b in range(slot_count):
        scores = join_rows(lax.dot_general(turned_ref[b], rows_ref[...], NT, preferred_element_type=jnp.float32))
        draft_seen = (column >= b * draft_count) & (column <= b * draft_count + token)
        scores = jnp.concatenate(
            [
                jnp.where(column_slot_ref[...] == b, scores[:, :arrived], FAR),
                jnp.where(draft_seen, scores[:, arrived:], FAR),
            ],
            1,
        )
        peak = jnp.maximum(jnp.max(scores, 1, keepdims=True), peak_ref[b])
        weights = jnp.exp2(scores - peak)
        fade = jnp.exp2(peak_ref[b] - peak)
        total = total_ref[b] * fade + jnp.sum(weights, 1, keepdims=True)
        mixed = join_rows(jnp.dot(split_rows(weights), rows_ref[...], preferred_element_type=jnp.float32))
        parted_ref[b] = split_rows((mixed_ref[b] * fade + mixed) / total)
    for k in range(heads_kv):
        part = []
        for b in range(slot_count):
            part.append(parted_ref[b, k * head_rows : (k + 1) * head_rows, :])
            part.append(parted_ref[b, rows + k * head_rows : rows + (k + 1) * head_rows, :])
        value_up = value_up_ref[:, k * HEAD_SIZE : (k + 1) * HEAD_SIZE]
        both = jnp.dot(jnp.concatenate(part, 0), value_up, preferred_element_type=jnp.float32)
        for b in range(slot_count):
            result = join_rows(both[b * 2 * head_rows : (b + 1) * 2 * head_rows])
            wide = jnp.concatenate(
                [result[g * draft_count : (g + 1) * draft_count] for g in range(group_size)], 1
            )
            out_ref[b, :, k * group_size * HEAD_SIZE : (k + 1) * group_size * HEAD_SIZE] = wide.astype(jnp.bfloat16)


def deliver(prompt_hidden, draft_hidden, shard, row_target, context_len):
    shard_rows, width = shard.shape
    count = prompt_hidden.shape[0]
    sizes = (2, 4, 2, 2)
    spots = [(r, z, y, c) for r in range(2) for z in range(4) for y in range(2) for c in range(2)]
    most_rows = count // 8
    f32, bf16 = jnp.float32, jnp.bfloat16

    def flat(spot):
        return ((spot[0] * 4 + spot[1]) * 2 + spot[2]) * 2 + spot[3]

    def move(x, *steps):
        pairs = []
        for spot in spots:
            to = [(spot[a] + steps[a]) % sizes[a] for a in range(4)]
            pairs.append((flat(spot), flat(to)))
        return lax.ppermute(x, ("rep", "wide"), pairs)

    def array(rows, dtype=bf16):
        return jax.ShapeDtypeStruct((rows, width), dtype)

    def call(kernel, out_shape, name, *operands, specs=None, flops=2**24, **more):
        return pl.pallas_call(
            kernel,
            out_shape=out_shape,
            in_specs=specs or [WHOLE] * len(operands),
            out_specs=[WHOLE] * len(out_shape) if isinstance(out_shape, list) else WHOLE,
            compiler_params=params(16),
            cost_estimate=pl.CostEstimate(flops=flops, bytes_accessed=2**20, transcendentals=0),
            name=name,
            **more,
        )(*operands)

    target = row_target.reshape(1, count)
    other_target = move(target, 0, 0, 0, 1)
    half_rows = shard_rows // 2
    ext = half_rows + 16
    place, half, full = call(
        functools.partial(start_kernel, most_rows),
        [jax.ShapeDtypeStruct((1, 2 * count), jnp.int32), array(ext), array(shard_rows + 16)],
        "start_rows",
        target,
        other_target,
        pltpu.with_memory_space_constraint(shard, pltpu.HBM),
        specs=[WHOLE, WHOLE, pl.BlockSpec(memory_space=pltpu.HBM)],
        scratch_shapes=[pltpu.SemaphoreType.DMA((2,))],
    )
    z1, z3 = move(half, 0, 1, 0, 0), move(half, 0, 3, 0, 0)
    y0 = move(full, 0, 0, 1, 0)
    other_prompt, other_draft = move(prompt_hidden, 0, 0, 0, 1), move(draft_hidden, 0, 0, 0, 1)
    z2 = move(z1, 0, 1, 0, 0)
    z13 = call(join_kernel, array(2 * ext), "join_pieces", z1, z3)
    yz13, xz13 = move(z13, 0, 0, 1, 0), move(z13, 1, 0, 0, 0)
    yz2, xz2 = move(z2, 0, 0, 1, 0), move(z2, 1, 0, 0, 0)
    xyz13 = move(yz13, 1, 0, 0, 0)
    yxz2 = move(xz2, 0, 0, 1, 0)

    def starts_of(trails):
        def starts():
            rep, wide = lax.axis_index("rep"), lax.axis_index("wide")
            z, y, c = wide // 4, wide // 2 % 2, wide % 2
            return [
                (((z + 4 - z_step) % 4 * 2 + (y + y_step) % 2) * 2 + c) * shard_rows
                + (0 if x_step is None else (rep + x_step) % 2 * half_rows)
                for x_step, z_step, y_step in trails
            ]

        return starts

    rows = [prompt_hidden, draft_hidden, other_prompt, other_draft]
    stages = [
        ([full, y0], [(0, 0, shard_rows, (None, 0, 0)), (1, 0, shard_rows, (None, 0, 1))]),
        (
            [z13, yz13],
            [(0, 0, half_rows, (0, 1, 0)), (0, ext, half_rows, (0, 3, 0)),
             (1, 0, half_rows, (0, 1, 1)), (1, ext, half_rows, (0, 3, 1))],
        ),
        (
            [xz13, z2, yz2],
            [(0, 0, half_rows, (1, 1, 0)), (0, ext, half_rows, (1, 3, 0)),
             (1, 0, half_rows, (0, 2, 0)), (2, 0, half_rows, (0, 2, 1))],
        ),
        (
            [xz2, yxz2, xyz13],
            [(0, 0, half_rows, (1, 2, 0)), (1, 0, half_rows, (1, 2, 1)),
             (2, 0, half_rows, (1, 1, 1)), (2, ext, half_rows, (1, 3, 1))],
        ),
    ]
    sums = []
    total_rows = 2 * count + 16
    for n, (pieces, uses) in enumerate(stages[:-1]):
        spans, trails = [use[:3] for use in uses], [use[3] for use in uses]
        sums = [
            call(
                functools.partial(down_kernel, starts_of(trails), spans, n == 0),
                array(total_rows, f32), "down_rows", *rows, *pieces, *sums, flops=2**28,
            )
        ]

    trails = [(0, 0), (1, 0), (3, 0), (2, 0), (0, 1), (1, 1), (3, 1), (2, 1)]
    limit, column_slot = call(
        functools.partial(
            count_kernel, most_rows,
            [(0, half_rows), (1, half_rows), (1, ext + half_rows), (2, half_rows),
             (3, shard_rows), (4, half_rows), (4, ext + half_rows), (5, half_rows)],
        ),
        [jax.ShapeDtypeStruct((2, 128), jnp.int32), jax.ShapeDtypeStruct((1, 2 * count), jnp.int32)],
        "count_rows",
        context_len, half, z13, z2, y0, yz13, yz2,
        specs=[SCALARS] + [WHOLE] * 6,
    )

    def finish(tie):
        pieces, uses = stages[-1]
        spans, ways = [use[:3] for use in uses], [use[3] for use in uses]
        keep, send = call(
            functools.partial(down_place_kernel, starts_of(ways), spans),
            [array(2 * count + 8, f32)] * 2, "down_place_rows", *rows, place, *sums, *pieces, tie,
            specs=[WHOLE] * (6 + len(pieces)) + [UNREAD], flops=2**28,
        )
        came = move(send, 0, 0, 0, 1)

        def blocks():
            wide = lax.axis_index("wide")
            z, y = wide // 4, wide // 2 % 2
            return [(z + z_step) % 4 * 2 + (y + y_step) % 2 for z_step, y_step in trails]

        draft_latent, *outgoing = call(
            functools.partial(route_kernel, blocks),
            [array(8, f32)] + [array(2 * most_rows)] * len(trails), "route_rows", keep, came,
            scratch_shapes=[pltpu.VMEM((2 * count + 8, width), f32)],
        )
        incoming = [x if n == 0 else move(x, 0, *trails[n], 0) for n, x in enumerate(outgoing)]
        return draft_latent, incoming

    return limit, column_slot, finish


def deliver_plain(prompt_hidden, draft_hidden, shard, row_target, context_len):
    wide_size = lax.axis_size("wide")
    row_count = prompt_hidden.shape[0]
    slot_count, draft_count, _ = draft_hidden.shape
    latent_width = shard.shape[1]
    most_rows = 2 * ((row_count + wide_size - 1) // wide_size)
    arrived = wide_size * most_rows
    weight = lax.all_gather(shard, "wide", axis=0, tiled=True)
    index = jnp.arange(row_count, dtype=jnp.int32)
    same = (row_target[:, None] == row_target[None, :]) & (index[None, :] < index[:, None])
    rank = jnp.sum(same.astype(jnp.int32), 1)
    front = row_target % slot_count == 0
    place = row_target // slot_count * most_rows + jnp.where(front, rank, most_rows - 1 - rank)
    request = jnp.arange(wide_size * slot_count, dtype=jnp.int32)
    counts = jnp.sum((row_target[None, :] == request[:, None]).astype(jnp.int32), 1)
    counts = lax.all_to_all(counts.reshape(wide_size, slot_count), "wide", split_axis=0, concat_axis=0, tiled=True)
    limit = jnp.broadcast_to((context_len - jnp.sum(counts, 0))[:, None], (slot_count, 128))
    spot = jnp.arange(most_rows, dtype=jnp.int32)[None, :]
    column_slot = jnp.where(
        spot < counts[:, 0:1], 0, jnp.where(spot >= most_rows - counts[:, 1:2], 1, -1)
    ).reshape(1, arrived)

    def finish(tie):
        outgoing, draft_latent = pl.pallas_call(
            plain_down_kernel,
            out_shape=[
                jax.ShapeDtypeStruct((arrived, latent_width), jnp.bfloat16),
                jax.ShapeDtypeStruct((slot_count * draft_count, latent_width), jnp.float32),
            ],
            in_specs=[WHOLE] * 4,
            out_specs=[WHOLE] * 2,
            compiler_params=params(24),
            name="down_rows",
        )(place.reshape(1, row_count), prompt_hidden, draft_hidden, weight)
        incoming = lax.all_to_all(
            outgoing.reshape(wide_size, most_rows, latent_width), "wide", split_axis=0, concat_axis=0, tiled=True
        )
        return draft_latent, [incoming.reshape(arrived, latent_width)]

    return limit, column_slot, finish


def local(
    prompt_hidden,
    resident_latent,
    row_target,
    row_offset,
    context_len,
    draft_hidden,
    draft_query_heads,
    down_weight,
    key_up_weight,
    value_up_weight,
):
    f32, bf16 = jnp.float32, jnp.bfloat16
    slot_count, span_rows, latent_width = resident_latent.shape
    draft_count = draft_hidden.shape[1]
    rows = QUERY_HEADS * draft_count
    known = lax.axis_size("wide") == 16 and lax.axis_size("rep") == 2
    limit, column_slot, finish = (deliver if known else deliver_plain)(
        prompt_hidden, draft_hidden, down_weight, row_target, context_len
    )
    hbm = pl.BlockSpec(memory_space=pltpu.HBM)
    turned, peak, total, mixed = pl.pallas_call(
        held_kernel,
        out_shape=[
            jax.ShapeDtypeStruct((slot_count, 2 * rows, latent_width), bf16),
            jax.ShapeDtypeStruct((slot_count, rows, 1), f32),
            jax.ShapeDtypeStruct((slot_count, rows, 1), f32),
            jax.ShapeDtypeStruct((slot_count, rows, latent_width), f32),
        ],
        in_specs=[WHOLE, hbm, hbm, hbm],
        out_specs=[WHOLE] * 4,
        scratch_shapes=[
            pltpu.VMEM(draft_query_heads.shape, bf16),
            pltpu.VMEM(key_up_weight.shape, bf16),
            pltpu.VMEM(resident_latent.shape, bf16),
            pltpu.VMEM((slot_count, rows, latent_width), f32),
            pltpu.VMEM((rows, span_rows), f32),
            pltpu.SemaphoreType.DMA((3,)),
        ],
        compiler_params=params(16),
        cost_estimate=pl.CostEstimate(flops=2**31, bytes_accessed=2**22, transcendentals=2**19),
        name="held_rows",
    )(limit, *(pltpu.with_memory_space_constraint(x, pltpu.HBM) for x in (draft_query_heads, key_up_weight, resident_latent)))

    draft_latent, incoming = finish(peak)
    arrived = column_slot.shape[1]
    span = (arrived + slot_count * draft_count + 127) // 128 * 128
    return pl.pallas_call(
        late_kernel,
        out_shape=jax.ShapeDtypeStruct((slot_count, draft_count, QUERY_HEADS * HEAD_SIZE), bf16),
        in_specs=[WHOLE] * (7 + len(incoming)),
        out_specs=WHOLE,
        scratch_shapes=[
            pltpu.VMEM((span, latent_width), bf16),
            pltpu.VMEM((slot_count, 2 * rows, latent_width), bf16),
        ],
        compiler_params=params(16),
        name="late_rows",
    )(column_slot, draft_latent, turned, peak, total, mixed, value_up_weight, *incoming)


def solution(mesh):
    placed = (
        P(("rep", "wide"), None),
        P(("rep", "wide"), None, None),
        P(("rep", "wide")),
        P(("rep", "wide")),
        P(("rep", "wide")),
        P(("rep", "wide"), None, None),
        P(("rep", "wide"), None, None),
        P("wide", None),
        P(),
        P(),
    )
    return jax.shard_map(
        local, mesh=mesh, in_specs=placed, out_specs=P(("rep", "wide"), None, None), check_vma=False
    )
```

```python
import functools
import math

import jax
import jax.numpy as jnp
from jax import lax
from jax.experimental import pallas as pl
from jax.experimental.pallas import tpu as pltpu
from jax.sharding import PartitionSpec as P

QUERY_HEADS = 64
HEAD_SIZE = 128
FAR = -1e30
NT = (((1,), (1,)), ((), ()))
WHOLE = pl.BlockSpec(memory_space=pltpu.VMEM)
SCALARS = pl.BlockSpec(memory_space=pltpu.SMEM)
UNREAD = pl.BlockSpec(memory_space=pl.ANY)


def params(mib):
    return pltpu.CompilerParams(vmem_limit_bytes=mib * 1024 * 1024)


def split_rows(x):
    top = x.astype(jnp.bfloat16)
    rest = (x - top.astype(jnp.float32)).astype(jnp.bfloat16)
    return jnp.concatenate([top, rest], 0)


def join_rows(x):
    half = x.shape[0] // 2
    return x[:half] + x[half:]


def held_kernel(
    limit_ref, query_hbm, key_up_hbm, cache_hbm, turned_ref, peak_ref, total_ref, mixed_ref,
    query_ref, key_up_ref, cache_ref, float_ref, scores_ref, sems,
):
    copies = [
        pltpu.make_async_copy(source, target, sems.at[n])
        for n, (source, target) in enumerate(
            [(query_hbm, query_ref), (key_up_hbm, key_up_ref), (cache_hbm, cache_ref)]
        )
    ]
    for copy in copies:
        copy.start()
    slot_count, span_rows, _ = cache_ref.shape
    draft_count = query_ref.shape[1]
    heads_kv = key_up_ref.shape[1] // HEAD_SIZE
    group_size = QUERY_HEADS // heads_kv
    rows = group_size * draft_count
    scale = math.log2(math.e) / math.sqrt(HEAD_SIZE)
    step = 256
    copies[0].wait()
    copies[1].wait()
    for k in range(heads_kv):
        pieces = []
        for b in range(slot_count):
            for g in range(group_size):
                lane = (k * group_size + g) * HEAD_SIZE
                pieces.append(query_ref[b, :, lane : lane + HEAD_SIZE].astype(jnp.float32))
        query = jnp.concatenate(pieces, 0).astype(jnp.bfloat16)
        key_up = key_up_ref[:, k * HEAD_SIZE : (k + 1) * HEAD_SIZE]
        turned = lax.dot_general(query, key_up, NT, preferred_element_type=jnp.float32) * scale
        for b in range(slot_count):
            float_ref[b, k * rows : (k + 1) * rows, :] = turned[b * rows : (b + 1) * rows]
    copies[2].wait()
    for b in range(slot_count):
        turned_ref[b] = split_rows(float_ref[b])
        peak = None
        for c in range(0, span_rows, step):
            scores = join_rows(
                lax.dot_general(turned_ref[b], cache_ref[b, c : c + step], NT, preferred_element_type=jnp.float32)
            )
            column = lax.broadcasted_iota(jnp.int32, (1, step), 1) + c
            scores = jnp.where(column < limit_ref[b : b + 1, 0:1], scores, FAR)
            scores_ref[:, c : c + step] = scores
            top = jnp.max(scores, 1, keepdims=True)
            peak = top if peak is None else jnp.maximum(peak, top)
        peak_ref[b] = peak
        total = jnp.zeros_like(peak)
        mixed = jnp.zeros(mixed_ref.shape[1:], jnp.float32)
        for c in range(0, span_rows, step):
            weights = jnp.exp2(scores_ref[:, c : c + step] - peak)
            total += jnp.sum(weights, 1, keepdims=True)
            mixed += join_rows(
                jnp.dot(split_rows(weights), cache_ref[b, c : c + step], preferred_element_type=jnp.float32)
            )
        total_ref[b] = total
        mixed_ref[b] = mixed


def piece_sums(starts, spans, row_refs, refs):
    total = None
    for start, (n, first, depth) in zip(starts, spans):
        lanes = pl.ds(pl.multiple_of(start, HEAD_SIZE), depth)
        rows = [ref[:, lanes] for ref in row_refs]
        piece = refs[n][first : first + depth, :]
        product = jnp.dot(jnp.concatenate(rows, 0), piece, preferred_element_type=jnp.float32)
        total = product if total is None else total + product
    return total


def down_kernel(starts_of, spans, first, *refs):
    row_refs, refs, out_ref = refs[:3], refs[3:-1], refs[-1]
    total = piece_sums(starts_of(), spans, row_refs, refs)
    out_ref[...] = total if first else total + refs[-1][...]


def down_place_kernel(starts_of, spans, *refs):
    row_refs, refs, (keep_ref, send_ref) = refs[:3], refs[3:-2], refs[-2:]
    place_ref, sum_ref, refs = refs[0], refs[1], refs[2:]
    total = piece_sums(starts_of(), spans, row_refs, refs) + sum_ref[...]
    slots, width = keep_ref.shape[0] - 8, keep_ref.shape[1]
    count = place_ref.shape[1]
    parts = []
    left = total[:count]
    for _ in range(3):
        part = left.astype(jnp.bfloat16)
        parts.append(part)
        left = left - part.astype(jnp.float32)
    parts = jnp.concatenate(parts, 1)
    core = lax.axis_index("wide") % 2
    spot = lax.broadcasted_iota(jnp.int32, (slots, count), 0)
    for ref, target, draft in ((keep_ref, core, count), (send_ref, 1 - core, count + 8)):
        chosen = jnp.where(spot + target * slots == place_ref[...], 1.0, 0.0).astype(jnp.bfloat16)
        moved = jnp.dot(chosen, parts, preferred_element_type=jnp.float32)
        ref[:slots, :] = moved[:, :width] + moved[:, width : 2 * width] + moved[:, 2 * width :]
        ref[slots:, :] = total[draft : draft + 8]


def route_kernel(keep_ref, came_ref, draft_latent_ref, stay_ref, send_ref, float_ref):
    float_ref[...] = keep_ref[...] + came_ref[...]
    slots = float_ref.shape[0] - 8
    draft_latent_ref[...] = float_ref[slots:, :].astype(jnp.bfloat16).astype(jnp.float32)
    size = slots // 8
    wide = lax.axis_index("wide")
    z, y = wide // 4, wide // 2 % 2
    for other, ref in ((0, stay_ref), (1, send_ref)):
        for n, (high, low) in enumerate(((0, 0), (0, 1), (1, 0), (1, 1))):
            there = (z // 2 + high) % 2 * 2 + (z + low) % 2
            block = there * 2 + (y + other) % 2
            rows = pl.ds(pl.multiple_of(block * size, size), size)
            ref[n * size : (n + 1) * size, :] = float_ref[rows, :].astype(jnp.bfloat16)


def mix_kernel(outer, keep_ref, came_ref, stay_ref, send_ref):
    half = keep_ref.shape[0] // 2
    size = half // outer
    for ref, first in ((stay_ref, 0), (send_ref, half)):
        for n in range(outer):
            for m, source in enumerate((keep_ref, came_ref)):
                spot = (n * 2 + m) * size
                ref[spot : spot + size, :] = source[first + n * size : first + (n + 1) * size, :]


def start_kernel(target_hbm, shard_hbm, half_ref, full_ref, target_ref, sems):
    half_rows, shard_rows = half_ref.shape[0] - 16, full_ref.shape[0] - 16
    mine = pl.ds(pl.multiple_of(lax.axis_index("rep") * half_rows, half_rows), half_rows)
    copies = [
        pltpu.make_async_copy(target_hbm, target_ref, sems.at[0]),
        pltpu.make_async_copy(shard_hbm.at[mine], half_ref.at[:half_rows], sems.at[1]),
        pltpu.make_async_copy(shard_hbm, full_ref.at[:shard_rows], sems.at[2]),
    ]
    for copy in copies:
        copy.start()
    width, count = half_ref.shape[1], target_ref.shape[1]
    copies[0].wait()
    hit = lax.broadcasted_iota(jnp.int32, (width, count), 0) == target_ref[...]
    hit = jnp.where(hit, 1.0, 0.0).astype(jnp.bfloat16)
    block = lax.dot_general(jnp.ones((16, count), jnp.bfloat16), hit, NT, preferred_element_type=jnp.float32)
    half_ref[half_rows:, :] = block.astype(jnp.bfloat16)
    full_ref[shard_rows:, :] = block.astype(jnp.bfloat16)
    copies[1].wait()
    copies[2].wait()


def join_kernel(one_ref, two_ref, _, out_ref):
    rows = one_ref.shape[0]
    out_ref[:rows, :] = one_ref[...]
    out_ref[rows:, :] = two_ref[...]


def pack_kernel(spans, target_ref, draft_ref, *refs):
    refs, out_ref = refs[:-1], refs[-1]
    slot_count, draft_count, model_width = draft_ref.shape
    drafts = slot_count * draft_count
    rows = [draft_ref[b].astype(jnp.float32) for b in range(slot_count)]
    counts = [refs[n][first : first + 16, :].astype(jnp.float32)[:1] for n, first in spans]
    counts.append(target_ref[...].astype(jnp.float32))
    used = sum(x.shape[1] for x in counts)
    counts.append(jnp.zeros((1, model_width - used), jnp.float32))
    rows.append(jnp.broadcast_to(jnp.concatenate(counts, 1), (16 - drafts, model_width)))
    out_ref[...] = jnp.concatenate(rows, 0).astype(jnp.bfloat16)


def count_kernel(most_rows, context_ref, mine_ref, other_ref, _, limit_ref, column_slot_ref, place_ref, draft_ref):
    f32, bf16 = jnp.float32, jnp.bfloat16
    count, width = place_ref.shape[1] // 2, 256
    wide = lax.axis_index("wide")
    core = wide % 2
    mine, other = mine_ref[...].astype(f32), other_ref[...].astype(f32)
    draft_ref[...] = jnp.concatenate([mine[:8], other[:8]], 0).astype(bf16)
    low = jnp.where(core == 0, mine[8:9], other[8:9])
    high = jnp.where(core == 0, other[8:9], mine[8:9])
    counts = []
    for n in range(8):
        counts += [low[:, n * width : (n + 1) * width], high[:, n * width : (n + 1) * width]]
    counts = jnp.concatenate(counts, 0)
    lane = lax.broadcasted_iota(jnp.int32, counts.shape, 1)
    row = lax.broadcasted_iota(jnp.int32, counts.shape, 0)
    spread = []
    for b in range(2):
        number = jnp.sum(jnp.where(lane == wide * 2 + b, counts, 0.0), 1, keepdims=True)
        limit = context_ref[b] - jnp.sum(number, 0, keepdims=True).astype(jnp.int32)
        limit_ref[b : b + 1, :] = jnp.broadcast_to(limit, (1, limit_ref.shape[1]))
        spread.append(jnp.sum(jnp.where(lane // most_rows == row, number, 0.0), 0, keepdims=True).astype(jnp.int32))
    spot = lax.broadcasted_iota(jnp.int32, column_slot_ref.shape, 1) % most_rows
    column_slot_ref[...] = jnp.where(spot < spread[0], 0, jnp.where(spot >= most_rows - spread[1], 1, -1))
    earlier = lax.broadcasted_iota(jnp.int32, (count, count), 0) < lax.broadcasted_iota(jnp.int32, (count, count), 1)
    earlier = jnp.where(earlier, 1.0, 0.0).astype(bf16)
    for n, (rows, owner) in enumerate(((mine, core), (other, 1 - core))):
        target = rows[8:9, 8 * width : 8 * width + count].astype(jnp.int32)
        hit = jnp.where(lax.broadcasted_iota(jnp.int32, (64, count), 0) == target, 1.0, 0.0)
        before = jnp.dot(hit.astype(bf16), earlier, preferred_element_type=f32)
        rank = jnp.sum(hit * before, 0, keepdims=True).astype(jnp.int32)
        spot = jnp.where(target % 2 == 0, rank, most_rows - 1 - rank)
        chip, side = target // 4, target // 2 % 2
        place_ref[:, n * count : (n + 1) * count] = side * 2 * count + (chip * 2 + owner) * most_rows + spot


def plain_down_kernel(place_ref, prompt_ref, draft_ref, weight_ref, outgoing_ref, draft_latent_ref):
    count = prompt_ref.shape[0]
    rows = jnp.concatenate([prompt_ref[...], draft_ref[...]], 0)
    total = jnp.dot(rows, weight_ref[...], preferred_element_type=jnp.float32)
    draft_latent_ref[...] = total[count : count + 8].astype(jnp.bfloat16).astype(jnp.float32)
    spot = lax.broadcasted_iota(jnp.int32, (outgoing_ref.shape[0], count), 0)
    chosen = jnp.where(spot == place_ref[...], 1.0, 0.0).astype(jnp.bfloat16)
    latent = total[:count].astype(jnp.bfloat16)
    outgoing_ref[...] = jnp.dot(chosen, latent, preferred_element_type=jnp.float32).astype(jnp.bfloat16)


def late_kernel(
    column_slot_ref, draft_latent_ref, turned_ref, peak_ref, total_ref, mixed_ref, value_up_ref, *refs
):
    incoming_refs, (out_ref, rows_ref, parted_ref) = refs[:-3], refs[-3:]
    slot_count, draft_count, _ = out_ref.shape
    tile = slot_count * draft_count
    heads_kv = value_up_ref.shape[1] // HEAD_SIZE
    group_size = QUERY_HEADS // heads_kv
    head_rows = group_size * draft_count
    rows = peak_ref.shape[1]
    block = incoming_refs[0].shape[0]
    arrived = block * len(incoming_refs)
    span = rows_ref.shape[0]
    drafts = jnp.concatenate([draft_latent_ref[...], jnp.zeros((span - arrived - tile, rows_ref.shape[1]), jnp.float32)], 0)
    for n, ref in enumerate(incoming_refs):
        rows_ref[n * block : (n + 1) * block, :] = ref[...]
    rows_ref[arrived:, :] = drafts.astype(jnp.bfloat16)
    token = lax.broadcasted_iota(jnp.int32, (rows, 1), 0) % draft_count
    column = lax.broadcasted_iota(jnp.int32, (rows, span - arrived), 1)
    for b in range(slot_count):
        scores = join_rows(lax.dot_general(turned_ref[b], rows_ref[...], NT, preferred_element_type=jnp.float32))
        draft_seen = (column >= b * draft_count) & (column <= b * draft_count + token)
        scores = jnp.concatenate(
            [
                jnp.where(column_slot_ref[...] == b, scores[:, :arrived], FAR),
                jnp.where(draft_seen, scores[:, arrived:], FAR),
            ],
            1,
        )
        peak = jnp.maximum(jnp.max(scores, 1, keepdims=True), peak_ref[b])
        weights = jnp.exp2(scores - peak)
        fade = jnp.exp2(peak_ref[b] - peak)
        total = total_ref[b] * fade + jnp.sum(weights, 1, keepdims=True)
        mixed = join_rows(jnp.dot(split_rows(weights), rows_ref[...], preferred_element_type=jnp.float32))
        parted_ref[b] = split_rows((mixed_ref[b] * fade + mixed) / total)
    for k in range(heads_kv):
        part = []
        for b in range(slot_count):
            part.append(parted_ref[b, k * head_rows : (k + 1) * head_rows, :])
            part.append(parted_ref[b, rows + k * head_rows : rows + (k + 1) * head_rows, :])
        value_up = value_up_ref[:, k * HEAD_SIZE : (k + 1) * HEAD_SIZE]
        both = jnp.dot(jnp.concatenate(part, 0), value_up, preferred_element_type=jnp.float32)
        for b in range(slot_count):
            result = join_rows(both[b * 2 * head_rows : (b + 1) * 2 * head_rows])
            wide = jnp.concatenate(
                [result[g * draft_count : (g + 1) * draft_count] for g in range(group_size)], 1
            )
            out_ref[b, :, k * group_size * HEAD_SIZE : (k + 1) * group_size * HEAD_SIZE] = wide.astype(jnp.bfloat16)


def deliver(prompt_hidden, draft_hidden, shard, row_target, context_len):
    shard_rows, width = shard.shape
    count = prompt_hidden.shape[0]
    spots = [(r, z, y, c) for r in range(2) for z in range(4) for y in range(2) for c in range(2)]
    most_rows = count // 8
    f32, bf16 = jnp.float32, jnp.bfloat16

    def flat(spot):
        return ((spot[0] * 4 + spot[1]) * 2 + spot[2]) * 2 + spot[3]

    def swap(x, r=0, z=0, y=0, c=0):
        pairs = [(flat(spot), flat([a ^ b for a, b in zip(spot, (r, z, y, c))])) for spot in spots]
        return lax.ppermute(x, ("rep", "wide"), pairs)

    def array(rows, dtype=bf16):
        return jax.ShapeDtypeStruct((rows, width), dtype)

    def call(kernel, out_shape, name, *operands, specs=None, flops=2**20, **more):
        return pl.pallas_call(
            kernel,
            out_shape=out_shape,
            in_specs=specs or [WHOLE] * len(operands),
            out_specs=[WHOLE] * len(out_shape) if isinstance(out_shape, list) else WHOLE,
            compiler_params=params(16),
            cost_estimate=pl.CostEstimate(flops=flops, bytes_accessed=2**16, transcendentals=0),
            name=name,
            **more,
        )(*operands)

    hbm = pl.BlockSpec(memory_space=pltpu.HBM)
    half_rows = shard_rows // 2
    ext = half_rows + 16
    half, full, target = call(
        start_kernel,
        [array(ext), array(shard_rows + 16), jax.ShapeDtypeStruct((1, count), jnp.int32)],
        "start_rows",
        *(pltpu.with_memory_space_constraint(x, pltpu.HBM) for x in (row_target.reshape(1, count), shard)),
        specs=[hbm, hbm],
        scratch_shapes=[pltpu.SemaphoreType.DMA((3,))],
    )
    za, zb = swap(half, z=1), swap(half, z=2)
    y0 = swap(full, y=1)
    other_prompt = swap(prompt_hidden, c=1)
    zab = call(join_kernel, array(2 * ext), "join_pieces", za, zb, y0, specs=[WHOLE, WHOLE, UNREAD])
    yab, xab = swap(zab, y=1), swap(zab, r=1)
    zc = swap(zb, z=1)
    yc, xc = swap(zc, y=1), swap(zc, r=1)
    xyab = swap(yab, r=1)
    yxc = swap(xc, y=1)

    order = [
        (half, half_rows), (y0, shard_rows), (zab, ext + half_rows), (yab, ext + half_rows),
        (zab, half_rows), (yab, half_rows), (zc, half_rows), (yc, half_rows),
    ]
    pack = call(
        functools.partial(pack_kernel, [(n, first) for n, (_, first) in enumerate(order)]),
        jax.ShapeDtypeStruct((16, draft_hidden.shape[2]), bf16), "pack_rows",
        target, draft_hidden, *(x for x, _ in order), xab,
        specs=[WHOLE] * (2 + len(order)) + [UNREAD],
    )
    other_pack = swap(pack, c=1)
    limit, column_slot, place, drafts = call(
        functools.partial(count_kernel, most_rows),
        [
            jax.ShapeDtypeStruct((2, 128), jnp.int32),
            jax.ShapeDtypeStruct((1, 2 * count), jnp.int32),
            jax.ShapeDtypeStruct((1, 2 * count), jnp.int32),
            jax.ShapeDtypeStruct(pack.shape, bf16),
        ],
        "count_rows", context_len, pack, other_pack, xc,
        specs=[SCALARS, WHOLE, WHOLE, UNREAD],
    )

    def starts_of(uses):
        def starts():
            rep, wide = lax.axis_index("rep"), lax.axis_index("wide")
            z, y, c = wide // 4, wide // 2 % 2, wide % 2
            found = []
            for _, _, _, (x_step, z_step, y_step) in uses:
                owner_z = (z // 2 + z_step // 2) % 2 * 2 + (z + z_step) % 2
                owner = (owner_z * 2 + (y + y_step) % 2) * 2 + c
                found.append(owner * shard_rows + (0 if x_step is None else (rep + x_step) % 2 * half_rows))
            return found

        return starts

    rows = [prompt_hidden, other_prompt, drafts]
    stages = [
        ([full, y0], [(0, 0, shard_rows, (None, 0, 0)), (1, 0, shard_rows, (None, 0, 1))]),
        (
            [zab, yab],
            [(0, 0, half_rows, (0, 1, 0)), (0, ext, half_rows, (0, 2, 0)),
             (1, 0, half_rows, (0, 1, 1)), (1, ext, half_rows, (0, 2, 1))],
        ),
        (
            [xab, zc, yc],
            [(0, 0, half_rows, (1, 1, 0)), (0, ext, half_rows, (1, 2, 0)),
             (1, 0, half_rows, (0, 3, 0)), (2, 0, half_rows, (0, 3, 1))],
        ),
        (
            [xc, yxc, xyab],
            [(0, 0, half_rows, (1, 3, 0)), (1, 0, half_rows, (1, 3, 1)),
             (2, 0, half_rows, (1, 1, 1)), (2, ext, half_rows, (1, 2, 1))],
        ),
    ]
    sums = []
    total_rows = 2 * count + 16
    for n, (pieces, uses) in enumerate(stages[:-1]):
        sums = [
            call(
                functools.partial(down_kernel, starts_of(uses), [use[:3] for use in uses], n == 0),
                array(total_rows, f32), "down_rows", *rows, *pieces, *sums, flops=2**26,
            )
        ]

    def finish(tie):
        pieces, uses = stages[-1]
        keep, send = call(
            functools.partial(down_place_kernel, starts_of(uses), [use[:3] for use in uses]),
            [array(2 * count + 8, f32)] * 2, "down_place_rows", *rows, place, *sums, *pieces, tie,
            specs=[WHOLE] * (5 + len(pieces)) + [UNREAD], flops=2**26,
        )
        came = swap(send, c=1)
        block = array(count)
        draft_latent, stay, send = call(
            route_kernel, [array(8, f32), block, block], "route_rows", keep, came,
            scratch_shapes=[pltpu.VMEM((2 * count + 8, width), f32)],
        )
        came = swap(send, y=1)
        stay, send = call(functools.partial(mix_kernel, 2), [block, block], "mix_rows", stay, came)
        came = swap(send, z=2)
        stay, send = call(functools.partial(mix_kernel, 1), [block, block], "mix_rows", stay, came)
        return draft_latent, [stay, swap(send, z=1)]

    return limit, column_slot, finish


def deliver_plain(prompt_hidden, draft_hidden, shard, row_target, context_len):
    wide_size = lax.axis_size("wide")
    row_count = prompt_hidden.shape[0]
    slot_count, draft_count, _ = draft_hidden.shape
    latent_width = shard.shape[1]
    most_rows = 2 * ((row_count + wide_size - 1) // wide_size)
    arrived = wide_size * most_rows
    weight = lax.all_gather(shard, "wide", axis=0, tiled=True)
    index = jnp.arange(row_count, dtype=jnp.int32)
    same = (row_target[:, None] == row_target[None, :]) & (index[None, :] < index[:, None])
    rank = jnp.sum(same.astype(jnp.int32), 1)
    front = row_target % slot_count == 0
    place = row_target // slot_count * most_rows + jnp.where(front, rank, most_rows - 1 - rank)
    request = jnp.arange(wide_size * slot_count, dtype=jnp.int32)
    counts = jnp.sum((row_target[None, :] == request[:, None]).astype(jnp.int32), 1)
    counts = lax.all_to_all(counts.reshape(wide_size, slot_count), "wide", split_axis=0, concat_axis=0, tiled=True)
    limit = jnp.broadcast_to((context_len - jnp.sum(counts, 0))[:, None], (slot_count, 128))
    spot = jnp.arange(most_rows, dtype=jnp.int32)[None, :]
    column_slot = jnp.where(
        spot < counts[:, 0:1], 0, jnp.where(spot >= most_rows - counts[:, 1:2], 1, -1)
    ).reshape(1, arrived)

    tile = slot_count * draft_count
    draft_flat = jnp.pad(draft_hidden.reshape(tile, draft_hidden.shape[2]), ((0, 16 - tile), (0, 0)))

    def finish(tie):
        outgoing, draft_latent = pl.pallas_call(
            plain_down_kernel,
            out_shape=[
                jax.ShapeDtypeStruct((arrived, latent_width), jnp.bfloat16),
                jax.ShapeDtypeStruct((slot_count * draft_count, latent_width), jnp.float32),
            ],
            in_specs=[WHOLE] * 4,
            out_specs=[WHOLE] * 2,
            compiler_params=params(24),
            name="down_rows",
        )(place.reshape(1, row_count), prompt_hidden, draft_flat, weight)
        incoming = lax.all_to_all(
            outgoing.reshape(wide_size, most_rows, latent_width), "wide", split_axis=0, concat_axis=0, tiled=True
        )
        return draft_latent, [incoming.reshape(arrived, latent_width)]

    return limit, column_slot, finish


def local(
    prompt_hidden,
    resident_latent,
    row_target,
    row_offset,
    context_len,
    draft_hidden,
    draft_query_heads,
    down_weight,
    key_up_weight,
    value_up_weight,
):
    f32, bf16 = jnp.float32, jnp.bfloat16
    slot_count, span_rows, latent_width = resident_latent.shape
    draft_count = draft_hidden.shape[1]
    rows = QUERY_HEADS * draft_count
    known = lax.axis_size("wide") == 16 and lax.axis_size("rep") == 2
    limit, column_slot, finish = (deliver if known else deliver_plain)(
        prompt_hidden, draft_hidden, down_weight, row_target, context_len
    )
    hbm = pl.BlockSpec(memory_space=pltpu.HBM)
    turned, peak, total, mixed = pl.pallas_call(
        held_kernel,
        out_shape=[
            jax.ShapeDtypeStruct((slot_count, 2 * rows, latent_width), bf16),
            jax.ShapeDtypeStruct((slot_count, rows, 1), f32),
            jax.ShapeDtypeStruct((slot_count, rows, 1), f32),
            jax.ShapeDtypeStruct((slot_count, rows, latent_width), f32),
        ],
        in_specs=[WHOLE, hbm, hbm, hbm],
        out_specs=[WHOLE] * 4,
        scratch_shapes=[
            pltpu.VMEM(draft_query_heads.shape, bf16),
            pltpu.VMEM(key_up_weight.shape, bf16),
            pltpu.VMEM(resident_latent.shape, bf16),
            pltpu.VMEM((slot_count, rows, latent_width), f32),
            pltpu.VMEM((rows, span_rows), f32),
            pltpu.SemaphoreType.DMA((3,)),
        ],
        compiler_params=params(16),
        cost_estimate=pl.CostEstimate(flops=2**31, bytes_accessed=2**22, transcendentals=2**19),
        name="held_rows",
    )(limit, *(pltpu.with_memory_space_constraint(x, pltpu.HBM) for x in (draft_query_heads, key_up_weight, resident_latent)))

    draft_latent, incoming = finish(peak)
    arrived = column_slot.shape[1]
    span = (arrived + slot_count * draft_count + 127) // 128 * 128
    return pl.pallas_call(
        late_kernel,
        out_shape=jax.ShapeDtypeStruct((slot_count, draft_count, QUERY_HEADS * HEAD_SIZE), bf16),
        in_specs=[WHOLE] * (7 + len(incoming)),
        out_specs=WHOLE,
        scratch_shapes=[
            pltpu.VMEM((span, latent_width), bf16),
            pltpu.VMEM((slot_count, 2 * rows, latent_width), bf16),
        ],
        compiler_params=params(16),
        name="late_rows",
    )(column_slot, draft_latent, turned, peak, total, mixed, value_up_weight, *incoming)


def solution(mesh):
    placed = (
        P(("rep", "wide"), None),
        P(("rep", "wide"), None, None),
        P(("rep", "wide")),
        P(("rep", "wide")),
        P(("rep", "wide")),
        P(("rep", "wide"), None, None),
        P(("rep", "wide"), None, None),
        P("wide", None),
        P(),
        P(),
    )
    return jax.shard_map(
        local, mesh=mesh, in_specs=placed, out_specs=P(("rep", "wide"), None, None), check_vma=False
    )
```

```python
import functools
import math

import jax
import jax.numpy as jnp
from jax import lax
from jax.experimental import pallas as pl
from jax.experimental.pallas import tpu as pltpu
from jax.sharding import PartitionSpec as P

QUERY_HEADS = 64
HEAD_SIZE = 128
FAR = -1e30
NT = (((1,), (1,)), ((), ()))
WHOLE = pl.BlockSpec(memory_space=pltpu.VMEM)
SCALARS = pl.BlockSpec(memory_space=pltpu.SMEM)
UNREAD = pl.BlockSpec(memory_space=pl.ANY)


def params(mib):
    return pltpu.CompilerParams(vmem_limit_bytes=mib * 1024 * 1024)


def split_rows(x):
    top = x.astype(jnp.bfloat16)
    rest = (x - top.astype(jnp.float32)).astype(jnp.bfloat16)
    return jnp.concatenate([top, rest], 0)


def join_rows(x):
    half = x.shape[0] // 2
    return x[:half] + x[half:]


def held_kernel(
    limit_ref, query_hbm, key_up_hbm, cache_hbm, turned_ref, peak_ref, total_ref, mixed_ref,
    query_ref, key_up_ref, cache_ref, float_ref, scores_ref, sems,
):
    copies = [
        pltpu.make_async_copy(source, target, sems.at[n])
        for n, (source, target) in enumerate(
            [(query_hbm, query_ref), (key_up_hbm, key_up_ref), (cache_hbm, cache_ref)]
        )
    ]
    for copy in copies:
        copy.start()
    slot_count, span_rows, _ = cache_ref.shape
    draft_count = query_ref.shape[1]
    heads_kv = key_up_ref.shape[1] // HEAD_SIZE
    group_size = QUERY_HEADS // heads_kv
    rows = group_size * draft_count
    scale = math.log2(math.e) / math.sqrt(HEAD_SIZE)
    step = 256
    copies[0].wait()
    copies[1].wait()
    for k in range(heads_kv):
        pieces = []
        for b in range(slot_count):
            for g in range(group_size):
                lane = (k * group_size + g) * HEAD_SIZE
                pieces.append(query_ref[b, :, lane : lane + HEAD_SIZE].astype(jnp.float32))
        query = jnp.concatenate(pieces, 0).astype(jnp.bfloat16)
        key_up = key_up_ref[:, k * HEAD_SIZE : (k + 1) * HEAD_SIZE]
        turned = lax.dot_general(query, key_up, NT, preferred_element_type=jnp.float32) * scale
        for b in range(slot_count):
            float_ref[b, k * rows : (k + 1) * rows, :] = turned[b * rows : (b + 1) * rows]
    copies[2].wait()
    for b in range(slot_count):
        turned_ref[b] = split_rows(float_ref[b])
        peak = None
        for c in range(0, span_rows, step):
            scores = join_rows(
                lax.dot_general(turned_ref[b], cache_ref[b, c : c + step], NT, preferred_element_type=jnp.float32)
            )
            column = lax.broadcasted_iota(jnp.int32, (1, step), 1) + c
            scores = jnp.where(column < limit_ref[b : b + 1, 0:1], scores, FAR)
            scores_ref[:, c : c + step] = scores
            top = jnp.max(scores, 1, keepdims=True)
            peak = top if peak is None else jnp.maximum(peak, top)
        peak_ref[b] = peak
        total = jnp.zeros_like(peak)
        mixed = jnp.zeros(mixed_ref.shape[1:], jnp.float32)
        for c in range(0, span_rows, step):
            weights = jnp.exp2(scores_ref[:, c : c + step] - peak)
            total += jnp.sum(weights, 1, keepdims=True)
            mixed += join_rows(
                jnp.dot(split_rows(weights), cache_ref[b, c : c + step], preferred_element_type=jnp.float32)
            )
        total_ref[b] = total
        mixed_ref[b] = mixed


def piece_sums(starts, spans, row_refs, refs):
    total = None
    for start, (n, first, depth) in zip(starts, spans):
        lanes = pl.ds(pl.multiple_of(start, HEAD_SIZE), depth)
        rows = [ref[:, lanes] for ref in row_refs]
        piece = refs[n][first : first + depth, :]
        product = jnp.dot(jnp.concatenate(rows, 0), piece, preferred_element_type=jnp.float32)
        total = product if total is None else total + product
    return total


def down_kernel(starts_of, spans, first, *refs):
    row_refs, refs, out_ref = refs[:3], refs[3:-1], refs[-1]
    total = piece_sums(starts_of(), spans, row_refs, refs)
    out_ref[...] = total if first else total + refs[-1][...]


def down_place_kernel(starts_of, spans, *refs):
    row_refs, refs, (keep_ref, send_ref) = refs[:3], refs[3:-2], refs[-2:]
    place_ref, sum_ref, refs = refs[0], refs[1], refs[2:]
    total = piece_sums(starts_of(), spans, row_refs, refs) + sum_ref[...]
    slots, width = keep_ref.shape[0] - 8, keep_ref.shape[1]
    count = place_ref.shape[1]
    parts = []
    left = total[:count]
    for _ in range(3):
        part = left.astype(jnp.bfloat16)
        parts.append(part)
        left = left - part.astype(jnp.float32)
    parts = jnp.concatenate(parts, 1)
    core = lax.axis_index("wide") % 2
    spot = lax.broadcasted_iota(jnp.int32, (slots, count), 0)
    for ref, target, draft in ((keep_ref, core, count), (send_ref, 1 - core, count + 8)):
        chosen = jnp.where(spot + target * slots == place_ref[...], 1.0, 0.0).astype(jnp.bfloat16)
        moved = jnp.dot(chosen, parts, preferred_element_type=jnp.float32)
        ref[:slots, :] = moved[:, :width] + moved[:, width : 2 * width] + moved[:, 2 * width :]
        ref[slots:, :] = total[draft : draft + 8]


def route_kernel(keep_ref, came_ref, draft_latent_ref, stay_ref, send_ref, float_ref):
    float_ref[...] = keep_ref[...] + came_ref[...]
    slots = float_ref.shape[0] - 8
    draft_latent_ref[...] = float_ref[slots:, :].astype(jnp.bfloat16).astype(jnp.float32)
    size = slots // 8
    wide = lax.axis_index("wide")
    z, y = wide // 4, wide // 2 % 2
    for other, ref in ((0, stay_ref), (1, send_ref)):
        for n, (high, low) in enumerate(((0, 0), (0, 1), (1, 0), (1, 1))):
            there = (z // 2 + high) % 2 * 2 + (z + low) % 2
            block = there * 2 + (y + other) % 2
            rows = pl.ds(pl.multiple_of(block * size, size), size)
            ref[n * size : (n + 1) * size, :] = float_ref[rows, :].astype(jnp.bfloat16)


def mix_kernel(outer, keep_ref, came_ref, stay_ref, send_ref):
    half = keep_ref.shape[0] // 2
    size = half // outer
    for ref, first in ((stay_ref, 0), (send_ref, half)):
        for n in range(outer):
            for m, source in enumerate((keep_ref, came_ref)):
                spot = (n * 2 + m) * size
                ref[spot : spot + size, :] = source[first + n * size : first + (n + 1) * size, :]


def start_kernel(target_hbm, shard_hbm, draft_hbm, half_ref, full_ref, target_ref, draft_ref, sems):
    half_rows, shard_rows = half_ref.shape[0] - 16, full_ref.shape[0] - 16
    mine = pl.ds(pl.multiple_of(lax.axis_index("rep") * half_rows, half_rows), half_rows)
    copies = [
        pltpu.make_async_copy(target_hbm, target_ref, sems.at[0]),
        pltpu.make_async_copy(shard_hbm.at[mine], half_ref.at[:half_rows], sems.at[1]),
        pltpu.make_async_copy(shard_hbm, full_ref.at[:shard_rows], sems.at[2]),
        pltpu.make_async_copy(draft_hbm, draft_ref, sems.at[3]),
    ]
    for copy in copies:
        copy.start()
    width, count = half_ref.shape[1], target_ref.shape[1]
    copies[0].wait()
    hit = lax.broadcasted_iota(jnp.int32, (width, count), 0) == target_ref[...]
    hit = jnp.where(hit, 1.0, 0.0).astype(jnp.bfloat16)
    block = lax.dot_general(jnp.ones((16, count), jnp.bfloat16), hit, NT, preferred_element_type=jnp.float32)
    half_ref[half_rows:, :] = block.astype(jnp.bfloat16)
    full_ref[shard_rows:, :] = block.astype(jnp.bfloat16)
    for copy in copies[1:]:
        copy.wait()


def join_kernel(one_ref, two_ref, y0_ref, prompt_ref, out_ref):
    rows = one_ref.shape[0]
    out_ref[:rows, :] = one_ref[...]
    out_ref[rows:, :] = two_ref[...]


def pack_kernel(spans, target_ref, draft_ref, *refs):
    refs, out_ref = refs[:-1], refs[-1]
    slot_count, draft_count, model_width = draft_ref.shape
    drafts = slot_count * draft_count
    rows = [draft_ref[b].astype(jnp.float32) for b in range(slot_count)]
    counts = [refs[n][first : first + 16, :].astype(jnp.float32)[:1] for n, first in spans]
    counts.append(target_ref[...].astype(jnp.float32))
    used = sum(x.shape[1] for x in counts)
    counts.append(jnp.zeros((1, model_width - used), jnp.float32))
    rows.append(jnp.broadcast_to(jnp.concatenate(counts, 1), (16 - drafts, model_width)))
    out_ref[...] = jnp.concatenate(rows, 0).astype(jnp.bfloat16)


def count_kernel(most_rows, context_ref, mine_ref, other_ref, limit_ref, column_slot_ref, place_ref, draft_ref):
    f32, bf16 = jnp.float32, jnp.bfloat16
    count, width = place_ref.shape[1] // 2, 256
    wide = lax.axis_index("wide")
    core = wide % 2
    mine, other = mine_ref[...].astype(f32), other_ref[...].astype(f32)
    draft_ref[...] = jnp.concatenate([mine[:8], other[:8]], 0).astype(bf16)
    low = jnp.where(core == 0, mine[8:9], other[8:9])
    high = jnp.where(core == 0, other[8:9], mine[8:9])
    counts = []
    for n in range(8):
        counts += [low[:, n * width : (n + 1) * width], high[:, n * width : (n + 1) * width]]
    counts = jnp.concatenate(counts, 0)
    lane = lax.broadcasted_iota(jnp.int32, counts.shape, 1)
    row = lax.broadcasted_iota(jnp.int32, counts.shape, 0)
    spread = []
    for b in range(2):
        number = jnp.sum(jnp.where(lane == wide * 2 + b, counts, 0.0), 1, keepdims=True)
        limit = context_ref[b] - jnp.sum(number, 0, keepdims=True).astype(jnp.int32)
        limit_ref[b : b + 1, :] = jnp.broadcast_to(limit, (1, limit_ref.shape[1]))
        spread.append(jnp.sum(jnp.where(lane // most_rows == row, number, 0.0), 0, keepdims=True).astype(jnp.int32))
    spot = lax.broadcasted_iota(jnp.int32, column_slot_ref.shape, 1) % most_rows
    column_slot_ref[...] = jnp.where(spot < spread[0], 0, jnp.where(spot >= most_rows - spread[1], 1, -1))
    earlier = lax.broadcasted_iota(jnp.int32, (count, count), 0) < lax.broadcasted_iota(jnp.int32, (count, count), 1)
    earlier = jnp.where(earlier, 1.0, 0.0).astype(bf16)
    for n, (rows, owner) in enumerate(((mine, core), (other, 1 - core))):
        target = rows[8:9, 8 * width : 8 * width + count].astype(jnp.int32)
        hit = jnp.where(lax.broadcasted_iota(jnp.int32, (64, count), 0) == target, 1.0, 0.0)
        before = jnp.dot(hit.astype(bf16), earlier, preferred_element_type=f32)
        rank = jnp.sum(hit * before, 0, keepdims=True).astype(jnp.int32)
        spot = jnp.where(target % 2 == 0, rank, most_rows - 1 - rank)
        chip, side = target // 4, target // 2 % 2
        place_ref[:, n * count : (n + 1) * count] = side * 2 * count + (chip * 2 + owner) * most_rows + spot


def plain_down_kernel(place_ref, prompt_ref, draft_ref, weight_ref, outgoing_ref, draft_latent_ref):
    count = prompt_ref.shape[0]
    rows = jnp.concatenate([prompt_ref[...], draft_ref[...]], 0)
    total = jnp.dot(rows, weight_ref[...], preferred_element_type=jnp.float32)
    draft_latent_ref[...] = total[count : count + 8].astype(jnp.bfloat16).astype(jnp.float32)
    spot = lax.broadcasted_iota(jnp.int32, (outgoing_ref.shape[0], count), 0)
    chosen = jnp.where(spot == place_ref[...], 1.0, 0.0).astype(jnp.bfloat16)
    latent = total[:count].astype(jnp.bfloat16)
    outgoing_ref[...] = jnp.dot(chosen, latent, preferred_element_type=jnp.float32).astype(jnp.bfloat16)


def late_kernel(
    column_slot_ref, draft_latent_ref, turned_ref, peak_ref, total_ref, mixed_ref, value_up_ref, *refs
):
    incoming_refs, (out_ref, rows_ref, parted_ref) = refs[:-3], refs[-3:]
    slot_count, draft_count, _ = out_ref.shape
    tile = slot_count * draft_count
    heads_kv = value_up_ref.shape[1] // HEAD_SIZE
    group_size = QUERY_HEADS // heads_kv
    head_rows = group_size * draft_count
    rows = peak_ref.shape[1]
    block = incoming_refs[0].shape[0]
    arrived = block * len(incoming_refs)
    span = rows_ref.shape[0]
    drafts = jnp.concatenate([draft_latent_ref[...], jnp.zeros((span - arrived - tile, rows_ref.shape[1]), jnp.float32)], 0)
    for n, ref in enumerate(incoming_refs):
        rows_ref[n * block : (n + 1) * block, :] = ref[...]
    rows_ref[arrived:, :] = drafts.astype(jnp.bfloat16)
    token = lax.broadcasted_iota(jnp.int32, (rows, 1), 0) % draft_count
    column = lax.broadcasted_iota(jnp.int32, (rows, span - arrived), 1)
    for b in range(slot_count):
        scores = join_rows(lax.dot_general(turned_ref[b], rows_ref[...], NT, preferred_element_type=jnp.float32))
        draft_seen = (column >= b * draft_count) & (column <= b * draft_count + token)
        scores = jnp.concatenate(
            [
                jnp.where(column_slot_ref[...] == b, scores[:, :arrived], FAR),
                jnp.where(draft_seen, scores[:, arrived:], FAR),
            ],
            1,
        )
        peak = jnp.maximum(jnp.max(scores, 1, keepdims=True), peak_ref[b])
        weights = jnp.exp2(scores - peak)
        fade = jnp.exp2(peak_ref[b] - peak)
        total = total_ref[b] * fade + jnp.sum(weights, 1, keepdims=True)
        mixed = join_rows(jnp.dot(split_rows(weights), rows_ref[...], preferred_element_type=jnp.float32))
        parted_ref[b] = split_rows((mixed_ref[b] * fade + mixed) / total)
    for k in range(heads_kv):
        part = []
        for b in range(slot_count):
            part.append(parted_ref[b, k * head_rows : (k + 1) * head_rows, :])
            part.append(parted_ref[b, rows + k * head_rows : rows + (k + 1) * head_rows, :])
        value_up = value_up_ref[:, k * HEAD_SIZE : (k + 1) * HEAD_SIZE]
        both = jnp.dot(jnp.concatenate(part, 0), value_up, preferred_element_type=jnp.float32)
        for b in range(slot_count):
            result = join_rows(both[b * 2 * head_rows : (b + 1) * 2 * head_rows])
            wide = jnp.concatenate(
                [result[g * draft_count : (g + 1) * draft_count] for g in range(group_size)], 1
            )
            out_ref[b, :, k * group_size * HEAD_SIZE : (k + 1) * group_size * HEAD_SIZE] = wide.astype(jnp.bfloat16)


def deliver(prompt_hidden, draft_hidden, shard, row_target, context_len):
    shard_rows, width = shard.shape
    count = prompt_hidden.shape[0]
    spots = [(r, z, y, c) for r in range(2) for z in range(4) for y in range(2) for c in range(2)]
    most_rows = count // 8
    f32, bf16 = jnp.float32, jnp.bfloat16

    def flat(spot):
        return ((spot[0] * 4 + spot[1]) * 2 + spot[2]) * 2 + spot[3]

    def swap(x, r=0, z=0, y=0, c=0):
        pairs = [(flat(spot), flat([a ^ b for a, b in zip(spot, (r, z, y, c))])) for spot in spots]
        return lax.ppermute(x, ("rep", "wide"), pairs)

    def array(rows, dtype=bf16):
        return jax.ShapeDtypeStruct((rows, width), dtype)

    def call(kernel, out_shape, name, *operands, specs=None, flops=2**20, **more):
        return pl.pallas_call(
            kernel,
            out_shape=out_shape,
            in_specs=specs or [WHOLE] * len(operands),
            out_specs=[WHOLE] * len(out_shape) if isinstance(out_shape, list) else WHOLE,
            compiler_params=params(16),
            cost_estimate=pl.CostEstimate(flops=flops, bytes_accessed=2**16, transcendentals=0),
            name=name,
            **more,
        )(*operands)

    hbm = pl.BlockSpec(memory_space=pltpu.HBM)
    half_rows = shard_rows // 2
    ext = half_rows + 16
    half, full, target, draft_rows = call(
        start_kernel,
        [
            array(ext),
            array(shard_rows + 16),
            jax.ShapeDtypeStruct((1, count), jnp.int32),
            jax.ShapeDtypeStruct(draft_hidden.shape, bf16),
        ],
        "start_rows",
        *(pltpu.with_memory_space_constraint(x, pltpu.HBM) for x in (row_target.reshape(1, count), shard, draft_hidden)),
        specs=[hbm] * 3,
        scratch_shapes=[pltpu.SemaphoreType.DMA((4,))],
    )
    za, zb = swap(half, z=1), swap(half, z=2)
    y0 = swap(full, y=1)
    other_prompt = swap(prompt_hidden, c=1)
    zab = call(join_kernel, array(2 * ext), "join_pieces", za, zb, y0, other_prompt, specs=[WHOLE, WHOLE, UNREAD, UNREAD])
    yab, xab = swap(zab, y=1), swap(zab, r=1)
    zc = swap(zb, z=1)
    yc, xc = swap(zc, y=1), swap(zc, r=1)
    xyab = swap(yab, r=1)
    yxc = swap(xc, y=1)

    order = [
        (half, half_rows), (y0, shard_rows), (zab, ext + half_rows), (yab, ext + half_rows),
        (zab, half_rows), (yab, half_rows), (zc, half_rows), (yc, half_rows),
    ]
    pack = call(
        functools.partial(pack_kernel, [(n, first) for n, (_, first) in enumerate(order)]),
        jax.ShapeDtypeStruct((16, draft_hidden.shape[2]), bf16), "pack_rows",
        target, draft_rows, *(x for x, _ in order), xab, xc,
        specs=[WHOLE] * (2 + len(order)) + [UNREAD] * 2,
    )
    other_pack = swap(pack, c=1)
    limit, column_slot, place, drafts = call(
        functools.partial(count_kernel, most_rows),
        [
            jax.ShapeDtypeStruct((2, 128), jnp.int32),
            jax.ShapeDtypeStruct((1, 2 * count), jnp.int32),
            jax.ShapeDtypeStruct((1, 2 * count), jnp.int32),
            jax.ShapeDtypeStruct(pack.shape, bf16),
        ],
        "count_rows", context_len, pack, other_pack,
        specs=[SCALARS, WHOLE, WHOLE],
    )

    def starts_of(uses):
        def starts():
            rep, wide = lax.axis_index("rep"), lax.axis_index("wide")
            z, y, c = wide // 4, wide // 2 % 2, wide % 2
            found = []
            for _, _, _, (x_step, z_step, y_step) in uses:
                owner_z = (z // 2 + z_step // 2) % 2 * 2 + (z + z_step) % 2
                owner = (owner_z * 2 + (y + y_step) % 2) * 2 + c
                found.append(owner * shard_rows + (0 if x_step is None else (rep + x_step) % 2 * half_rows))
            return found

        return starts

    rows = [prompt_hidden, other_prompt, drafts]
    stages = [
        ([full, y0], [(0, 0, shard_rows, (None, 0, 0)), (1, 0, shard_rows, (None, 0, 1))]),
        (
            [zab, yab],
            [(0, 0, half_rows, (0, 1, 0)), (0, ext, half_rows, (0, 2, 0)),
             (1, 0, half_rows, (0, 1, 1)), (1, ext, half_rows, (0, 2, 1))],
        ),
        (
            [xab, zc, yc],
            [(0, 0, half_rows, (1, 1, 0)), (0, ext, half_rows, (1, 2, 0)),
             (1, 0, half_rows, (0, 3, 0)), (2, 0, half_rows, (0, 3, 1))],
        ),
        (
            [xc, yxc, xyab],
            [(0, 0, half_rows, (1, 3, 0)), (1, 0, half_rows, (1, 3, 1)),
             (2, 0, half_rows, (1, 1, 1)), (2, ext, half_rows, (1, 2, 1))],
        ),
    ]
    sums = []
    total_rows = 2 * count + 16
    for n, (pieces, uses) in enumerate(stages[:-1]):
        sums = [
            call(
                functools.partial(down_kernel, starts_of(uses), [use[:3] for use in uses], n == 0),
                array(total_rows, f32), "down_rows", *rows, *pieces, *sums, flops=2**26,
            )
        ]

    def finish(tie):
        pieces, uses = stages[-1]
        keep, send = call(
            functools.partial(down_place_kernel, starts_of(uses), [use[:3] for use in uses]),
            [array(2 * count + 8, f32)] * 2, "down_place_rows", *rows, place, *sums, *pieces, tie,
            specs=[WHOLE] * (5 + len(pieces)) + [UNREAD], flops=2**26,
        )
        came = swap(send, c=1)
        block = array(count)
        draft_latent, stay, send = call(
            route_kernel, [array(8, f32), block, block], "route_rows", keep, came,
            scratch_shapes=[pltpu.VMEM((2 * count + 8, width), f32)],
        )
        came = swap(send, y=1)
        stay, send = call(functools.partial(mix_kernel, 2), [block, block], "mix_rows", stay, came)
        came = swap(send, z=2)
        stay, send = call(functools.partial(mix_kernel, 1), [block, block], "mix_rows", stay, came)
        return draft_latent, [stay, swap(send, z=1)]

    return limit, column_slot, finish


def deliver_plain(prompt_hidden, draft_hidden, shard, row_target, context_len):
    wide_size = lax.axis_size("wide")
    row_count = prompt_hidden.shape[0]
    slot_count, draft_count, _ = draft_hidden.shape
    latent_width = shard.shape[1]
    most_rows = 2 * ((row_count + wide_size - 1) // wide_size)
    arrived = wide_size * most_rows
    weight = lax.all_gather(shard, "wide", axis=0, tiled=True)
    index = jnp.arange(row_count, dtype=jnp.int32)
    same = (row_target[:, None] == row_target[None, :]) & (index[None, :] < index[:, None])
    rank = jnp.sum(same.astype(jnp.int32), 1)
    front = row_target % slot_count == 0
    place = row_target // slot_count * most_rows + jnp.where(front, rank, most_rows - 1 - rank)
    request = jnp.arange(wide_size * slot_count, dtype=jnp.int32)
    counts = jnp.sum((row_target[None, :] == request[:, None]).astype(jnp.int32), 1)
    counts = lax.all_to_all(counts.reshape(wide_size, slot_count), "wide", split_axis=0, concat_axis=0, tiled=True)
    limit = jnp.broadcast_to((context_len - jnp.sum(counts, 0))[:, None], (slot_count, 128))
    spot = jnp.arange(most_rows, dtype=jnp.int32)[None, :]
    column_slot = jnp.where(
        spot < counts[:, 0:1], 0, jnp.where(spot >= most_rows - counts[:, 1:2], 1, -1)
    ).reshape(1, arrived)

    tile = slot_count * draft_count
    draft_flat = jnp.pad(draft_hidden.reshape(tile, draft_hidden.shape[2]), ((0, 16 - tile), (0, 0)))

    def finish(tie):
        outgoing, draft_latent = pl.pallas_call(
            plain_down_kernel,
            out_shape=[
                jax.ShapeDtypeStruct((arrived, latent_width), jnp.bfloat16),
                jax.ShapeDtypeStruct((slot_count * draft_count, latent_width), jnp.float32),
            ],
            in_specs=[WHOLE] * 4,
            out_specs=[WHOLE] * 2,
            compiler_params=params(24),
            name="down_rows",
        )(place.reshape(1, row_count), prompt_hidden, draft_flat, weight)
        incoming = lax.all_to_all(
            outgoing.reshape(wide_size, most_rows, latent_width), "wide", split_axis=0, concat_axis=0, tiled=True
        )
        return draft_latent, [incoming.reshape(arrived, latent_width)]

    return limit, column_slot, finish


def local(
    prompt_hidden,
    resident_latent,
    row_target,
    row_offset,
    context_len,
    draft_hidden,
    draft_query_heads,
    down_weight,
    key_up_weight,
    value_up_weight,
):
    f32, bf16 = jnp.float32, jnp.bfloat16
    slot_count, span_rows, latent_width = resident_latent.shape
    draft_count = draft_hidden.shape[1]
    rows = QUERY_HEADS * draft_count
    known = lax.axis_size("wide") == 16 and lax.axis_size("rep") == 2
    limit, column_slot, finish = (deliver if known else deliver_plain)(
        prompt_hidden, draft_hidden, down_weight, row_target, context_len
    )
    hbm = pl.BlockSpec(memory_space=pltpu.HBM)
    turned, peak, total, mixed = pl.pallas_call(
        held_kernel,
        out_shape=[
            jax.ShapeDtypeStruct((slot_count, 2 * rows, latent_width), bf16),
            jax.ShapeDtypeStruct((slot_count, rows, 1), f32),
            jax.ShapeDtypeStruct((slot_count, rows, 1), f32),
            jax.ShapeDtypeStruct((slot_count, rows, latent_width), f32),
        ],
        in_specs=[WHOLE, hbm, hbm, hbm],
        out_specs=[WHOLE] * 4,
        scratch_shapes=[
            pltpu.VMEM(draft_query_heads.shape, bf16),
            pltpu.VMEM(key_up_weight.shape, bf16),
            pltpu.VMEM(resident_latent.shape, bf16),
            pltpu.VMEM((slot_count, rows, latent_width), f32),
            pltpu.VMEM((rows, span_rows), f32),
            pltpu.SemaphoreType.DMA((3,)),
        ],
        compiler_params=params(16),
        cost_estimate=pl.CostEstimate(flops=2**20, bytes_accessed=2**16, transcendentals=0),
        name="held_rows",
    )(limit, *(pltpu.with_memory_space_constraint(x, pltpu.HBM) for x in (draft_query_heads, key_up_weight, resident_latent)))

    draft_latent, incoming = finish(peak)
    arrived = column_slot.shape[1]
    span = (arrived + slot_count * draft_count + 127) // 128 * 128
    return pl.pallas_call(
        late_kernel,
        out_shape=jax.ShapeDtypeStruct((slot_count, draft_count, QUERY_HEADS * HEAD_SIZE), bf16),
        in_specs=[WHOLE] * (7 + len(incoming)),
        out_specs=WHOLE,
        scratch_shapes=[
            pltpu.VMEM((span, latent_width), bf16),
            pltpu.VMEM((slot_count, 2 * rows, latent_width), bf16),
        ],
        compiler_params=params(16),
        name="late_rows",
    )(column_slot, draft_latent, turned, peak, total, mixed, value_up_weight, *incoming)


def solution(mesh):
    placed = (
        P(("rep", "wide"), None),
        P(("rep", "wide"), None, None),
        P(("rep", "wide")),
        P(("rep", "wide")),
        P(("rep", "wide")),
        P(("rep", "wide"), None, None),
        P(("rep", "wide"), None, None),
        P("wide", None),
        P(),
        P(),
    )
    return jax.shard_map(
        local, mesh=mesh, in_specs=placed, out_specs=P(("rep", "wide"), None, None), check_vma=False
    )
```

```python
import functools
import math

import jax
import jax.numpy as jnp
from jax import lax
from jax.experimental import pallas as pl
from jax.experimental.pallas import tpu as pltpu
from jax.sharding import PartitionSpec as P

QUERY_HEADS = 64
HEAD_SIZE = 128
FAR = -1e30
NT = (((1,), (1,)), ((), ()))
WHOLE = pl.BlockSpec(memory_space=pltpu.VMEM)
SCALARS = pl.BlockSpec(memory_space=pltpu.SMEM)
UNREAD = pl.BlockSpec(memory_space=pl.ANY)


def params(mib):
    return pltpu.CompilerParams(vmem_limit_bytes=mib * 1024 * 1024)


def split_rows(x):
    top = x.astype(jnp.bfloat16)
    rest = (x - top.astype(jnp.float32)).astype(jnp.bfloat16)
    return jnp.concatenate([top, rest], 0)


def join_rows(x):
    half = x.shape[0] // 2
    return x[:half] + x[half:]


def held_kernel(
    arrived, context_ref, query_hbm, key_up_hbm, cache_hbm, turned_ref, peak_ref, total_ref, mixed_ref, window_ref,
    query_ref, key_up_ref, cache_ref, float_ref, scores_ref, sems,
):
    copies = [
        pltpu.make_async_copy(source, target, sems.at[n])
        for n, (source, target) in enumerate(
            [(query_hbm, query_ref), (key_up_hbm, key_up_ref), (cache_hbm, cache_ref)]
        )
    ]
    for copy in copies:
        copy.start()
    slot_count, span_rows, _ = cache_ref.shape
    draft_count = query_ref.shape[1]
    heads_kv = key_up_ref.shape[1] // HEAD_SIZE
    group_size = QUERY_HEADS // heads_kv
    rows = group_size * draft_count
    scale = math.log2(math.e) / math.sqrt(HEAD_SIZE)
    step = 256
    copies[0].wait()
    copies[1].wait()
    for k in range(heads_kv):
        pieces = []
        for b in range(slot_count):
            for g in range(group_size):
                lane = (k * group_size + g) * HEAD_SIZE
                pieces.append(query_ref[b, :, lane : lane + HEAD_SIZE].astype(jnp.float32))
        query = jnp.concatenate(pieces, 0).astype(jnp.bfloat16)
        key_up = key_up_ref[:, k * HEAD_SIZE : (k + 1) * HEAD_SIZE]
        turned = lax.dot_general(query, key_up, NT, preferred_element_type=jnp.float32) * scale
        for b in range(slot_count):
            float_ref[b, k * rows : (k + 1) * rows, :] = turned[b * rows : (b + 1) * rows]
    copies[2].wait()
    for b in range(slot_count):
        first = pl.multiple_of(window_start(context_ref[b], arrived, window_ref.shape[1], span_rows), 128)
        window_ref[b] = cache_ref[b, pl.ds(first, window_ref.shape[1]), :]
        turned_ref[b] = split_rows(float_ref[b])
        peak = None
        for c in range(0, span_rows, step):
            scores = join_rows(
                lax.dot_general(turned_ref[b], cache_ref[b, c : c + step], NT, preferred_element_type=jnp.float32)
            )
            column = lax.broadcasted_iota(jnp.int32, (1, step), 1) + c
            scores = jnp.where(column < context_ref[b] - arrived, scores, FAR)
            scores_ref[:, c : c + step] = scores
            top = jnp.max(scores, 1, keepdims=True)
            peak = top if peak is None else jnp.maximum(peak, top)
        peak_ref[b] = peak
        total = jnp.zeros_like(peak)
        mixed = jnp.zeros(mixed_ref.shape[1:], jnp.float32)
        for c in range(0, span_rows, step):
            weights = jnp.exp2(scores_ref[:, c : c + step] - peak)
            total += jnp.sum(weights, 1, keepdims=True)
            mixed += join_rows(
                jnp.dot(split_rows(weights), cache_ref[b, c : c + step], preferred_element_type=jnp.float32)
            )
        total_ref[b] = total
        mixed_ref[b] = mixed


def window_start(context, arrived, size, span_rows):
    return jnp.clip((context - arrived) // 128 * 128, 0, span_rows - size)


def window_kernel(
    arrived, span_rows, context_ref, limit_ref, turned_ref, peak_ref, total_ref, mixed_ref, window_ref,
    new_peak_ref, new_total_ref, new_mixed_ref,
):
    slot_count, size, _ = window_ref.shape
    for b in range(slot_count):
        first = window_start(context_ref[b], arrived, size, span_rows)
        scores = join_rows(
            lax.dot_general(turned_ref[b], window_ref[b], NT, preferred_element_type=jnp.float32)
        )
        column = lax.broadcasted_iota(jnp.int32, (1, size), 1) + first
        seen = (column >= context_ref[b] - arrived) & (column < limit_ref[b : b + 1, 0:1])
        scores = jnp.where(seen, scores, FAR)
        peak = jnp.maximum(jnp.max(scores, 1, keepdims=True), peak_ref[b])
        weights = jnp.exp2(scores - peak)
        fade = jnp.exp2(peak_ref[b] - peak)
        new_peak_ref[b] = peak
        new_total_ref[b] = total_ref[b] * fade + jnp.sum(weights, 1, keepdims=True)
        mixed = join_rows(jnp.dot(split_rows(weights), window_ref[b], preferred_element_type=jnp.float32))
        new_mixed_ref[b] = mixed_ref[b] * fade + mixed


def piece_sums(starts, spans, row_refs, refs):
    total = None
    for start, (n, first, depth) in zip(starts, spans):
        lanes = pl.ds(pl.multiple_of(start, HEAD_SIZE), depth)
        rows = [ref[:, lanes] for ref in row_refs]
        piece = refs[n][first : first + depth, :]
        product = jnp.dot(jnp.concatenate(rows, 0), piece, preferred_element_type=jnp.float32)
        total = product if total is None else total + product
    return total


def down_kernel(starts_of, spans, first, *refs):
    row_refs, refs, out_ref = refs[:2], refs[2:-1], refs[-1]
    total = piece_sums(starts_of(), spans, row_refs, refs)
    out_ref[...] = total if first else total + refs[-1][...]


def down_place_kernel(starts_of, spans, *refs):
    row_refs, refs, (keep_ref, send_ref) = refs[:2], refs[2:-2], refs[-2:]
    place_ref, sum_ref, refs = refs[0], refs[1], refs[2:]
    total = piece_sums(starts_of(), spans, row_refs, refs) + sum_ref[...]
    slots, width = keep_ref.shape[0] - 8, keep_ref.shape[1]
    count = place_ref.shape[1]
    mine, both = count // 2, row_refs[0].shape[0]
    parts = []
    left = jnp.concatenate([total[:mine], total[both : both + mine]], 0)
    for _ in range(3):
        part = left.astype(jnp.bfloat16)
        parts.append(part)
        left = left - part.astype(jnp.float32)
    parts = jnp.concatenate(parts, 1)
    core = lax.axis_index("wide") % 2
    spot = lax.broadcasted_iota(jnp.int32, (slots, count), 0)
    for ref, target, draft in ((keep_ref, core, mine), (send_ref, 1 - core, both + mine)):
        chosen = jnp.where(spot + target * slots == place_ref[...], 1.0, 0.0).astype(jnp.bfloat16)
        moved = jnp.dot(chosen, parts, preferred_element_type=jnp.float32)
        ref[:slots, :] = moved[:, :width] + moved[:, width : 2 * width] + moved[:, 2 * width :]
        ref[slots:, :] = total[draft : draft + 8]


def route_kernel(keep_ref, came_ref, draft_latent_ref, stay_ref, send_ref, float_ref):
    float_ref[...] = keep_ref[...] + came_ref[...]
    slots = float_ref.shape[0] - 8
    draft_latent_ref[...] = float_ref[slots:, :].astype(jnp.bfloat16).astype(jnp.float32)
    size = slots // 8
    wide = lax.axis_index("wide")
    z, y = wide // 4, wide // 2 % 2
    for other, ref in ((0, stay_ref), (1, send_ref)):
        for n, (high, low) in enumerate(((0, 0), (0, 1), (1, 0), (1, 1))):
            there = (z // 2 + high) % 2 * 2 + (z + low) % 2
            block = there * 2 + (y + other) % 2
            rows = pl.ds(pl.multiple_of(block * size, size), size)
            ref[n * size : (n + 1) * size, :] = float_ref[rows, :].astype(jnp.bfloat16)


def mix_kernel(outer, keep_ref, came_ref, stay_ref, send_ref):
    half = keep_ref.shape[0] // 2
    size = half // outer
    for ref, first in ((stay_ref, 0), (send_ref, half)):
        for n in range(outer):
            for m, source in enumerate((keep_ref, came_ref)):
                spot = (n * 2 + m) * size
                ref[spot : spot + size, :] = source[first + n * size : first + (n + 1) * size, :]


def start_kernel(
    target_hbm, shard_hbm, prompt_hbm, draft_hbm, half_ref, full_ref, target_ref, rows_ref, draft_ref, sems
):
    half_rows, shard_rows = half_ref.shape[0] - 16, full_ref.shape[0] - 16
    mine = pl.ds(pl.multiple_of(lax.axis_index("rep") * half_rows, half_rows), half_rows)
    copies = [
        pltpu.make_async_copy(target_hbm, target_ref, sems.at[0]),
        pltpu.make_async_copy(shard_hbm.at[mine], half_ref.at[:half_rows], sems.at[1]),
        pltpu.make_async_copy(shard_hbm, full_ref.at[:shard_rows], sems.at[2]),
        pltpu.make_async_copy(draft_hbm, draft_ref, sems.at[3]),
        pltpu.make_async_copy(prompt_hbm, rows_ref.at[: prompt_hbm.shape[0]], sems.at[4]),
    ]
    for copy in copies:
        copy.start()
    width, count = half_ref.shape[1], target_ref.shape[1]
    copies[0].wait()
    hit = lax.broadcasted_iota(jnp.int32, (width, count), 0) == target_ref[...]
    hit = jnp.where(hit, 1.0, 0.0).astype(jnp.bfloat16)
    block = lax.dot_general(jnp.ones((16, count), jnp.bfloat16), hit, NT, preferred_element_type=jnp.float32)
    half_ref[half_rows:, :] = block.astype(jnp.bfloat16)
    full_ref[shard_rows:, :] = block.astype(jnp.bfloat16)
    copies[3].wait()
    rows = [draft_ref[b].astype(jnp.float32) for b in range(draft_ref.shape[0])]
    rows.append(jnp.zeros((8, rows_ref.shape[1]), jnp.float32))
    rows_ref[count:, :] = jnp.concatenate(rows, 0).astype(jnp.bfloat16)
    for n in (1, 2, 4):
        copies[n].wait()


def join_kernel(one_ref, two_ref, *refs):
    rows, out_ref = one_ref.shape[0], refs[-1]
    out_ref[:rows, :] = one_ref[...]
    out_ref[rows:, :] = two_ref[...]


def copy_kernel(one_ref, tie_ref, out_ref):
    out_ref[...] = one_ref[...]


def pack_kernel(spans, target_ref, *refs):
    out_ref, width = refs[-1], refs[0].shape[1]
    for m, (n, first) in enumerate(spans):
        out_ref[:, m * width : (m + 1) * width] = refs[n][first : first + 16, :]
    target = jnp.broadcast_to(target_ref[...].astype(jnp.float32), (16, target_ref.shape[1]))
    out_ref[:, len(spans) * width :] = target.astype(jnp.bfloat16)


def count_kernel(most_rows, context_ref, mine_ref, other_ref, limit_ref, column_slot_ref, place_ref):
    f32, bf16 = jnp.float32, jnp.bfloat16
    count, width = place_ref.shape[1] // 2, 256
    wide = lax.axis_index("wide")
    core = wide % 2
    mine, other = mine_ref[...].astype(f32), other_ref[...].astype(f32)
    low = jnp.where(core == 0, mine[:1], other[:1])
    high = jnp.where(core == 0, other[:1], mine[:1])
    counts = []
    for n in range(8):
        counts += [low[:, n * width : (n + 1) * width], high[:, n * width : (n + 1) * width]]
    counts = jnp.concatenate(counts, 0)
    lane = lax.broadcasted_iota(jnp.int32, counts.shape, 1)
    row = lax.broadcasted_iota(jnp.int32, counts.shape, 0)
    spread = []
    for b in range(2):
        number = jnp.sum(jnp.where(lane == wide * 2 + b, counts, 0.0), 1, keepdims=True)
        limit = context_ref[b] - jnp.sum(number, 0, keepdims=True).astype(jnp.int32)
        limit_ref[b : b + 1, :] = jnp.broadcast_to(limit, (1, limit_ref.shape[1]))
        spread.append(jnp.sum(jnp.where(lane // most_rows == row, number, 0.0), 0, keepdims=True).astype(jnp.int32))
    spot = lax.broadcasted_iota(jnp.int32, column_slot_ref.shape, 1) % most_rows
    column_slot_ref[...] = jnp.where(spot < spread[0], 0, jnp.where(spot >= most_rows - spread[1], 1, -1))
    earlier = lax.broadcasted_iota(jnp.int32, (count, count), 0) < lax.broadcasted_iota(jnp.int32, (count, count), 1)
    earlier = jnp.where(earlier, 1.0, 0.0).astype(bf16)
    for n, (rows, owner) in enumerate(((mine, core), (other, 1 - core))):
        target = rows[:1, 8 * width : 8 * width + count].astype(jnp.int32)
        hit = jnp.where(lax.broadcasted_iota(jnp.int32, (64, count), 0) == target, 1.0, 0.0)
        before = jnp.dot(hit.astype(bf16), earlier, preferred_element_type=f32)
        rank = jnp.sum(hit * before, 0, keepdims=True).astype(jnp.int32)
        spot = jnp.where(target % 2 == 0, rank, most_rows - 1 - rank)
        chip, side = target // 4, target // 2 % 2
        place_ref[:, n * count : (n + 1) * count] = side * 2 * count + (chip * 2 + owner) * most_rows + spot


def plain_down_kernel(place_ref, prompt_ref, draft_ref, weight_ref, outgoing_ref, draft_latent_ref):
    count = prompt_ref.shape[0]
    rows = jnp.concatenate([prompt_ref[...], draft_ref[...]], 0)
    total = jnp.dot(rows, weight_ref[...], preferred_element_type=jnp.float32)
    draft_latent_ref[...] = total[count : count + 8].astype(jnp.bfloat16).astype(jnp.float32)
    spot = lax.broadcasted_iota(jnp.int32, (outgoing_ref.shape[0], count), 0)
    chosen = jnp.where(spot == place_ref[...], 1.0, 0.0).astype(jnp.bfloat16)
    latent = total[:count].astype(jnp.bfloat16)
    outgoing_ref[...] = jnp.dot(chosen, latent, preferred_element_type=jnp.float32).astype(jnp.bfloat16)


def late_kernel(
    column_slot_ref, draft_latent_ref, turned_ref, peak_ref, total_ref, mixed_ref, value_up_ref, *refs
):
    incoming_refs, (out_ref, rows_ref, parted_ref) = refs[:-3], refs[-3:]
    slot_count, draft_count, _ = out_ref.shape
    tile = slot_count * draft_count
    heads_kv = value_up_ref.shape[1] // HEAD_SIZE
    group_size = QUERY_HEADS // heads_kv
    head_rows = group_size * draft_count
    rows = peak_ref.shape[1]
    block = incoming_refs[0].shape[0]
    arrived = block * len(incoming_refs)
    span = rows_ref.shape[0]
    drafts = jnp.concatenate([draft_latent_ref[...], jnp.zeros((span - arrived - tile, rows_ref.shape[1]), jnp.float32)], 0)
    for n, ref in enumerate(incoming_refs):
        rows_ref[n * block : (n + 1) * block, :] = ref[...]
    rows_ref[arrived:, :] = drafts.astype(jnp.bfloat16)
    token = lax.broadcasted_iota(jnp.int32, (rows, 1), 0) % draft_count
    column = lax.broadcasted_iota(jnp.int32, (rows, span - arrived), 1)
    for b in range(slot_count):
        scores = join_rows(lax.dot_general(turned_ref[b], rows_ref[...], NT, preferred_element_type=jnp.float32))
        draft_seen = (column >= b * draft_count) & (column <= b * draft_count + token)
        scores = jnp.concatenate(
            [
                jnp.where(column_slot_ref[...] == b, scores[:, :arrived], FAR),
                jnp.where(draft_seen, scores[:, arrived:], FAR),
            ],
            1,
        )
        peak = jnp.maximum(jnp.max(scores, 1, keepdims=True), peak_ref[b])
        weights = jnp.exp2(scores - peak)
        fade = jnp.exp2(peak_ref[b] - peak)
        total = total_ref[b] * fade + jnp.sum(weights, 1, keepdims=True)
        mixed = join_rows(jnp.dot(split_rows(weights), rows_ref[...], preferred_element_type=jnp.float32))
        parted_ref[b] = split_rows((mixed_ref[b] * fade + mixed) / total)
    for k in range(heads_kv):
        part = []
        for b in range(slot_count):
            part.append(parted_ref[b, k * head_rows : (k + 1) * head_rows, :])
            part.append(parted_ref[b, rows + k * head_rows : rows + (k + 1) * head_rows, :])
        value_up = value_up_ref[:, k * HEAD_SIZE : (k + 1) * HEAD_SIZE]
        both = jnp.dot(jnp.concatenate(part, 0), value_up, preferred_element_type=jnp.float32)
        for b in range(slot_count):
            result = join_rows(both[b * 2 * head_rows : (b + 1) * 2 * head_rows])
            wide = jnp.concatenate(
                [result[g * draft_count : (g + 1) * draft_count] for g in range(group_size)], 1
            )
            out_ref[b, :, k * group_size * HEAD_SIZE : (k + 1) * group_size * HEAD_SIZE] = wide.astype(jnp.bfloat16)


def deliver(prompt_hidden, draft_hidden, shard, row_target, context_len, held):
    shard_rows, width = shard.shape
    count = prompt_hidden.shape[0]
    spots = [(r, z, y, c) for r in range(2) for z in range(4) for y in range(2) for c in range(2)]
    most_rows = count // 8
    f32, bf16 = jnp.float32, jnp.bfloat16

    def flat(spot):
        return ((spot[0] * 4 + spot[1]) * 2 + spot[2]) * 2 + spot[3]

    def swap(x, r=0, z=0, y=0, c=0):
        pairs = [(flat(spot), flat([a ^ b for a, b in zip(spot, (r, z, y, c))])) for spot in spots]
        return lax.ppermute(x, ("rep", "wide"), pairs)

    def array(rows, dtype=bf16):
        return jax.ShapeDtypeStruct((rows, width), dtype)

    def call(kernel, out_shape, name, *operands, specs=None, flops=2**20, **more):
        return pl.pallas_call(
            kernel,
            out_shape=out_shape,
            in_specs=specs or [WHOLE] * len(operands),
            out_specs=[WHOLE] * len(out_shape) if isinstance(out_shape, list) else WHOLE,
            compiler_params=params(16),
            cost_estimate=pl.CostEstimate(flops=flops, bytes_accessed=2**16, transcendentals=0),
            name=name,
            **more,
        )(*operands)

    hbm = pl.BlockSpec(memory_space=pltpu.HBM)
    half_rows = shard_rows // 2
    ext = half_rows + 16
    padded = (count + 16, prompt_hidden.shape[1])
    half, full, target, rows = call(
        start_kernel,
        [
            array(ext),
            array(shard_rows + 16),
            jax.ShapeDtypeStruct((1, count), jnp.int32),
            jax.ShapeDtypeStruct(padded, bf16),
        ],
        "start_rows",
        *(
            pltpu.with_memory_space_constraint(x, pltpu.HBM)
            for x in (row_target.reshape(1, count), shard, prompt_hidden, draft_hidden)
        ),
        specs=[hbm] * 4,
        scratch_shapes=[pltpu.VMEM(draft_hidden.shape, bf16), pltpu.SemaphoreType.DMA((5,))],
    )
    za, zb = swap(half, z=1), swap(half, z=2)
    y0 = swap(full, y=1)
    rows = [rows, swap(rows, c=1)]
    zab = call(
        join_kernel, array(2 * ext), "join_pieces", za, zb, y0, rows[1], held, specs=[WHOLE] * 2 + [UNREAD] * 3
    )
    yab, xab = swap(zab, y=1), swap(zab, r=1)
    zc = swap(zb, z=1)
    xc = swap(zc, r=1)
    xyab = swap(yab, r=1)
    yc = swap(call(copy_kernel, array(ext), "copy_piece", zc, yab, specs=[WHOLE, UNREAD]), y=1)
    yxc = swap(xc, y=1)

    order = [
        (half, half_rows), (y0, shard_rows), (zab, ext + half_rows), (yab, ext + half_rows),
        (zab, half_rows), (yab, half_rows), (zc, half_rows), (yc, half_rows),
    ]
    pack = call(
        functools.partial(pack_kernel, [(n, first) for n, (_, first) in enumerate(order)]),
        jax.ShapeDtypeStruct((16, len(order) * width + count), bf16), "pack_rows",
        target, *(x for x, _ in order), xab, xc,
        specs=[WHOLE] * (1 + len(order)) + [UNREAD] * 2,
    )
    other_pack = swap(pack, c=1)
    limit, column_slot, place = call(
        functools.partial(count_kernel, most_rows),
        [
            jax.ShapeDtypeStruct((2, 128), jnp.int32),
            jax.ShapeDtypeStruct((1, 2 * count), jnp.int32),
            jax.ShapeDtypeStruct((1, 2 * count), jnp.int32),
        ],
        "count_rows", context_len, pack, other_pack,
        specs=[SCALARS, WHOLE, WHOLE],
    )

    def starts_of(uses):
        def starts():
            rep, wide = lax.axis_index("rep"), lax.axis_index("wide")
            z, y, c = wide // 4, wide // 2 % 2, wide % 2
            found = []
            for _, _, _, (x_step, z_step, y_step) in uses:
                owner_z = (z // 2 + z_step // 2) % 2 * 2 + (z + z_step) % 2
                owner = (owner_z * 2 + (y + y_step) % 2) * 2 + c
                found.append(owner * shard_rows + (0 if x_step is None else (rep + x_step) % 2 * half_rows))
            return found

        return starts

    stages = [
        ([full, y0], [(0, 0, shard_rows, (None, 0, 0)), (1, 0, shard_rows, (None, 0, 1))]),
        (
            [zab, yab],
            [(0, 0, half_rows, (0, 1, 0)), (0, ext, half_rows, (0, 2, 0)),
             (1, 0, half_rows, (0, 1, 1)), (1, ext, half_rows, (0, 2, 1))],
        ),
        (
            [xab, zc, yc],
            [(0, 0, half_rows, (1, 1, 0)), (0, ext, half_rows, (1, 2, 0)),
             (1, 0, half_rows, (0, 3, 0)), (2, 0, half_rows, (0, 3, 1))],
        ),
        (
            [xc, yxc, xyab],
            [(0, 0, half_rows, (1, 3, 0)), (1, 0, half_rows, (1, 3, 1)),
             (2, 0, half_rows, (1, 1, 1)), (2, ext, half_rows, (1, 2, 1))],
        ),
    ]
    sums = []
    total_rows = 2 * padded[0]
    for n, (pieces, uses) in enumerate(stages[:-1]):
        sums = [
            call(
                functools.partial(down_kernel, starts_of(uses), [use[:3] for use in uses], n == 0),
                array(total_rows, f32), "down_rows", *rows, *pieces, *sums, flops=2**26,
            )
        ]

    def finish(tie):
        pieces, uses = stages[-1]
        keep, send = call(
            functools.partial(down_place_kernel, starts_of(uses), [use[:3] for use in uses]),
            [array(2 * count + 8, f32)] * 2, "down_place_rows", *rows, place, *sums, *pieces, tie,
            specs=[WHOLE] * (4 + len(pieces)) + [UNREAD], flops=2**26,
        )
        came = swap(send, c=1)
        block = array(count)
        draft_latent, stay, send = call(
            route_kernel, [array(8, f32), block, block], "route_rows", keep, came,
            scratch_shapes=[pltpu.VMEM((2 * count + 8, width), f32)],
        )
        came = swap(send, y=1)
        stay, send = call(functools.partial(mix_kernel, 2), [block, block], "mix_rows", stay, came)
        came = swap(send, z=2)
        stay, send = call(functools.partial(mix_kernel, 1), [block, block], "mix_rows", stay, came)
        return draft_latent, [stay, swap(send, z=1)]

    return limit, column_slot, finish


def deliver_plain(prompt_hidden, draft_hidden, shard, row_target, context_len, held):
    wide_size = lax.axis_size("wide")
    row_count = prompt_hidden.shape[0]
    slot_count, draft_count, _ = draft_hidden.shape
    latent_width = shard.shape[1]
    most_rows = 2 * ((row_count + wide_size - 1) // wide_size)
    arrived = wide_size * most_rows
    weight = lax.all_gather(shard, "wide", axis=0, tiled=True)
    index = jnp.arange(row_count, dtype=jnp.int32)
    same = (row_target[:, None] == row_target[None, :]) & (index[None, :] < index[:, None])
    rank = jnp.sum(same.astype(jnp.int32), 1)
    front = row_target % slot_count == 0
    place = row_target // slot_count * most_rows + jnp.where(front, rank, most_rows - 1 - rank)
    request = jnp.arange(wide_size * slot_count, dtype=jnp.int32)
    counts = jnp.sum((row_target[None, :] == request[:, None]).astype(jnp.int32), 1)
    counts = lax.all_to_all(counts.reshape(wide_size, slot_count), "wide", split_axis=0, concat_axis=0, tiled=True)
    limit = jnp.broadcast_to((context_len - jnp.sum(counts, 0))[:, None], (slot_count, 128))
    spot = jnp.arange(most_rows, dtype=jnp.int32)[None, :]
    column_slot = jnp.where(
        spot < counts[:, 0:1], 0, jnp.where(spot >= most_rows - counts[:, 1:2], 1, -1)
    ).reshape(1, arrived)

    tile = slot_count * draft_count
    draft_flat = jnp.pad(draft_hidden.reshape(tile, draft_hidden.shape[2]), ((0, 16 - tile), (0, 0)))

    def finish(tie):
        outgoing, draft_latent = pl.pallas_call(
            plain_down_kernel,
            out_shape=[
                jax.ShapeDtypeStruct((arrived, latent_width), jnp.bfloat16),
                jax.ShapeDtypeStruct((slot_count * draft_count, latent_width), jnp.float32),
            ],
            in_specs=[WHOLE] * 4,
            out_specs=[WHOLE] * 2,
            compiler_params=params(24),
            name="down_rows",
        )(place.reshape(1, row_count), prompt_hidden, draft_flat, weight)
        incoming = lax.all_to_all(
            outgoing.reshape(wide_size, most_rows, latent_width), "wide", split_axis=0, concat_axis=0, tiled=True
        )
        return draft_latent, [incoming.reshape(arrived, latent_width)]

    return limit, column_slot, finish


def local(
    prompt_hidden,
    resident_latent,
    row_target,
    row_offset,
    context_len,
    draft_hidden,
    draft_query_heads,
    down_weight,
    key_up_weight,
    value_up_weight,
):
    f32, bf16 = jnp.float32, jnp.bfloat16
    slot_count, span_rows, latent_width = resident_latent.shape
    draft_count = draft_hidden.shape[1]
    rows = QUERY_HEADS * draft_count
    wide_size, row_count = lax.axis_size("wide"), prompt_hidden.shape[0]
    arrived = 2 * ((row_count + wide_size - 1) // wide_size) * wide_size
    window = min(arrived + 128, span_rows)
    hbm = pl.BlockSpec(memory_space=pltpu.HBM)
    stats = [
        jax.ShapeDtypeStruct((slot_count, rows, 1), f32),
        jax.ShapeDtypeStruct((slot_count, rows, 1), f32),
        jax.ShapeDtypeStruct((slot_count, rows, latent_width), f32),
    ]
    turned, peak, total, mixed, edge = pl.pallas_call(
        functools.partial(held_kernel, arrived),
        out_shape=[
            jax.ShapeDtypeStruct((slot_count, 2 * rows, latent_width), bf16),
            *stats,
            jax.ShapeDtypeStruct((slot_count, window, latent_width), bf16),
        ],
        in_specs=[SCALARS, hbm, hbm, hbm],
        out_specs=[WHOLE] * 5,
        scratch_shapes=[
            pltpu.VMEM(draft_query_heads.shape, bf16),
            pltpu.VMEM(key_up_weight.shape, bf16),
            pltpu.VMEM(resident_latent.shape, bf16),
            pltpu.VMEM((slot_count, rows, latent_width), f32),
            pltpu.VMEM((rows, span_rows), f32),
            pltpu.SemaphoreType.DMA((3,)),
        ],
        compiler_params=params(16),
        cost_estimate=pl.CostEstimate(flops=2**31, bytes_accessed=2**21, transcendentals=0),
        name="held_rows",
    )(context_len, *(pltpu.with_memory_space_constraint(x, pltpu.HBM) for x in (draft_query_heads, key_up_weight, resident_latent)))
    known = wide_size == 16 and lax.axis_size("rep") == 2
    limit, column_slot, finish = (deliver if known else deliver_plain)(
        prompt_hidden, draft_hidden, down_weight, row_target, context_len, peak
    )
    peak, total, mixed = pl.pallas_call(
        functools.partial(window_kernel, arrived, span_rows),
        out_shape=stats,
        in_specs=[SCALARS] + [WHOLE] * 6,
        out_specs=[WHOLE] * 3,
        compiler_params=params(16),
        cost_estimate=pl.CostEstimate(flops=2**20, bytes_accessed=2**16, transcendentals=0),
        name="window_rows",
    )(context_len, limit, turned, peak, total, mixed, edge)

    draft_latent, incoming = finish(peak)
    span = (arrived + slot_count * draft_count + 127) // 128 * 128
    return pl.pallas_call(
        late_kernel,
        out_shape=jax.ShapeDtypeStruct((slot_count, draft_count, QUERY_HEADS * HEAD_SIZE), bf16),
        in_specs=[WHOLE] * (7 + len(incoming)),
        out_specs=WHOLE,
        scratch_shapes=[
            pltpu.VMEM((span, latent_width), bf16),
            pltpu.VMEM((slot_count, 2 * rows, latent_width), bf16),
        ],
        compiler_params=params(16),
        name="late_rows",
    )(column_slot, draft_latent, turned, peak, total, mixed, value_up_weight, *incoming)


def solution(mesh):
    placed = (
        P(("rep", "wide"), None),
        P(("rep", "wide"), None, None),
        P(("rep", "wide")),
        P(("rep", "wide")),
        P(("rep", "wide")),
        P(("rep", "wide"), None, None),
        P(("rep", "wide"), None, None),
        P("wide", None),
        P(),
        P(),
    )
    return jax.shard_map(
        local, mesh=mesh, in_specs=placed, out_specs=P(("rep", "wide"), None, None), check_vma=False
    )
```

```python
import functools
import math

import jax
import jax.numpy as jnp
from jax import lax
from jax.experimental import pallas as pl
from jax.experimental.pallas import tpu as pltpu
from jax.sharding import PartitionSpec as P

QUERY_HEADS = 64
HEAD_SIZE = 128
FAR = -1e30
NT = (((1,), (1,)), ((), ()))
WHOLE = pl.BlockSpec(memory_space=pltpu.VMEM)
SCALARS = pl.BlockSpec(memory_space=pltpu.SMEM)
UNREAD = pl.BlockSpec(memory_space=pl.ANY)


def params(mib):
    return pltpu.CompilerParams(vmem_limit_bytes=mib * 1024 * 1024)


def split_rows(x):
    top = x.astype(jnp.bfloat16)
    rest = (x - top.astype(jnp.float32)).astype(jnp.bfloat16)
    return jnp.concatenate([top, rest], 0)


def join_rows(x):
    half = x.shape[0] // 2
    return x[:half] + x[half:]


def held_kernel(
    arrived, context_ref, query_hbm, key_up_hbm, cache_hbm, turned_ref, peak_ref, total_ref, mixed_ref, window_ref,
    query_ref, key_up_ref, cache_ref, float_ref, scores_ref, sems,
):
    copies = [
        pltpu.make_async_copy(source, target, sems.at[n])
        for n, (source, target) in enumerate(
            [(query_hbm, query_ref), (key_up_hbm, key_up_ref), (cache_hbm, cache_ref)]
        )
    ]
    for copy in copies:
        copy.start()
    slot_count, span_rows, _ = cache_ref.shape
    draft_count = query_ref.shape[1]
    heads_kv = key_up_ref.shape[1] // HEAD_SIZE
    group_size = QUERY_HEADS // heads_kv
    rows = group_size * draft_count
    scale = math.log2(math.e) / math.sqrt(HEAD_SIZE)
    step = 256
    copies[0].wait()
    copies[1].wait()
    for k in range(heads_kv):
        pieces = []
        for b in range(slot_count):
            for g in range(group_size):
                lane = (k * group_size + g) * HEAD_SIZE
                pieces.append(query_ref[b, :, lane : lane + HEAD_SIZE].astype(jnp.float32))
        query = jnp.concatenate(pieces, 0).astype(jnp.bfloat16)
        key_up = key_up_ref[:, k * HEAD_SIZE : (k + 1) * HEAD_SIZE]
        turned = lax.dot_general(query, key_up, NT, preferred_element_type=jnp.float32) * scale
        for b in range(slot_count):
            float_ref[b, k * rows : (k + 1) * rows, :] = turned[b * rows : (b + 1) * rows]
    copies[2].wait()
    for b in range(slot_count):
        first = pl.multiple_of(window_start(context_ref[b], arrived, window_ref.shape[1], span_rows), 128)
        window_ref[b] = cache_ref[b, pl.ds(first, window_ref.shape[1]), :]
        turned_ref[b] = split_rows(float_ref[b])
        peak = None
        for c in range(0, span_rows, step):
            scores = join_rows(
                lax.dot_general(turned_ref[b], cache_ref[b, c : c + step], NT, preferred_element_type=jnp.float32)
            )
            column = lax.broadcasted_iota(jnp.int32, (1, step), 1) + c
            scores = jnp.where(column < context_ref[b] - arrived, scores, FAR)
            scores_ref[:, c : c + step] = scores
            top = jnp.max(scores, 1, keepdims=True)
            peak = top if peak is None else jnp.maximum(peak, top)
        peak_ref[b] = peak
        total = jnp.zeros_like(peak)
        mixed = jnp.zeros(mixed_ref.shape[1:], jnp.float32)
        for c in range(0, span_rows, step):
            weights = jnp.exp2(scores_ref[:, c : c + step] - peak)
            total += jnp.sum(weights, 1, keepdims=True)
            mixed += join_rows(
                jnp.dot(split_rows(weights), cache_ref[b, c : c + step], preferred_element_type=jnp.float32)
            )
        total_ref[b] = total
        mixed_ref[b] = mixed


def window_start(context, arrived, size, span_rows):
    return jnp.clip((context - arrived) // 128 * 128, 0, span_rows - size)


def window_kernel(
    arrived, span_rows, draft_count, context_ref, limit_ref, turned_ref, peak_ref, total_ref, mixed_ref, window_ref,
    draft_latent_ref, new_peak_ref, new_total_ref, new_mixed_ref,
):
    slot_count, size, width = window_ref.shape
    rows = peak_ref.shape[1]
    drafts = draft_latent_ref[...]
    drafts = jnp.concatenate([drafts, jnp.zeros((128 - drafts.shape[0], width), jnp.float32)], 0).astype(jnp.bfloat16)
    token = lax.broadcasted_iota(jnp.int32, (rows, 1), 0) % draft_count
    spot = lax.broadcasted_iota(jnp.int32, (rows, 128), 1)
    for b in range(slot_count):
        first = window_start(context_ref[b], arrived, size, span_rows)
        scores = join_rows(lax.dot_general(turned_ref[b], window_ref[b], NT, preferred_element_type=jnp.float32))
        column = lax.broadcasted_iota(jnp.int32, (1, size), 1) + first
        seen = (column >= context_ref[b] - arrived) & (column < limit_ref[b : b + 1, 0:1])
        scores = jnp.where(seen, scores, FAR)
        draft_scores = join_rows(lax.dot_general(turned_ref[b], drafts, NT, preferred_element_type=jnp.float32))
        draft_seen = (spot >= b * draft_count) & (spot <= b * draft_count + token)
        draft_scores = jnp.where(draft_seen, draft_scores, FAR)
        peak = jnp.maximum(jnp.max(scores, 1, keepdims=True), jnp.max(draft_scores, 1, keepdims=True))
        peak = jnp.maximum(peak, peak_ref[b])
        weights, draft_weights = jnp.exp2(scores - peak), jnp.exp2(draft_scores - peak)
        fade = jnp.exp2(peak_ref[b] - peak)
        new_peak_ref[b] = peak
        total = jnp.sum(weights, 1, keepdims=True) + jnp.sum(draft_weights, 1, keepdims=True)
        new_total_ref[b] = total_ref[b] * fade + total
        mixed = jnp.dot(split_rows(weights), window_ref[b], preferred_element_type=jnp.float32)
        mixed += jnp.dot(split_rows(draft_weights), drafts, preferred_element_type=jnp.float32)
        new_mixed_ref[b] = mixed_ref[b] * fade + join_rows(mixed)


def piece_sums(starts, spans, row_refs, refs):
    total = None
    for start, (n, first, depth) in zip(starts, spans):
        lanes = pl.ds(pl.multiple_of(start, HEAD_SIZE), depth)
        rows = [ref[:, lanes] for ref in row_refs]
        piece = refs[n][first : first + depth, :]
        product = jnp.dot(jnp.concatenate(rows, 0), piece, preferred_element_type=jnp.float32)
        total = product if total is None else total + product
    return total


def down_kernel(starts_of, spans, first, *refs):
    row_refs, refs, out_ref = refs[:2], refs[2:-1], refs[-1]
    total = piece_sums(starts_of(), spans, row_refs, refs)
    out_ref[...] = total if first else total + refs[-1][...]


def down_place_kernel(starts_of, spans, *refs):
    row_refs, refs, (keep_ref, send_ref) = refs[:2], refs[2:-2], refs[-2:]
    place_ref, sum_ref, refs = refs[0], refs[1], refs[2:]
    total = piece_sums(starts_of(), spans, row_refs, refs) + sum_ref[...]
    slots, width = keep_ref.shape[0] - 8, keep_ref.shape[1]
    count = place_ref.shape[1]
    mine, both = count // 2, row_refs[0].shape[0]
    parts = []
    left = jnp.concatenate([total[:mine], total[both : both + mine]], 0)
    for _ in range(3):
        part = left.astype(jnp.bfloat16)
        parts.append(part)
        left = left - part.astype(jnp.float32)
    parts = jnp.concatenate(parts, 1)
    core = lax.axis_index("wide") % 2
    spot = lax.broadcasted_iota(jnp.int32, (slots, count), 0)
    for ref, target, draft in ((keep_ref, core, mine), (send_ref, 1 - core, both + mine)):
        chosen = jnp.where(spot + target * slots == place_ref[...], 1.0, 0.0).astype(jnp.bfloat16)
        moved = jnp.dot(chosen, parts, preferred_element_type=jnp.float32)
        ref[:slots, :] = moved[:, :width] + moved[:, width : 2 * width] + moved[:, 2 * width :]
        ref[slots:, :] = total[draft : draft + 8]


def route_kernel(keep_ref, came_ref, draft_latent_ref, stay_ref, send_ref, float_ref):
    float_ref[...] = keep_ref[...] + came_ref[...]
    slots = float_ref.shape[0] - 8
    draft_latent_ref[...] = float_ref[slots:, :].astype(jnp.bfloat16).astype(jnp.float32)
    size = slots // 8
    wide = lax.axis_index("wide")
    z, y = wide // 4, wide // 2 % 2
    for other, ref in ((0, stay_ref), (1, send_ref)):
        for n, (high, low) in enumerate(((0, 0), (0, 1), (1, 0), (1, 1))):
            there = (z // 2 + high) % 2 * 2 + (z + low) % 2
            block = there * 2 + (y + other) % 2
            rows = pl.ds(pl.multiple_of(block * size, size), size)
            ref[n * size : (n + 1) * size, :] = float_ref[rows, :].astype(jnp.bfloat16)


def mix_kernel(outer, keep_ref, came_ref, stay_ref, send_ref):
    half = keep_ref.shape[0] // 2
    size = half // outer
    for ref, first in ((stay_ref, 0), (send_ref, half)):
        for n in range(outer):
            for m, source in enumerate((keep_ref, came_ref)):
                spot = (n * 2 + m) * size
                ref[spot : spot + size, :] = source[first + n * size : first + (n + 1) * size, :]


def start_kernel(
    target_hbm, shard_hbm, prompt_hbm, draft_hbm, half_ref, full_ref, target_ref, rows_ref, draft_ref, sems
):
    half_rows, shard_rows = half_ref.shape[0] - 16, full_ref.shape[0] - 16
    mine = pl.ds(pl.multiple_of(lax.axis_index("rep") * half_rows, half_rows), half_rows)
    copies = [
        pltpu.make_async_copy(target_hbm, target_ref, sems.at[0]),
        pltpu.make_async_copy(shard_hbm.at[mine], half_ref.at[:half_rows], sems.at[1]),
        pltpu.make_async_copy(shard_hbm, full_ref.at[:shard_rows], sems.at[2]),
        pltpu.make_async_copy(draft_hbm, draft_ref, sems.at[3]),
        pltpu.make_async_copy(prompt_hbm, rows_ref.at[: prompt_hbm.shape[0]], sems.at[4]),
    ]
    for copy in copies:
        copy.start()
    width, count = half_ref.shape[1], target_ref.shape[1]
    copies[0].wait()
    hit = lax.broadcasted_iota(jnp.int32, (width, count), 0) == target_ref[...]
    hit = jnp.where(hit, 1.0, 0.0).astype(jnp.bfloat16)
    block = lax.dot_general(jnp.ones((16, count), jnp.bfloat16), hit, NT, preferred_element_type=jnp.float32)
    half_ref[half_rows:, :] = block.astype(jnp.bfloat16)
    full_ref[shard_rows:, :] = block.astype(jnp.bfloat16)
    copies[3].wait()
    rows = [draft_ref[b].astype(jnp.float32) for b in range(draft_ref.shape[0])]
    rows.append(jnp.zeros((8, rows_ref.shape[1]), jnp.float32))
    rows_ref[count:, :] = jnp.concatenate(rows, 0).astype(jnp.bfloat16)
    for n in (1, 2, 4):
        copies[n].wait()


def join_kernel(one_ref, two_ref, *refs):
    rows, (out_ref, bare_ref) = one_ref.shape[0], refs[-2:]
    out_ref[:rows, :] = one_ref[...]
    out_ref[rows:, :] = two_ref[...]
    bare_ref[: rows - 16, :] = one_ref[: rows - 16, :]
    bare_ref[rows - 16 :, :] = two_ref[: rows - 16, :]


def copy_kernel(spans, one_ref, *refs):
    done = 0
    for first, count in spans:
        refs[-1][done : done + count, :] = one_ref[first : first + count, :]
        done += count


def pack_kernel(spans, target_ref, *refs):
    out_ref, width = refs[-1], refs[0].shape[1]
    for m, (n, first) in enumerate(spans):
        out_ref[:, m * width : (m + 1) * width] = refs[n][first : first + 16, :]
    target = jnp.broadcast_to(target_ref[...].astype(jnp.float32), (16, target_ref.shape[1]))
    out_ref[:, len(spans) * width :] = target.astype(jnp.bfloat16)


def count_kernel(most_rows, context_ref, mine_ref, other_ref, limit_ref, column_slot_ref, place_ref):
    f32, bf16 = jnp.float32, jnp.bfloat16
    count, width = place_ref.shape[1] // 2, 256
    wide = lax.axis_index("wide")
    core = wide % 2
    mine, other = mine_ref[...].astype(f32), other_ref[...].astype(f32)
    low = jnp.where(core == 0, mine[:1], other[:1])
    high = jnp.where(core == 0, other[:1], mine[:1])
    counts = []
    for n in range(8):
        counts += [low[:, n * width : (n + 1) * width], high[:, n * width : (n + 1) * width]]
    counts = jnp.concatenate(counts, 0)
    lane = lax.broadcasted_iota(jnp.int32, counts.shape, 1)
    row = lax.broadcasted_iota(jnp.int32, counts.shape, 0)
    spread = []
    for b in range(2):
        number = jnp.sum(jnp.where(lane == wide * 2 + b, counts, 0.0), 1, keepdims=True)
        limit = context_ref[b] - jnp.sum(number, 0, keepdims=True).astype(jnp.int32)
        limit_ref[b : b + 1, :] = jnp.broadcast_to(limit, (1, limit_ref.shape[1]))
        spread.append(jnp.sum(jnp.where(lane // most_rows == row, number, 0.0), 0, keepdims=True).astype(jnp.int32))
    spot = lax.broadcasted_iota(jnp.int32, column_slot_ref.shape, 1) % most_rows
    column_slot_ref[...] = jnp.where(spot < spread[0], 0, jnp.where(spot >= most_rows - spread[1], 1, -1))
    earlier = lax.broadcasted_iota(jnp.int32, (count, count), 0) < lax.broadcasted_iota(jnp.int32, (count, count), 1)
    earlier = jnp.where(earlier, 1.0, 0.0).astype(bf16)
    for n, (rows, owner) in enumerate(((mine, core), (other, 1 - core))):
        target = rows[:1, 8 * width : 8 * width + count].astype(jnp.int32)
        hit = jnp.where(lax.broadcasted_iota(jnp.int32, (64, count), 0) == target, 1.0, 0.0)
        before = jnp.dot(hit.astype(bf16), earlier, preferred_element_type=f32)
        rank = jnp.sum(hit * before, 0, keepdims=True).astype(jnp.int32)
        spot = jnp.where(target % 2 == 0, rank, most_rows - 1 - rank)
        chip, side = target // 4, target // 2 % 2
        place_ref[:, n * count : (n + 1) * count] = side * 2 * count + (chip * 2 + owner) * most_rows + spot


def plain_down_kernel(place_ref, prompt_ref, draft_ref, weight_ref, outgoing_ref, draft_latent_ref):
    count = prompt_ref.shape[0]
    rows = jnp.concatenate([prompt_ref[...], draft_ref[...]], 0)
    total = jnp.dot(rows, weight_ref[...], preferred_element_type=jnp.float32)
    draft_latent_ref[...] = total[count : count + 8].astype(jnp.bfloat16).astype(jnp.float32)
    spot = lax.broadcasted_iota(jnp.int32, (outgoing_ref.shape[0], count), 0)
    chosen = jnp.where(spot == place_ref[...], 1.0, 0.0).astype(jnp.bfloat16)
    latent = total[:count].astype(jnp.bfloat16)
    outgoing_ref[...] = jnp.dot(chosen, latent, preferred_element_type=jnp.float32).astype(jnp.bfloat16)


def late_kernel(column_slot_ref, turned_ref, peak_ref, total_ref, mixed_ref, value_up_ref, *refs):
    incoming_refs, (out_ref, rows_ref, parted_ref) = refs[:-3], refs[-3:]
    slot_count, draft_count, _ = out_ref.shape
    heads_kv = value_up_ref.shape[1] // HEAD_SIZE
    group_size = QUERY_HEADS // heads_kv
    head_rows = group_size * draft_count
    rows = peak_ref.shape[1]
    block = incoming_refs[0].shape[0]
    for n, ref in enumerate(incoming_refs):
        rows_ref[n * block : (n + 1) * block, :] = ref[...]
    for b in range(slot_count):
        scores = join_rows(lax.dot_general(turned_ref[b], rows_ref[...], NT, preferred_element_type=jnp.float32))
        scores = jnp.where(column_slot_ref[...] == b, scores, FAR)
        peak = jnp.maximum(jnp.max(scores, 1, keepdims=True), peak_ref[b])
        weights = jnp.exp2(scores - peak)
        fade = jnp.exp2(peak_ref[b] - peak)
        total = total_ref[b] * fade + jnp.sum(weights, 1, keepdims=True)
        mixed = join_rows(jnp.dot(split_rows(weights), rows_ref[...], preferred_element_type=jnp.float32))
        parted_ref[b] = split_rows((mixed_ref[b] * fade + mixed) / total)
    for k in range(heads_kv):
        part = []
        for b in range(slot_count):
            part.append(parted_ref[b, k * head_rows : (k + 1) * head_rows, :])
            part.append(parted_ref[b, rows + k * head_rows : rows + (k + 1) * head_rows, :])
        value_up = value_up_ref[:, k * HEAD_SIZE : (k + 1) * HEAD_SIZE]
        both = jnp.dot(jnp.concatenate(part, 0), value_up, preferred_element_type=jnp.float32)
        for b in range(slot_count):
            result = join_rows(both[b * 2 * head_rows : (b + 1) * 2 * head_rows])
            wide = jnp.concatenate(
                [result[g * draft_count : (g + 1) * draft_count] for g in range(group_size)], 1
            )
            out_ref[b, :, k * group_size * HEAD_SIZE : (k + 1) * group_size * HEAD_SIZE] = wide.astype(jnp.bfloat16)


def deliver(prompt_hidden, draft_hidden, shard, row_target, context_len, held):
    shard_rows, width = shard.shape
    count = prompt_hidden.shape[0]
    spots = [(r, z, y, c) for r in range(2) for z in range(4) for y in range(2) for c in range(2)]
    most_rows = count // 8
    f32, bf16 = jnp.float32, jnp.bfloat16

    def flat(spot):
        return ((spot[0] * 4 + spot[1]) * 2 + spot[2]) * 2 + spot[3]

    def swap(x, r=0, z=0, y=0, c=0):
        pairs = [(flat(spot), flat([a ^ b for a, b in zip(spot, (r, z, y, c))])) for spot in spots]
        return lax.ppermute(x, ("rep", "wide"), pairs)

    def array(rows, dtype=bf16):
        return jax.ShapeDtypeStruct((rows, width), dtype)

    def call(kernel, out_shape, name, *operands, specs=None, flops=2**20, **more):
        return pl.pallas_call(
            kernel,
            out_shape=out_shape,
            in_specs=specs or [WHOLE] * len(operands),
            out_specs=[WHOLE] * len(out_shape) if isinstance(out_shape, list) else WHOLE,
            compiler_params=params(16),
            cost_estimate=pl.CostEstimate(flops=flops, bytes_accessed=2**16, transcendentals=0),
            name=name,
            **more,
        )(*operands)

    hbm = pl.BlockSpec(memory_space=pltpu.HBM)
    half_rows = shard_rows // 2
    ext = half_rows + 16
    padded = (count + 16, prompt_hidden.shape[1])
    half, full, target, rows = call(
        start_kernel,
        [
            array(ext),
            array(shard_rows + 16),
            jax.ShapeDtypeStruct((1, count), jnp.int32),
            jax.ShapeDtypeStruct(padded, bf16),
        ],
        "start_rows",
        *(
            pltpu.with_memory_space_constraint(x, pltpu.HBM)
            for x in (row_target.reshape(1, count), shard, prompt_hidden, draft_hidden)
        ),
        specs=[hbm] * 4,
        scratch_shapes=[pltpu.VMEM(draft_hidden.shape, bf16), pltpu.SemaphoreType.DMA((5,))],
    )
    za, zb = swap(half, z=1), swap(half, z=2)
    y0 = swap(full, y=1)
    rows = [rows, swap(rows, c=1)]
    zab, bare = call(
        join_kernel, [array(2 * ext), array(2 * half_rows)], "join_pieces", za, zb, y0, rows[1], held,
        specs=[WHOLE] * 2 + [UNREAD] * 3,
    )
    yab, xab = swap(zab, y=1), swap(bare, r=1)
    zc = swap(zb, z=1)

    def copy(x, spans, *ties):
        return call(
            functools.partial(copy_kernel, spans), array(sum(rows for _, rows in spans)), "copy_piece", x, *ties,
            specs=[WHOLE] + [UNREAD] * len(ties),
        )

    xc = swap(copy(zc, [(0, half_rows)]), r=1)
    xyab = swap(copy(yab, [(0, half_rows), (ext, half_rows)]), r=1)
    yc = swap(copy(zc, [(0, ext)], yab), y=1)
    yxc = swap(xc, y=1)

    order = [
        (half, half_rows), (y0, shard_rows), (zab, ext + half_rows), (yab, ext + half_rows),
        (zab, half_rows), (yab, half_rows), (zc, half_rows), (yc, half_rows),
    ]
    pack = call(
        functools.partial(pack_kernel, [(n, first) for n, (_, first) in enumerate(order)]),
        jax.ShapeDtypeStruct((16, len(order) * width + count), bf16), "pack_rows",
        target, *(x for x, _ in order), xab, xc,
        specs=[WHOLE] * (1 + len(order)) + [UNREAD] * 2,
    )
    other_pack = swap(pack, c=1)
    limit, column_slot, place = call(
        functools.partial(count_kernel, most_rows),
        [
            jax.ShapeDtypeStruct((2, 128), jnp.int32),
            jax.ShapeDtypeStruct((1, 2 * count), jnp.int32),
            jax.ShapeDtypeStruct((1, 2 * count), jnp.int32),
        ],
        "count_rows", context_len, pack, other_pack,
        specs=[SCALARS, WHOLE, WHOLE],
    )

    def starts_of(uses):
        def starts():
            rep, wide = lax.axis_index("rep"), lax.axis_index("wide")
            z, y, c = wide // 4, wide // 2 % 2, wide % 2
            found = []
            for _, _, _, (x_step, z_step, y_step) in uses:
                owner_z = (z // 2 + z_step // 2) % 2 * 2 + (z + z_step) % 2
                owner = (owner_z * 2 + (y + y_step) % 2) * 2 + c
                found.append(owner * shard_rows + (0 if x_step is None else (rep + x_step) % 2 * half_rows))
            return found

        return starts

    stages = [
        ([full, y0], [(0, 0, shard_rows, (None, 0, 0)), (1, 0, shard_rows, (None, 0, 1))]),
        (
            [zab, yab],
            [(0, 0, half_rows, (0, 1, 0)), (0, ext, half_rows, (0, 2, 0)),
             (1, 0, half_rows, (0, 1, 1)), (1, ext, half_rows, (0, 2, 1))],
        ),
        (
            [xab, zc, yc],
            [(0, 0, half_rows, (1, 1, 0)), (0, half_rows, half_rows, (1, 2, 0)),
             (1, 0, half_rows, (0, 3, 0)), (2, 0, half_rows, (0, 3, 1))],
        ),
        (
            [xc, yxc, xyab],
            [(0, 0, half_rows, (1, 3, 0)), (1, 0, half_rows, (1, 3, 1)),
             (2, 0, half_rows, (1, 1, 1)), (2, half_rows, half_rows, (1, 2, 1))],
        ),
    ]
    sums = []
    total_rows = 2 * padded[0]
    for n, (pieces, uses) in enumerate(stages[:-1]):
        sums = [
            call(
                functools.partial(down_kernel, starts_of(uses), [use[:3] for use in uses], n == 0),
                array(total_rows, f32), "down_rows", *rows, *pieces, *sums, flops=2**26,
            )
        ]

    def finish():
        pieces, uses = stages[-1]
        keep, send = call(
            functools.partial(down_place_kernel, starts_of(uses), [use[:3] for use in uses]),
            [array(2 * count + 8, f32)] * 2, "down_place_rows", *rows, place, *sums, *pieces, flops=2**26,
        )
        came = swap(send, c=1)
        block = array(count)
        draft_latent, stay, send = call(
            route_kernel, [array(8, f32), block, block], "route_rows", keep, came,
            scratch_shapes=[pltpu.VMEM((2 * count + 8, width), f32)],
        )
        came = swap(send, y=1)
        stay, send = call(functools.partial(mix_kernel, 2), [block, block], "mix_rows", stay, came)
        came = swap(send, z=2)
        stay, send = call(functools.partial(mix_kernel, 1), [block, block], "mix_rows", stay, came)
        return draft_latent, [stay, swap(send, z=1)]

    return limit, column_slot, finish


def deliver_plain(prompt_hidden, draft_hidden, shard, row_target, context_len, held):
    wide_size = lax.axis_size("wide")
    row_count = prompt_hidden.shape[0]
    slot_count, draft_count, _ = draft_hidden.shape
    latent_width = shard.shape[1]
    most_rows = 2 * ((row_count + wide_size - 1) // wide_size)
    arrived = wide_size * most_rows
    weight = lax.all_gather(shard, "wide", axis=0, tiled=True)
    index = jnp.arange(row_count, dtype=jnp.int32)
    same = (row_target[:, None] == row_target[None, :]) & (index[None, :] < index[:, None])
    rank = jnp.sum(same.astype(jnp.int32), 1)
    front = row_target % slot_count == 0
    place = row_target // slot_count * most_rows + jnp.where(front, rank, most_rows - 1 - rank)
    request = jnp.arange(wide_size * slot_count, dtype=jnp.int32)
    counts = jnp.sum((row_target[None, :] == request[:, None]).astype(jnp.int32), 1)
    counts = lax.all_to_all(counts.reshape(wide_size, slot_count), "wide", split_axis=0, concat_axis=0, tiled=True)
    limit = jnp.broadcast_to((context_len - jnp.sum(counts, 0))[:, None], (slot_count, 128))
    spot = jnp.arange(most_rows, dtype=jnp.int32)[None, :]
    column_slot = jnp.where(
        spot < counts[:, 0:1], 0, jnp.where(spot >= most_rows - counts[:, 1:2], 1, -1)
    ).reshape(1, arrived)

    tile = slot_count * draft_count
    draft_flat = jnp.pad(draft_hidden.reshape(tile, draft_hidden.shape[2]), ((0, 16 - tile), (0, 0)))

    def finish():
        outgoing, draft_latent = pl.pallas_call(
            plain_down_kernel,
            out_shape=[
                jax.ShapeDtypeStruct((arrived, latent_width), jnp.bfloat16),
                jax.ShapeDtypeStruct((slot_count * draft_count, latent_width), jnp.float32),
            ],
            in_specs=[WHOLE] * 4,
            out_specs=[WHOLE] * 2,
            compiler_params=params(24),
            name="down_rows",
        )(place.reshape(1, row_count), prompt_hidden, draft_flat, weight)
        incoming = lax.all_to_all(
            outgoing.reshape(wide_size, most_rows, latent_width), "wide", split_axis=0, concat_axis=0, tiled=True
        )
        return draft_latent, [incoming.reshape(arrived, latent_width)]

    return limit, column_slot, finish


def local(
    prompt_hidden,
    resident_latent,
    row_target,
    row_offset,
    context_len,
    draft_hidden,
    draft_query_heads,
    down_weight,
    key_up_weight,
    value_up_weight,
):
    f32, bf16 = jnp.float32, jnp.bfloat16
    slot_count, span_rows, latent_width = resident_latent.shape
    draft_count = draft_hidden.shape[1]
    rows = QUERY_HEADS * draft_count
    wide_size, row_count = lax.axis_size("wide"), prompt_hidden.shape[0]
    arrived = 2 * ((row_count + wide_size - 1) // wide_size) * wide_size
    window = min(arrived + 128, span_rows)
    hbm = pl.BlockSpec(memory_space=pltpu.HBM)
    stats = [
        jax.ShapeDtypeStruct((slot_count, rows, 1), f32),
        jax.ShapeDtypeStruct((slot_count, rows, 1), f32),
        jax.ShapeDtypeStruct((slot_count, rows, latent_width), f32),
    ]
    turned, peak, total, mixed, edge = pl.pallas_call(
        functools.partial(held_kernel, arrived),
        out_shape=[
            jax.ShapeDtypeStruct((slot_count, 2 * rows, latent_width), bf16),
            *stats,
            jax.ShapeDtypeStruct((slot_count, window, latent_width), bf16),
        ],
        in_specs=[SCALARS, hbm, hbm, hbm],
        out_specs=[WHOLE] * 5,
        scratch_shapes=[
            pltpu.VMEM(draft_query_heads.shape, bf16),
            pltpu.VMEM(key_up_weight.shape, bf16),
            pltpu.VMEM(resident_latent.shape, bf16),
            pltpu.VMEM((slot_count, rows, latent_width), f32),
            pltpu.VMEM((rows, span_rows), f32),
            pltpu.SemaphoreType.DMA((3,)),
        ],
        compiler_params=params(16),
        cost_estimate=pl.CostEstimate(flops=2**31, bytes_accessed=2**21, transcendentals=0),
        name="held_rows",
    )(context_len, *(pltpu.with_memory_space_constraint(x, pltpu.HBM) for x in (draft_query_heads, key_up_weight, resident_latent)))
    known = wide_size == 16 and lax.axis_size("rep") == 2
    limit, column_slot, finish = (deliver if known else deliver_plain)(
        prompt_hidden, draft_hidden, down_weight, row_target, context_len, peak
    )
    draft_latent, incoming = finish()
    peak, total, mixed = pl.pallas_call(
        functools.partial(window_kernel, arrived, span_rows, draft_count),
        out_shape=stats,
        in_specs=[SCALARS] + [WHOLE] * 7,
        out_specs=[WHOLE] * 3,
        compiler_params=params(16),
        cost_estimate=pl.CostEstimate(flops=2**30, bytes_accessed=2**16, transcendentals=0),
        name="window_rows",
    )(context_len, limit, turned, peak, total, mixed, edge, draft_latent)
    return pl.pallas_call(
        late_kernel,
        out_shape=jax.ShapeDtypeStruct((slot_count, draft_count, QUERY_HEADS * HEAD_SIZE), bf16),
        in_specs=[WHOLE] * (6 + len(incoming)),
        out_specs=WHOLE,
        scratch_shapes=[
            pltpu.VMEM((arrived, latent_width), bf16),
            pltpu.VMEM((slot_count, 2 * rows, latent_width), bf16),
        ],
        compiler_params=params(16),
        name="late_rows",
    )(column_slot, turned, peak, total, mixed, value_up_weight, *incoming)


def solution(mesh):
    placed = (
        P(("rep", "wide"), None),
        P(("rep", "wide"), None, None),
        P(("rep", "wide")),
        P(("rep", "wide")),
        P(("rep", "wide")),
        P(("rep", "wide"), None, None),
        P(("rep", "wide"), None, None),
        P("wide", None),
        P(),
        P(),
    )
    return jax.shard_map(
        local, mesh=mesh, in_specs=placed, out_specs=P(("rep", "wide"), None, None), check_vma=False
    )
```

```python
import functools
import math

import jax
import jax.numpy as jnp
from jax import lax
from jax.experimental import pallas as pl
from jax.experimental.pallas import tpu as pltpu
from jax.sharding import PartitionSpec as P

QUERY_HEADS = 64
HEAD_SIZE = 128
FAR = -1e30
NT = (((1,), (1,)), ((), ()))
WHOLE = pl.BlockSpec(memory_space=pltpu.VMEM)
SCALARS = pl.BlockSpec(memory_space=pltpu.SMEM)
UNREAD = pl.BlockSpec(memory_space=pl.ANY)


def params(mib):
    return pltpu.CompilerParams(vmem_limit_bytes=mib * 1024 * 1024)


def split_rows(x):
    top = x.astype(jnp.bfloat16)
    rest = (x - top.astype(jnp.float32)).astype(jnp.bfloat16)
    return jnp.concatenate([top, rest], 0)


def join_rows(x):
    half = x.shape[0] // 2
    return x[:half] + x[half:]


def held_kernel(
    slot, arrived, context_ref, query_hbm, key_up_hbm, cache_hbm, tie_ref,
    turned_ref, peak_ref, total_ref, mixed_ref, window_ref,
    query_ref, key_up_ref, cache_ref, float_ref, scores_ref, sems,
):
    copies = [
        pltpu.make_async_copy(source, target, sems.at[n])
        for n, (source, target) in enumerate(
            [(query_hbm.at[slot], query_ref), (key_up_hbm, key_up_ref), (cache_hbm.at[slot], cache_ref)]
        )
    ]
    for copy in copies:
        copy.start()
    span_rows = cache_ref.shape[0]
    heads_kv = key_up_ref.shape[1] // HEAD_SIZE
    group_size = QUERY_HEADS // heads_kv
    rows = group_size * query_ref.shape[0]
    scale = math.log2(math.e) / math.sqrt(HEAD_SIZE)
    step = 256
    copies[0].wait()
    copies[1].wait()
    for k in range(heads_kv):
        lanes = [slice(h * HEAD_SIZE, (h + 1) * HEAD_SIZE) for h in range(k * group_size, (k + 1) * group_size)]
        query = jnp.concatenate([query_ref[:, lane].astype(jnp.float32) for lane in lanes], 0).astype(jnp.bfloat16)
        key_up = key_up_ref[:, k * HEAD_SIZE : (k + 1) * HEAD_SIZE]
        turned = lax.dot_general(query, key_up, NT, preferred_element_type=jnp.float32)
        float_ref[k * rows : (k + 1) * rows, :] = turned * scale
    copies[2].wait()
    first = pl.multiple_of(window_start(context_ref[slot], arrived, window_ref.shape[0], span_rows), 128)
    window_ref[...] = cache_ref[pl.ds(first, window_ref.shape[0]), :]
    turned_ref[...] = split_rows(float_ref[...])
    peak = None
    for c in range(0, span_rows, step):
        scores = join_rows(
            lax.dot_general(turned_ref[...], cache_ref[c : c + step], NT, preferred_element_type=jnp.float32)
        )
        column = lax.broadcasted_iota(jnp.int32, (1, step), 1) + c
        scores = jnp.where(column < context_ref[slot] - arrived, scores, FAR)
        scores_ref[:, c : c + step] = scores
        top = jnp.max(scores, 1, keepdims=True)
        peak = top if peak is None else jnp.maximum(peak, top)
    peak_ref[...] = peak
    total = jnp.zeros_like(peak)
    mixed = jnp.zeros(mixed_ref.shape, jnp.float32)
    for c in range(0, span_rows, step):
        weights = jnp.exp2(scores_ref[:, c : c + step] - peak)
        total += jnp.sum(weights, 1, keepdims=True)
        mixed += join_rows(jnp.dot(split_rows(weights), cache_ref[c : c + step], preferred_element_type=jnp.float32))
    total_ref[...] = total
    mixed_ref[...] = mixed


def window_start(context, arrived, size, span_rows):
    return jnp.clip((context - arrived) // 128 * 128, 0, span_rows - size)


def window_kernel(
    arrived, span_rows, draft_count, context_ref, limit_ref, draft_latent_ref, *refs
):
    held_refs, (new_peak_ref, new_total_ref, new_mixed_ref) = refs[:-3], refs[-3:]
    slot_count, rows, width = new_mixed_ref.shape
    drafts = draft_latent_ref[...]
    drafts = jnp.concatenate([drafts, jnp.zeros((128 - drafts.shape[0], width), jnp.float32)], 0).astype(jnp.bfloat16)
    token = lax.broadcasted_iota(jnp.int32, (rows, 1), 0) % draft_count
    spot = lax.broadcasted_iota(jnp.int32, (rows, 128), 1)
    for b in range(slot_count):
        turned_ref, peak_ref, total_ref, mixed_ref, window_ref = held_refs[5 * b : 5 * b + 5]
        size = window_ref.shape[0]
        first = window_start(context_ref[b], arrived, size, span_rows)
        scores = join_rows(lax.dot_general(turned_ref[...], window_ref[...], NT, preferred_element_type=jnp.float32))
        column = lax.broadcasted_iota(jnp.int32, (1, size), 1) + first
        seen = (column >= context_ref[b] - arrived) & (column < limit_ref[b : b + 1, 0:1])
        scores = jnp.where(seen, scores, FAR)
        draft_scores = join_rows(lax.dot_general(turned_ref[...], drafts, NT, preferred_element_type=jnp.float32))
        draft_seen = (spot >= b * draft_count) & (spot <= b * draft_count + token)
        draft_scores = jnp.where(draft_seen, draft_scores, FAR)
        peak = jnp.maximum(jnp.max(scores, 1, keepdims=True), jnp.max(draft_scores, 1, keepdims=True))
        peak = jnp.maximum(peak, peak_ref[...])
        weights, draft_weights = jnp.exp2(scores - peak), jnp.exp2(draft_scores - peak)
        fade = jnp.exp2(peak_ref[...] - peak)
        new_peak_ref[b] = peak
        total = jnp.sum(weights, 1, keepdims=True) + jnp.sum(draft_weights, 1, keepdims=True)
        new_total_ref[b] = total_ref[...] * fade + total
        mixed = jnp.dot(split_rows(weights), window_ref[...], preferred_element_type=jnp.float32)
        mixed += jnp.dot(split_rows(draft_weights), drafts, preferred_element_type=jnp.float32)
        new_mixed_ref[b] = mixed_ref[...] * fade + join_rows(mixed)


def piece_sums(starts, spans, row_refs, refs):
    total = None
    for start, (n, first, depth) in zip(starts, spans):
        lanes = pl.ds(pl.multiple_of(start, HEAD_SIZE), depth)
        rows = [ref[:, lanes] for ref in row_refs]
        piece = refs[n][first : first + depth, :]
        product = jnp.dot(jnp.concatenate(rows, 0), piece, preferred_element_type=jnp.float32)
        total = product if total is None else total + product
    return total


def down_kernel(starts_of, spans, first, *refs):
    row_refs, refs, out_ref = refs[:4], refs[4:-1], refs[-1]
    total = piece_sums(starts_of(), spans, row_refs, refs)
    out_ref[...] = total if first else total + refs[-1][...]


def down_place_kernel(starts_of, spans, *refs):
    row_refs, refs, (keep_ref, send_ref) = refs[:4], refs[4:-2], refs[-2:]
    place_ref, sum_ref, refs = refs[0], refs[1], refs[2:]
    total = piece_sums(starts_of(), spans, row_refs, refs) + sum_ref[...]
    slots, width = keep_ref.shape[0] - 8, keep_ref.shape[1]
    count = place_ref.shape[1]
    parts = []
    left = total[:count]
    for _ in range(3):
        part = left.astype(jnp.bfloat16)
        parts.append(part)
        left = left - part.astype(jnp.float32)
    parts = jnp.concatenate(parts, 1)
    core = lax.axis_index("wide") % 2
    spot = lax.broadcasted_iota(jnp.int32, (slots, count), 0)
    for ref, target, draft in ((keep_ref, core, count), (send_ref, 1 - core, count + 16)):
        chosen = jnp.where(spot + target * slots == place_ref[...], 1.0, 0.0).astype(jnp.bfloat16)
        moved = jnp.dot(chosen, parts, preferred_element_type=jnp.float32)
        ref[:slots, :] = moved[:, :width] + moved[:, width : 2 * width] + moved[:, 2 * width :]
        ref[slots:, :] = total[draft : draft + 8]


def route_kernel(keep_ref, came_ref, draft_latent_ref, stay_ref, send_ref, float_ref):
    float_ref[...] = keep_ref[...] + came_ref[...]
    slots = float_ref.shape[0] - 8
    draft_latent_ref[...] = float_ref[slots:, :].astype(jnp.bfloat16).astype(jnp.float32)
    size = slots // 8
    wide = lax.axis_index("wide")
    z, y = wide // 4, wide // 2 % 2
    for other, ref in ((0, stay_ref), (1, send_ref)):
        for n, (high, low) in enumerate(((0, 0), (0, 1), (1, 0), (1, 1))):
            there = (z // 2 + high) % 2 * 2 + (z + low) % 2
            block = there * 2 + (y + other) % 2
            rows = pl.ds(pl.multiple_of(block * size, size), size)
            ref[n * size : (n + 1) * size, :] = float_ref[rows, :].astype(jnp.bfloat16)


def mix_kernel(outer, keep_ref, came_ref, stay_ref, send_ref):
    half = keep_ref.shape[0] // 2
    size = half // outer
    for ref, first in ((stay_ref, 0), (send_ref, half)):
        for n in range(outer):
            for m, source in enumerate((keep_ref, came_ref)):
                spot = (n * 2 + m) * size
                ref[spot : spot + size, :] = source[first + n * size : first + (n + 1) * size, :]


def start_kernel(target_hbm, shard_hbm, draft_hbm, half_ref, full_ref, target_ref, rows_ref, draft_ref, sems):
    half_rows, shard_rows = half_ref.shape[0] - 16, full_ref.shape[0] - 16
    mine = pl.ds(pl.multiple_of(lax.axis_index("rep") * half_rows, half_rows), half_rows)
    copies = [
        pltpu.make_async_copy(target_hbm, target_ref, sems.at[0]),
        pltpu.make_async_copy(shard_hbm.at[mine], half_ref.at[:half_rows], sems.at[1]),
        pltpu.make_async_copy(shard_hbm, full_ref.at[:shard_rows], sems.at[2]),
        pltpu.make_async_copy(draft_hbm, draft_ref, sems.at[3]),
    ]
    for copy in copies:
        copy.start()
    width, count = half_ref.shape[1], target_ref.shape[1]
    copies[0].wait()
    hit = lax.broadcasted_iota(jnp.int32, (width, count), 0) == target_ref[...]
    hit = jnp.where(hit, 1.0, 0.0).astype(jnp.bfloat16)
    block = lax.dot_general(jnp.ones((16, count), jnp.bfloat16), hit, NT, preferred_element_type=jnp.float32)
    half_ref[half_rows:, :] = block.astype(jnp.bfloat16)
    full_ref[shard_rows:, :] = block.astype(jnp.bfloat16)
    copies[3].wait()
    rows = [draft_ref[b].astype(jnp.float32) for b in range(draft_ref.shape[0])]
    rows.append(jnp.zeros((8, rows_ref.shape[1]), jnp.float32))
    rows_ref[...] = jnp.concatenate(rows, 0).astype(jnp.bfloat16)
    for copy in copies[1:3]:
        copy.wait()


def join_kernel(one_ref, two_ref, *refs):
    rows, (out_ref, bare_ref) = one_ref.shape[0], refs[-2:]
    out_ref[:rows, :] = one_ref[...]
    out_ref[rows:, :] = two_ref[...]
    bare_ref[: rows - 16, :] = one_ref[: rows - 16, :]
    bare_ref[rows - 16 :, :] = two_ref[: rows - 16, :]


def tail_kernel(one_ref, two_ref, out_ref):
    rest = out_ref.shape[0] - two_ref.shape[0]
    out_ref[:rest, :] = one_ref[one_ref.shape[0] - rest :, :]
    out_ref[rest:, :] = two_ref[...]


def copy_kernel(spans, one_ref, *refs):
    done = 0
    for first, count in spans:
        refs[-1][done : done + count, :] = one_ref[first : first + count, :]
        done += count


def pack_kernel(spans, target_ref, *refs):
    out_ref, width = refs[-1], refs[0].shape[1]
    for m, (n, first) in enumerate(spans):
        out_ref[:, m * width : (m + 1) * width] = refs[n][first : first + 16, :]
    target = jnp.broadcast_to(target_ref[...].astype(jnp.float32), (16, target_ref.shape[1]))
    out_ref[:, len(spans) * width :] = target.astype(jnp.bfloat16)


def count_kernel(most_rows, context_ref, mine_ref, other_ref, limit_ref, column_slot_ref, place_ref):
    f32, bf16 = jnp.float32, jnp.bfloat16
    count, width = place_ref.shape[1] // 2, 256
    wide = lax.axis_index("wide")
    core = wide % 2
    mine, other = mine_ref[...].astype(f32), other_ref[...].astype(f32)
    low = jnp.where(core == 0, mine[:1], other[:1])
    high = jnp.where(core == 0, other[:1], mine[:1])
    counts = []
    for n in range(8):
        counts += [low[:, n * width : (n + 1) * width], high[:, n * width : (n + 1) * width]]
    counts = jnp.concatenate(counts, 0)
    lane = lax.broadcasted_iota(jnp.int32, counts.shape, 1)
    row = lax.broadcasted_iota(jnp.int32, counts.shape, 0)
    spread = []
    for b in range(2):
        number = jnp.sum(jnp.where(lane == wide * 2 + b, counts, 0.0), 1, keepdims=True)
        limit = context_ref[b] - jnp.sum(number, 0, keepdims=True).astype(jnp.int32)
        limit_ref[b : b + 1, :] = jnp.broadcast_to(limit, (1, limit_ref.shape[1]))
        spread.append(jnp.sum(jnp.where(lane // most_rows == row, number, 0.0), 0, keepdims=True).astype(jnp.int32))
    spot = lax.broadcasted_iota(jnp.int32, column_slot_ref.shape, 1) % most_rows
    column_slot_ref[...] = jnp.where(spot < spread[0], 0, jnp.where(spot >= most_rows - spread[1], 1, -1))
    earlier = lax.broadcasted_iota(jnp.int32, (count, count), 0) < lax.broadcasted_iota(jnp.int32, (count, count), 1)
    earlier = jnp.where(earlier, 1.0, 0.0).astype(bf16)
    for n, (rows, owner) in enumerate(((mine, core), (other, 1 - core))):
        target = rows[:1, 8 * width : 8 * width + count].astype(jnp.int32)
        hit = jnp.where(lax.broadcasted_iota(jnp.int32, (64, count), 0) == target, 1.0, 0.0)
        before = jnp.dot(hit.astype(bf16), earlier, preferred_element_type=f32)
        rank = jnp.sum(hit * before, 0, keepdims=True).astype(jnp.int32)
        spot = jnp.where(target % 2 == 0, rank, most_rows - 1 - rank)
        chip, side = target // 4, target // 2 % 2
        place_ref[:, n * count : (n + 1) * count] = side * 2 * count + (chip * 2 + owner) * most_rows + spot


def plain_down_kernel(place_ref, prompt_ref, draft_ref, weight_ref, outgoing_ref, draft_latent_ref):
    count = prompt_ref.shape[0]
    rows = jnp.concatenate([prompt_ref[...], draft_ref[...]], 0)
    total = jnp.dot(rows, weight_ref[...], preferred_element_type=jnp.float32)
    draft_latent_ref[...] = total[count : count + 8].astype(jnp.bfloat16).astype(jnp.float32)
    spot = lax.broadcasted_iota(jnp.int32, (outgoing_ref.shape[0], count), 0)
    chosen = jnp.where(spot == place_ref[...], 1.0, 0.0).astype(jnp.bfloat16)
    latent = total[:count].astype(jnp.bfloat16)
    outgoing_ref[...] = jnp.dot(chosen, latent, preferred_element_type=jnp.float32).astype(jnp.bfloat16)


def late_kernel(column_slot_ref, peak_ref, total_ref, mixed_ref, value_up_ref, *refs):
    refs, (out_ref, rows_ref, parted_ref) = refs[:-3], refs[-3:]
    slot_count, draft_count, _ = out_ref.shape
    turned_refs, incoming_refs = refs[:slot_count], refs[slot_count:]
    heads_kv = value_up_ref.shape[1] // HEAD_SIZE
    group_size = QUERY_HEADS // heads_kv
    head_rows = group_size * draft_count
    rows = peak_ref.shape[1]
    block = incoming_refs[0].shape[0]
    for n, ref in enumerate(incoming_refs):
        rows_ref[n * block : (n + 1) * block, :] = ref[...]
    for b in range(slot_count):
        scores = join_rows(lax.dot_general(turned_refs[b][...], rows_ref[...], NT, preferred_element_type=jnp.float32))
        scores = jnp.where(column_slot_ref[...] == b, scores, FAR)
        peak = jnp.maximum(jnp.max(scores, 1, keepdims=True), peak_ref[b])
        weights = jnp.exp2(scores - peak)
        fade = jnp.exp2(peak_ref[b] - peak)
        total = total_ref[b] * fade + jnp.sum(weights, 1, keepdims=True)
        mixed = join_rows(jnp.dot(split_rows(weights), rows_ref[...], preferred_element_type=jnp.float32))
        parted_ref[b] = split_rows((mixed_ref[b] * fade + mixed) / total)
    for k in range(heads_kv):
        part = []
        for b in range(slot_count):
            part.append(parted_ref[b, k * head_rows : (k + 1) * head_rows, :])
            part.append(parted_ref[b, rows + k * head_rows : rows + (k + 1) * head_rows, :])
        value_up = value_up_ref[:, k * HEAD_SIZE : (k + 1) * HEAD_SIZE]
        both = jnp.dot(jnp.concatenate(part, 0), value_up, preferred_element_type=jnp.float32)
        for b in range(slot_count):
            result = join_rows(both[b * 2 * head_rows : (b + 1) * 2 * head_rows])
            wide = jnp.concatenate(
                [result[g * draft_count : (g + 1) * draft_count] for g in range(group_size)], 1
            )
            out_ref[b, :, k * group_size * HEAD_SIZE : (k + 1) * group_size * HEAD_SIZE] = wide.astype(jnp.bfloat16)


def deliver(prompt_hidden, draft_hidden, shard, row_target, context_len, held):
    shard_rows, width = shard.shape
    count = prompt_hidden.shape[0]
    spots = [(r, z, y, c) for r in range(2) for z in range(4) for y in range(2) for c in range(2)]
    most_rows = count // 8
    f32, bf16 = jnp.float32, jnp.bfloat16

    def flat(spot):
        return ((spot[0] * 4 + spot[1]) * 2 + spot[2]) * 2 + spot[3]

    def swap(x, r=0, z=0, y=0, c=0):
        pairs = [(flat(spot), flat([a ^ b for a, b in zip(spot, (r, z, y, c))])) for spot in spots]
        return lax.ppermute(x, ("rep", "wide"), pairs)

    def array(rows, dtype=bf16):
        return jax.ShapeDtypeStruct((rows, width), dtype)

    def call(kernel, out_shape, name, *operands, specs=None, flops=2**20, **more):
        return pl.pallas_call(
            kernel,
            out_shape=out_shape,
            in_specs=specs or [WHOLE] * len(operands),
            out_specs=[WHOLE] * len(out_shape) if isinstance(out_shape, list) else WHOLE,
            compiler_params=params(16),
            cost_estimate=pl.CostEstimate(flops=flops, bytes_accessed=2**16, transcendentals=0),
            name=name,
            **more,
        )(*operands)

    hbm = pl.BlockSpec(memory_space=pltpu.HBM)
    half_rows = shard_rows // 2
    ext = half_rows + 16
    half, full, target, draft_rows = call(
        start_kernel,
        [
            array(ext),
            array(shard_rows + 16),
            jax.ShapeDtypeStruct((1, count), jnp.int32),
            jax.ShapeDtypeStruct((16, draft_hidden.shape[2]), bf16),
        ],
        "start_rows",
        *(pltpu.with_memory_space_constraint(x, pltpu.HBM) for x in (row_target.reshape(1, count), shard, draft_hidden)),
        specs=[hbm] * 3,
        scratch_shapes=[pltpu.VMEM(draft_hidden.shape, bf16), pltpu.SemaphoreType.DMA((4,))],
    )
    za, zb = swap(half, z=1), swap(half, z=2)
    y0 = swap(full, y=1)
    other_prompt, other_drafts = swap(prompt_hidden, c=1), swap(draft_rows, c=1)

    def copy(x, spans, *ties):
        return call(
            functools.partial(copy_kernel, spans), array(sum(rows for _, rows in spans)), "copy_piece", x, *ties,
            specs=[WHOLE] + [UNREAD] * len(ties),
        )

    held_rows = [held(b, half) for b in range(2)]
    zab, bare = call(
        join_kernel, [array(2 * ext), array(2 * half_rows)], "join_pieces", za, zb, y0, other_drafts,
        *(x[1] for x in held_rows), specs=[WHOLE] * 2 + [UNREAD] * 4,
    )
    yab, xab = swap(zab, y=1), swap(bare, r=1)
    zc = swap(zb, z=1)
    xc = swap(copy(zc, [(0, half_rows)]), r=1)
    quarter = half_rows // 2
    xy = swap(copy(yab, [(0, half_rows), (ext, quarter)]), r=1)
    yc = swap(copy(zc, [(0, ext)], yab), y=1)
    yx = swap(call(tail_kernel, array(quarter + half_rows), "tail_piece", xab, xc), y=1)

    order = [
        (half, half_rows), (y0, shard_rows), (zab, ext + half_rows), (yab, ext + half_rows),
        (zab, half_rows), (yab, half_rows), (zc, half_rows), (yc, half_rows),
    ]
    pack = call(
        functools.partial(pack_kernel, [(n, first) for n, (_, first) in enumerate(order)]),
        jax.ShapeDtypeStruct((16, len(order) * width + count), bf16), "pack_rows",
        target, *(x for x, _ in order), xab, xc, other_prompt,
        specs=[WHOLE] * (1 + len(order)) + [UNREAD] * 3,
    )
    other_pack = swap(pack, c=1)
    limit, column_slot, place = call(
        functools.partial(count_kernel, most_rows),
        [
            jax.ShapeDtypeStruct((2, 128), jnp.int32),
            jax.ShapeDtypeStruct((1, 2 * count), jnp.int32),
            jax.ShapeDtypeStruct((1, 2 * count), jnp.int32),
        ],
        "count_rows", context_len, pack, other_pack,
        specs=[SCALARS, WHOLE, WHOLE],
    )

    def starts_of(uses):
        def starts():
            rep, wide = lax.axis_index("rep"), lax.axis_index("wide")
            z, y, c = wide // 4, wide // 2 % 2, wide % 2
            found = []
            for _, _, _, (x_step, z_step, y_step), *further in uses:
                owner_z = (z // 2 + z_step // 2) % 2 * 2 + (z + z_step) % 2
                owner = (owner_z * 2 + (y + y_step) % 2) * 2 + c
                start = owner * shard_rows + (0 if x_step is None else (rep + x_step) % 2 * half_rows)
                found.append(start + sum(further))
            return found

        return starts

    rows = [prompt_hidden, other_prompt, draft_rows, other_drafts]
    stages = [
        ([full, y0], [(0, 0, shard_rows, (None, 0, 0)), (1, 0, shard_rows, (None, 0, 1))]),
        (
            [zab, yab],
            [(0, 0, half_rows, (0, 1, 0)), (0, ext, half_rows, (0, 2, 0)),
             (1, 0, half_rows, (0, 1, 1)), (1, ext, half_rows, (0, 2, 1))],
        ),
        (
            [xab, zc, yc],
            [(0, 0, half_rows, (1, 1, 0)), (0, half_rows, half_rows, (1, 2, 0)),
             (1, 0, half_rows, (0, 3, 0)), (2, 0, half_rows, (0, 3, 1))],
        ),
        (
            [xc, yx, xy],
            [(0, 0, half_rows, (1, 3, 0)), (1, quarter, half_rows, (1, 3, 1)), (2, 0, half_rows, (1, 1, 1)),
             (2, half_rows, quarter, (1, 2, 1)), (1, 0, quarter, (1, 2, 1), quarter)],
        ),
    ]
    sums = []
    total_rows = 2 * count + 32
    for n, (pieces, uses) in enumerate(stages[:-1]):
        sums = [
            call(
                functools.partial(down_kernel, starts_of(uses), [use[:3] for use in uses], n == 0),
                array(total_rows, f32), "down_rows", *rows, *pieces, *sums, flops=2**26,
            )
        ]

    def finish():
        pieces, uses = stages[-1]
        keep, send = call(
            functools.partial(down_place_kernel, starts_of(uses), [use[:3] for use in uses]),
            [array(2 * count + 8, f32)] * 2, "down_place_rows", *rows, place, *sums, *pieces, flops=2**26,
        )
        came = swap(send, c=1)
        block = array(count)
        draft_latent, stay, send = call(
            route_kernel, [array(8, f32), block, block], "route_rows", keep, came,
            scratch_shapes=[pltpu.VMEM((2 * count + 8, width), f32)],
        )
        came = swap(send, y=1)
        stay, send = call(functools.partial(mix_kernel, 2), [block, block], "mix_rows", stay, came)
        came = swap(send, z=2)
        stay, send = call(functools.partial(mix_kernel, 1), [block, block], "mix_rows", stay, came)
        return draft_latent, [stay, swap(send, z=1)]

    return limit, column_slot, finish, held_rows


def deliver_plain(prompt_hidden, draft_hidden, shard, row_target, context_len, held):
    wide_size = lax.axis_size("wide")
    row_count = prompt_hidden.shape[0]
    slot_count, draft_count, _ = draft_hidden.shape
    latent_width = shard.shape[1]
    most_rows = 2 * ((row_count + wide_size - 1) // wide_size)
    arrived = wide_size * most_rows
    weight = lax.all_gather(shard, "wide", axis=0, tiled=True)
    index = jnp.arange(row_count, dtype=jnp.int32)
    same = (row_target[:, None] == row_target[None, :]) & (index[None, :] < index[:, None])
    rank = jnp.sum(same.astype(jnp.int32), 1)
    front = row_target % slot_count == 0
    place = row_target // slot_count * most_rows + jnp.where(front, rank, most_rows - 1 - rank)
    request = jnp.arange(wide_size * slot_count, dtype=jnp.int32)
    counts = jnp.sum((row_target[None, :] == request[:, None]).astype(jnp.int32), 1)
    counts = lax.all_to_all(counts.reshape(wide_size, slot_count), "wide", split_axis=0, concat_axis=0, tiled=True)
    limit = jnp.broadcast_to((context_len - jnp.sum(counts, 0))[:, None], (slot_count, 128))
    spot = jnp.arange(most_rows, dtype=jnp.int32)[None, :]
    column_slot = jnp.where(
        spot < counts[:, 0:1], 0, jnp.where(spot >= most_rows - counts[:, 1:2], 1, -1)
    ).reshape(1, arrived)

    tile = slot_count * draft_count
    draft_flat = jnp.pad(draft_hidden.reshape(tile, draft_hidden.shape[2]), ((0, 16 - tile), (0, 0)))

    def finish():
        outgoing, draft_latent = pl.pallas_call(
            plain_down_kernel,
            out_shape=[
                jax.ShapeDtypeStruct((arrived, latent_width), jnp.bfloat16),
                jax.ShapeDtypeStruct((slot_count * draft_count, latent_width), jnp.float32),
            ],
            in_specs=[WHOLE] * 4,
            out_specs=[WHOLE] * 2,
            compiler_params=params(24),
            name="down_rows",
        )(place.reshape(1, row_count), prompt_hidden, draft_flat, weight)
        incoming = lax.all_to_all(
            outgoing.reshape(wide_size, most_rows, latent_width), "wide", split_axis=0, concat_axis=0, tiled=True
        )
        return draft_latent, [incoming.reshape(arrived, latent_width)]

    return limit, column_slot, finish, [held(b, context_len) for b in range(slot_count)]


def local(
    prompt_hidden,
    resident_latent,
    row_target,
    row_offset,
    context_len,
    draft_hidden,
    draft_query_heads,
    down_weight,
    key_up_weight,
    value_up_weight,
):
    f32, bf16 = jnp.float32, jnp.bfloat16
    slot_count, span_rows, latent_width = resident_latent.shape
    draft_count = draft_hidden.shape[1]
    rows = QUERY_HEADS * draft_count
    wide_size, row_count = lax.axis_size("wide"), prompt_hidden.shape[0]
    arrived = 2 * ((row_count + wide_size - 1) // wide_size) * wide_size
    window = min(arrived + 128, span_rows)
    hbm = pl.BlockSpec(memory_space=pltpu.HBM)
    stats = [
        jax.ShapeDtypeStruct((slot_count, rows, 1), f32),
        jax.ShapeDtypeStruct((slot_count, rows, 1), f32),
        jax.ShapeDtypeStruct((slot_count, rows, latent_width), f32),
    ]
    held_rows = [
        jax.ShapeDtypeStruct((2 * rows, latent_width), bf16),
        *(jax.ShapeDtypeStruct(x.shape[1:], f32) for x in stats),
        jax.ShapeDtypeStruct((window, latent_width), bf16),
    ]
    sources = [
        pltpu.with_memory_space_constraint(x, pltpu.HBM) for x in (draft_query_heads, key_up_weight, resident_latent)
    ]

    def held(slot, tie):
        return pl.pallas_call(
            functools.partial(held_kernel, slot, arrived),
            out_shape=held_rows,
            in_specs=[SCALARS, hbm, hbm, hbm, UNREAD],
            out_specs=[WHOLE] * 5,
            scratch_shapes=[
                pltpu.VMEM(draft_query_heads.shape[1:], bf16),
                pltpu.VMEM(key_up_weight.shape, bf16),
                pltpu.VMEM(resident_latent.shape[1:], bf16),
                pltpu.VMEM((rows, latent_width), f32),
                pltpu.VMEM((rows, span_rows), f32),
                pltpu.SemaphoreType.DMA((3,)),
            ],
            compiler_params=params(16),
            cost_estimate=pl.CostEstimate(flops=2**31, bytes_accessed=2**21, transcendentals=0),
            name="held_rows",
        )(context_len, *sources, tie)

    known = wide_size == 16 and lax.axis_size("rep") == 2
    limit, column_slot, finish, held = (deliver if known else deliver_plain)(
        prompt_hidden, draft_hidden, down_weight, row_target, context_len, held
    )
    draft_latent, incoming = finish()
    peak, total, mixed = pl.pallas_call(
        functools.partial(window_kernel, arrived, span_rows, draft_count),
        out_shape=stats,
        in_specs=[SCALARS] + [WHOLE] * (2 + 5 * slot_count),
        out_specs=[WHOLE] * 3,
        compiler_params=params(16),
        cost_estimate=pl.CostEstimate(flops=2**30, bytes_accessed=2**16, transcendentals=0),
        name="window_rows",
    )(context_len, limit, draft_latent, *(x for one in held for x in one))
    return pl.pallas_call(
        late_kernel,
        out_shape=jax.ShapeDtypeStruct((slot_count, draft_count, QUERY_HEADS * HEAD_SIZE), bf16),
        in_specs=[WHOLE] * (5 + slot_count + len(incoming)),
        out_specs=WHOLE,
        scratch_shapes=[
            pltpu.VMEM((arrived, latent_width), bf16),
            pltpu.VMEM((slot_count, 2 * rows, latent_width), bf16),
        ],
        compiler_params=params(16),
        name="late_rows",
    )(column_slot, peak, total, mixed, value_up_weight, *(one[0] for one in held), *incoming)


def solution(mesh):
    placed = (
        P(("rep", "wide"), None),
        P(("rep", "wide"), None, None),
        P(("rep", "wide")),
        P(("rep", "wide")),
        P(("rep", "wide")),
        P(("rep", "wide"), None, None),
        P(("rep", "wide"), None, None),
        P("wide", None),
        P(),
        P(),
    )
    return jax.shard_map(
        local, mesh=mesh, in_specs=placed, out_specs=P(("rep", "wide"), None, None), check_vma=False
    )
```

```python
import functools
import math

import jax
import jax.numpy as jnp
from jax import lax
from jax.experimental import pallas as pl
from jax.experimental.pallas import tpu as pltpu
from jax.sharding import PartitionSpec as P

QUERY_HEADS = 64
HEAD_SIZE = 128
FAR = -1e30
NT = (((1,), (1,)), ((), ()))
WHOLE = pl.BlockSpec(memory_space=pltpu.VMEM)
SCALARS = pl.BlockSpec(memory_space=pltpu.SMEM)
UNREAD = pl.BlockSpec(memory_space=pl.ANY)


def params(mib):
    return pltpu.CompilerParams(vmem_limit_bytes=mib * 1024 * 1024)


def split_rows(x):
    top = x.astype(jnp.bfloat16)
    rest = (x - top.astype(jnp.float32)).astype(jnp.bfloat16)
    return jnp.concatenate([top, rest], 0)


def join_rows(x):
    half = x.shape[0] // 2
    return x[:half] + x[half:]


def held_kernel(
    arrived, context_ref, query_hbm, key_up_hbm, cache_hbm, turned_ref, peak_ref, total_ref, mixed_ref, window_ref,
    query_ref, key_up_ref, cache_ref, float_ref, scores_ref, sems,
):
    copies = [
        pltpu.make_async_copy(source, target, sems.at[n])
        for n, (source, target) in enumerate(
            [(query_hbm, query_ref), (key_up_hbm, key_up_ref), (cache_hbm, cache_ref)]
        )
    ]
    for copy in copies:
        copy.start()
    slot_count, span_rows, _ = cache_ref.shape
    draft_count = query_ref.shape[1]
    heads_kv = key_up_ref.shape[1] // HEAD_SIZE
    group_size = QUERY_HEADS // heads_kv
    rows = group_size * draft_count
    scale = math.log2(math.e) / math.sqrt(HEAD_SIZE)
    step = 256
    copies[0].wait()
    copies[1].wait()
    for k in range(heads_kv):
        pieces = []
        for b in range(slot_count):
            for g in range(group_size):
                lane = (k * group_size + g) * HEAD_SIZE
                pieces.append(query_ref[b, :, lane : lane + HEAD_SIZE].astype(jnp.float32))
        query = jnp.concatenate(pieces, 0).astype(jnp.bfloat16)
        key_up = key_up_ref[:, k * HEAD_SIZE : (k + 1) * HEAD_SIZE]
        turned = lax.dot_general(query, key_up, NT, preferred_element_type=jnp.float32) * scale
        for b in range(slot_count):
            float_ref[b, k * rows : (k + 1) * rows, :] = turned[b * rows : (b + 1) * rows]
    copies[2].wait()
    for b in range(slot_count):
        first = pl.multiple_of(window_start(context_ref[b], arrived, window_ref.shape[1], span_rows), 128)
        window_ref[b] = cache_ref[b, pl.ds(first, window_ref.shape[1]), :]
        turned_ref[b] = split_rows(float_ref[b])
        peak = None
        for c in range(0, span_rows, step):
            scores = join_rows(
                lax.dot_general(turned_ref[b], cache_ref[b, c : c + step], NT, preferred_element_type=jnp.float32)
            )
            column = lax.broadcasted_iota(jnp.int32, (1, step), 1) + c
            scores = jnp.where(column < context_ref[b] - arrived, scores, FAR)
            scores_ref[:, c : c + step] = scores
            top = jnp.max(scores, 1, keepdims=True)
            peak = top if peak is None else jnp.maximum(peak, top)
        peak_ref[b] = peak
        total = jnp.zeros_like(peak)
        mixed = jnp.zeros(mixed_ref.shape[1:], jnp.float32)
        for c in range(0, span_rows, step):
            weights = jnp.exp2(scores_ref[:, c : c + step] - peak)
            total += jnp.sum(weights, 1, keepdims=True)
            mixed += join_rows(
                jnp.dot(split_rows(weights), cache_ref[b, c : c + step], preferred_element_type=jnp.float32)
            )
        total_ref[b] = total
        mixed_ref[b] = mixed


def window_start(context, arrived, size, span_rows):
    return jnp.clip((context - arrived) // 128 * 128, 0, span_rows - size)


def window_kernel(
    arrived, span_rows, draft_count, context_ref, limit_ref, turned_ref, peak_ref, total_ref, mixed_ref, window_ref,
    draft_latent_ref, new_peak_ref, new_total_ref, new_mixed_ref,
):
    slot_count, size, width = window_ref.shape
    rows = peak_ref.shape[1]
    drafts = draft_latent_ref[...]
    drafts = jnp.concatenate([drafts, jnp.zeros((128 - drafts.shape[0], width), jnp.float32)], 0).astype(jnp.bfloat16)
    token = lax.broadcasted_iota(jnp.int32, (rows, 1), 0) % draft_count
    spot = lax.broadcasted_iota(jnp.int32, (rows, 128), 1)
    for b in range(slot_count):
        first = window_start(context_ref[b], arrived, size, span_rows)
        scores = join_rows(lax.dot_general(turned_ref[b], window_ref[b], NT, preferred_element_type=jnp.float32))
        column = lax.broadcasted_iota(jnp.int32, (1, size), 1) + first
        seen = (column >= context_ref[b] - arrived) & (column < limit_ref[b : b + 1, 0:1])
        scores = jnp.where(seen, scores, FAR)
        draft_scores = join_rows(lax.dot_general(turned_ref[b], drafts, NT, preferred_element_type=jnp.float32))
        draft_seen = (spot >= b * draft_count) & (spot <= b * draft_count + token)
        draft_scores = jnp.where(draft_seen, draft_scores, FAR)
        peak = jnp.maximum(jnp.max(scores, 1, keepdims=True), jnp.max(draft_scores, 1, keepdims=True))
        peak = jnp.maximum(peak, peak_ref[b])
        weights, draft_weights = jnp.exp2(scores - peak), jnp.exp2(draft_scores - peak)
        fade = jnp.exp2(peak_ref[b] - peak)
        new_peak_ref[b] = peak
        total = jnp.sum(weights, 1, keepdims=True) + jnp.sum(draft_weights, 1, keepdims=True)
        new_total_ref[b] = total_ref[b] * fade + total
        mixed = jnp.dot(split_rows(weights), window_ref[b], preferred_element_type=jnp.float32)
        mixed += jnp.dot(split_rows(draft_weights), drafts, preferred_element_type=jnp.float32)
        new_mixed_ref[b] = mixed_ref[b] * fade + join_rows(mixed)


def piece_sums(starts, spans, row_refs, refs):
    total = None
    for start, (n, first, depth) in zip(starts, spans):
        lanes = pl.ds(pl.multiple_of(start, HEAD_SIZE), depth)
        rows = [ref[:, lanes] for ref in row_refs]
        piece = refs[n][first : first + depth, :]
        product = jnp.dot(jnp.concatenate(rows, 0), piece, preferred_element_type=jnp.float32)
        total = product if total is None else total + product
    return total


def down_kernel(starts_of, spans, first, *refs):
    row_refs, refs, out_ref = refs[:4], refs[4:-1], refs[-1]
    total = piece_sums(starts_of(), spans, row_refs, refs)
    out_ref[...] = total if first else total + refs[-1][...]


def down_place_kernel(starts_of, spans, *refs):
    row_refs, refs, (keep_ref, send_ref) = refs[:4], refs[4:-2], refs[-2:]
    place_ref, sum_ref, refs = refs[0], refs[1], refs[2:]
    total = piece_sums(starts_of(), spans, row_refs, refs) + sum_ref[...]
    slots, width = keep_ref.shape[0] - 8, keep_ref.shape[1]
    count = place_ref.shape[1]
    parts = []
    left = total[:count]
    for _ in range(3):
        part = left.astype(jnp.bfloat16)
        parts.append(part)
        left = left - part.astype(jnp.float32)
    parts = jnp.concatenate(parts, 1)
    core = lax.axis_index("wide") % 2
    spot = lax.broadcasted_iota(jnp.int32, (slots, count), 0)
    for ref, target, draft in ((keep_ref, core, count), (send_ref, 1 - core, count + 16)):
        chosen = jnp.where(spot + target * slots == place_ref[...], 1.0, 0.0).astype(jnp.bfloat16)
        moved = jnp.dot(chosen, parts, preferred_element_type=jnp.float32)
        ref[:slots, :] = moved[:, :width] + moved[:, width : 2 * width] + moved[:, 2 * width :]
        ref[slots:, :] = total[draft : draft + 8]


def route_kernel(keep_ref, came_ref, draft_latent_ref, stay_ref, send_ref, float_ref):
    float_ref[...] = keep_ref[...] + came_ref[...]
    slots = float_ref.shape[0] - 8
    draft_latent_ref[...] = float_ref[slots:, :].astype(jnp.bfloat16).astype(jnp.float32)
    size = slots // 8
    wide = lax.axis_index("wide")
    z, y = wide // 4, wide // 2 % 2
    for other, ref in ((0, stay_ref), (1, send_ref)):
        for n, (high, low) in enumerate(((0, 0), (0, 1), (1, 0), (1, 1))):
            there = (z // 2 + high) % 2 * 2 + (z + low) % 2
            block = there * 2 + (y + other) % 2
            rows = pl.ds(pl.multiple_of(block * size, size), size)
            ref[n * size : (n + 1) * size, :] = float_ref[rows, :].astype(jnp.bfloat16)


def mix_kernel(outer, keep_ref, came_ref, stay_ref, send_ref):
    half = keep_ref.shape[0] // 2
    size = half // outer
    for ref, first in ((stay_ref, 0), (send_ref, half)):
        for n in range(outer):
            for m, source in enumerate((keep_ref, came_ref)):
                spot = (n * 2 + m) * size
                ref[spot : spot + size, :] = source[first + n * size : first + (n + 1) * size, :]


def start_kernel(target_hbm, shard_hbm, draft_hbm, half_ref, full_ref, rows_ref, target_ref, draft_ref, sems):
    half_rows, shard_rows = half_ref.shape[0] - 16, full_ref.shape[0] - 16
    mine = pl.ds(pl.multiple_of(lax.axis_index("rep") * half_rows, half_rows), half_rows)
    copies = [
        pltpu.make_async_copy(target_hbm, target_ref, sems.at[0]),
        pltpu.make_async_copy(shard_hbm.at[mine], half_ref.at[:half_rows], sems.at[1]),
        pltpu.make_async_copy(shard_hbm, full_ref.at[:shard_rows], sems.at[2]),
        pltpu.make_async_copy(draft_hbm, draft_ref, sems.at[3]),
    ]
    for copy in copies:
        copy.start()
    width, count = half_ref.shape[1], target_ref.shape[1]
    copies[0].wait()
    hit = lax.broadcasted_iota(jnp.int32, (width, count), 0) == target_ref[...]
    hit = jnp.where(hit, 1.0, 0.0).astype(jnp.bfloat16)
    block = lax.dot_general(jnp.ones((16, count), jnp.bfloat16), hit, NT, preferred_element_type=jnp.float32)
    half_ref[half_rows:, :] = block.astype(jnp.bfloat16)
    full_ref[shard_rows:, :] = block.astype(jnp.bfloat16)
    copies[3].wait()
    rows = [draft_ref[b].astype(jnp.float32) for b in range(draft_ref.shape[0])]
    target = jnp.broadcast_to(target_ref[...].astype(jnp.float32), (8, count))
    rows.append(jnp.concatenate([target, jnp.zeros((8, rows_ref.shape[1] - count), jnp.float32)], 1))
    rows_ref[...] = jnp.concatenate(rows, 0).astype(jnp.bfloat16)
    for copy in copies[1:3]:
        copy.wait()


def join_kernel(one_ref, two_ref, *refs):
    rows, (out_ref, bare_ref) = one_ref.shape[0], refs[-2:]
    out_ref[:rows, :] = one_ref[...]
    out_ref[rows:, :] = two_ref[...]
    bare_ref[: rows - 16, :] = one_ref[: rows - 16, :]
    bare_ref[rows - 16 :, :] = two_ref[: rows - 16, :]


def append_kernel(one_ref, two_ref, out_ref):
    rows = one_ref.shape[0]
    out_ref[:rows, :] = one_ref[...]
    out_ref[rows:, :] = two_ref[...]


def copy_kernel(spans, one_ref, *refs):
    done = 0
    for first, count in spans:
        refs[-1][done : done + count, :] = one_ref[first : first + count, :]
        done += count


def other_half_kernel(shard_ref, out_ref):
    rows = out_ref.shape[0]
    first = pl.multiple_of((1 - lax.axis_index("rep")) * rows, rows)
    out_ref[...] = shard_ref[pl.ds(first, rows), :]


def pack_kernel(spans, *refs):
    out_ref, width = refs[-1], refs[0].shape[1]
    for m, (n, first) in enumerate(spans):
        out_ref[:, m * width : (m + 1) * width] = refs[n][first : first + 16, :]


def count_kernel(most_rows, context_ref, mine_ref, other_ref, limit_ref, column_slot_ref):
    f32 = jnp.float32
    width = mine_ref.shape[1] // 8
    wide = lax.axis_index("wide")
    core = wide % 2
    mine, other = mine_ref[...].astype(f32), other_ref[...].astype(f32)
    low = jnp.where(core == 0, mine[:1], other[:1])
    high = jnp.where(core == 0, other[:1], mine[:1])
    counts = []
    for n in range(8):
        counts += [low[:, n * width : (n + 1) * width], high[:, n * width : (n + 1) * width]]
    counts = jnp.concatenate(counts, 0)
    lane = lax.broadcasted_iota(jnp.int32, counts.shape, 1)
    row = lax.broadcasted_iota(jnp.int32, counts.shape, 0)
    spread = []
    for b in range(2):
        number = jnp.sum(jnp.where(lane == wide * 2 + b, counts, 0.0), 1, keepdims=True)
        limit = context_ref[b] - jnp.sum(number, 0, keepdims=True).astype(jnp.int32)
        limit_ref[b : b + 1, :] = jnp.broadcast_to(limit, (1, limit_ref.shape[1]))
        spread.append(jnp.sum(jnp.where(lane // most_rows == row, number, 0.0), 0, keepdims=True).astype(jnp.int32))
    spot = lax.broadcasted_iota(jnp.int32, column_slot_ref.shape, 1) % most_rows
    column_slot_ref[...] = jnp.where(spot < spread[0], 0, jnp.where(spot >= most_rows - spread[1], 1, -1))


def place_kernel(most_rows, mine_ref, other_ref, place_ref):
    f32, bf16 = jnp.float32, jnp.bfloat16
    count = place_ref.shape[1] // 2
    core = lax.axis_index("wide") % 2
    earlier = lax.broadcasted_iota(jnp.int32, (count, count), 0) < lax.broadcasted_iota(jnp.int32, (count, count), 1)
    earlier = jnp.where(earlier, 1.0, 0.0).astype(bf16)
    for n, (ref, owner) in enumerate(((mine_ref, core), (other_ref, 1 - core))):
        target = ref[:, :count].astype(f32)[8:9].astype(jnp.int32)
        hit = jnp.where(lax.broadcasted_iota(jnp.int32, (64, count), 0) == target, 1.0, 0.0)
        before = jnp.dot(hit.astype(bf16), earlier, preferred_element_type=f32)
        rank = jnp.sum(hit * before, 0, keepdims=True).astype(jnp.int32)
        spot = jnp.where(target % 2 == 0, rank, most_rows - 1 - rank)
        chip, side = target // 4, target // 2 % 2
        place_ref[:, n * count : (n + 1) * count] = side * 2 * count + (chip * 2 + owner) * most_rows + spot


def plain_down_kernel(place_ref, prompt_ref, draft_ref, weight_ref, outgoing_ref, draft_latent_ref):
    count = prompt_ref.shape[0]
    rows = jnp.concatenate([prompt_ref[...], draft_ref[...]], 0)
    total = jnp.dot(rows, weight_ref[...], preferred_element_type=jnp.float32)
    draft_latent_ref[...] = total[count : count + 8].astype(jnp.bfloat16).astype(jnp.float32)
    spot = lax.broadcasted_iota(jnp.int32, (outgoing_ref.shape[0], count), 0)
    chosen = jnp.where(spot == place_ref[...], 1.0, 0.0).astype(jnp.bfloat16)
    latent = total[:count].astype(jnp.bfloat16)
    outgoing_ref[...] = jnp.dot(chosen, latent, preferred_element_type=jnp.float32).astype(jnp.bfloat16)


def late_kernel(column_slot_ref, turned_ref, peak_ref, total_ref, mixed_ref, value_up_ref, *refs):
    incoming_refs, (out_ref, rows_ref, parted_ref) = refs[:-3], refs[-3:]
    slot_count, draft_count, _ = out_ref.shape
    heads_kv = value_up_ref.shape[1] // HEAD_SIZE
    group_size = QUERY_HEADS // heads_kv
    head_rows = group_size * draft_count
    rows = peak_ref.shape[1]
    block = incoming_refs[0].shape[0]
    for n, ref in enumerate(incoming_refs):
        rows_ref[n * block : (n + 1) * block, :] = ref[...]
    for b in range(slot_count):
        scores = join_rows(lax.dot_general(turned_ref[b], rows_ref[...], NT, preferred_element_type=jnp.float32))
        scores = jnp.where(column_slot_ref[...] == b, scores, FAR)
        peak = jnp.maximum(jnp.max(scores, 1, keepdims=True), peak_ref[b])
        weights = jnp.exp2(scores - peak)
        fade = jnp.exp2(peak_ref[b] - peak)
        total = total_ref[b] * fade + jnp.sum(weights, 1, keepdims=True)
        mixed = join_rows(jnp.dot(split_rows(weights), rows_ref[...], preferred_element_type=jnp.float32))
        parted_ref[b] = split_rows((mixed_ref[b] * fade + mixed) / total)
    for k in range(heads_kv):
        part = []
        for b in range(slot_count):
            part.append(parted_ref[b, k * head_rows : (k + 1) * head_rows, :])
            part.append(parted_ref[b, rows + k * head_rows : rows + (k + 1) * head_rows, :])
        value_up = value_up_ref[:, k * HEAD_SIZE : (k + 1) * HEAD_SIZE]
        both = jnp.dot(jnp.concatenate(part, 0), value_up, preferred_element_type=jnp.float32)
        for b in range(slot_count):
            result = join_rows(both[b * 2 * head_rows : (b + 1) * 2 * head_rows])
            wide = jnp.concatenate(
                [result[g * draft_count : (g + 1) * draft_count] for g in range(group_size)], 1
            )
            out_ref[b, :, k * group_size * HEAD_SIZE : (k + 1) * group_size * HEAD_SIZE] = wide.astype(jnp.bfloat16)


def deliver(prompt_hidden, draft_hidden, shard, row_target, context_len, held):
    shard_rows, width = shard.shape
    count = prompt_hidden.shape[0]
    spots = [(r, z, y, c) for r in range(2) for z in range(4) for y in range(2) for c in range(2)]
    most_rows = count // 8
    f32, bf16 = jnp.float32, jnp.bfloat16

    def flat(spot):
        return ((spot[0] * 4 + spot[1]) * 2 + spot[2]) * 2 + spot[3]

    def swap(x, r=0, z=0, y=0, c=0):
        pairs = [(flat(spot), flat([a ^ b for a, b in zip(spot, (r, z, y, c))])) for spot in spots]
        return lax.ppermute(x, ("rep", "wide"), pairs)

    def array(rows, dtype=bf16):
        return jax.ShapeDtypeStruct((rows, width), dtype)

    def call(kernel, out_shape, name, *operands, specs=None, flops=2**20, **more):
        return pl.pallas_call(
            kernel,
            out_shape=out_shape,
            in_specs=specs or [WHOLE] * len(operands),
            out_specs=[WHOLE] * len(out_shape) if isinstance(out_shape, list) else WHOLE,
            compiler_params=params(16),
            cost_estimate=pl.CostEstimate(flops=flops, bytes_accessed=2**16, transcendentals=0),
            name=name,
            **more,
        )(*operands)

    hbm = pl.BlockSpec(memory_space=pltpu.HBM)
    half_rows = shard_rows // 2
    ext = half_rows + 16
    half, full, draft_rows = call(
        start_kernel,
        [
            array(ext),
            array(shard_rows + 16),
            jax.ShapeDtypeStruct((16, draft_hidden.shape[2]), bf16),
        ],
        "start_rows",
        *(pltpu.with_memory_space_constraint(x, pltpu.HBM) for x in (row_target.reshape(1, count), shard, draft_hidden)),
        specs=[hbm] * 3,
        scratch_shapes=[
            pltpu.VMEM((1, count), jnp.int32), pltpu.VMEM(draft_hidden.shape, bf16), pltpu.SemaphoreType.DMA((4,))
        ],
    )
    za, zb = swap(half, z=1), swap(half, z=2)
    y0 = swap(full, y=1)
    other_prompt, other_drafts = swap(prompt_hidden, c=1), swap(draft_rows, c=1)

    def copy(x, spans, *ties):
        return call(
            functools.partial(copy_kernel, spans), array(sum(rows for _, rows in spans)), "copy_piece", x, *ties,
            specs=[WHOLE] + [UNREAD] * len(ties),
        )

    rest = call(other_half_kernel, array(half_rows), "other_half", y0)
    db = swap(rest, z=2)
    zab, bare = call(
        join_kernel, [array(2 * ext), array(2 * half_rows)], "join_pieces", za, zb, other_drafts, held,
        specs=[WHOLE] * 2 + [UNREAD] * 2,
    )
    yab, xab = swap(zab, y=1), swap(bare, r=1)
    zc_da = swap(call(append_kernel, array(ext + half_rows), "append_piece", zb, rest), z=1)
    dc = swap(db, z=1)
    xc = swap(copy(zc_da, [(0, half_rows)]), r=1)
    yc = swap(copy(zc_da, [(0, ext)], yab), y=1)

    order = [
        (half, half_rows), (y0, shard_rows), (zab, ext + half_rows), (yab, ext + half_rows),
        (zab, half_rows), (yab, half_rows), (zc_da, half_rows), (yc, half_rows),
    ]
    pack = call(
        functools.partial(pack_kernel, [(n, first) for n, (_, first) in enumerate(order)]),
        jax.ShapeDtypeStruct((16, len(order) * width), bf16), "pack_rows", *(x for x, _ in order),
    )
    other_pack = swap(pack, c=1)
    limit, column_slot = call(
        functools.partial(count_kernel, most_rows),
        [jax.ShapeDtypeStruct((2, 128), jnp.int32), jax.ShapeDtypeStruct((1, 2 * count), jnp.int32)],
        "count_rows", context_len, pack, other_pack,
        specs=[SCALARS, WHOLE, WHOLE],
    )
    place = call(
        functools.partial(place_kernel, most_rows), jax.ShapeDtypeStruct((1, 2 * count), jnp.int32), "place_rows",
        draft_rows, other_drafts,
    )

    def starts_of(uses):
        def starts():
            rep, wide = lax.axis_index("rep"), lax.axis_index("wide")
            z, y, c = wide // 4, wide // 2 % 2, wide % 2
            found = []
            for _, _, _, (x_step, z_step, y_step), *further in uses:
                owner_z = (z // 2 + z_step // 2) % 2 * 2 + (z + z_step) % 2
                owner = (owner_z * 2 + (y + y_step) % 2) * 2 + c
                start = owner * shard_rows + (0 if x_step is None else (rep + x_step) % 2 * half_rows)
                found.append(start + sum(further))
            return found

        return starts

    rows = [prompt_hidden, other_prompt, draft_rows, other_drafts]
    stages = [
        ([full, y0], [(0, 0, shard_rows, (None, 0, 0)), (1, 0, shard_rows, (None, 0, 1))]),
        (
            [zab, yab],
            [(0, 0, half_rows, (0, 1, 0)), (0, ext, half_rows, (0, 2, 0)),
             (1, 0, half_rows, (0, 1, 1)), (1, ext, half_rows, (0, 2, 1))],
        ),
        (
            [xab, zc_da],
            [(0, 0, half_rows, (1, 1, 0)), (0, half_rows, half_rows, (1, 2, 0)),
             (1, 0, half_rows, (0, 3, 0)), (1, ext, half_rows, (1, 1, 1))],
        ),
        (
            [xc, yc, db, dc],
            [(0, 0, half_rows, (1, 3, 0)), (1, 0, half_rows, (0, 3, 1)),
             (2, 0, half_rows, (1, 2, 1)), (3, 0, half_rows, (1, 3, 1))],
        ),
    ]
    sums = []
    total_rows = 2 * count + 32
    for n, (pieces, uses) in enumerate(stages[:-1]):
        sums = [
            call(
                functools.partial(down_kernel, starts_of(uses), [use[:3] for use in uses], n == 0),
                array(total_rows, f32), "down_rows", *rows, *pieces, *sums, flops=2**26,
            )
        ]

    def finish():
        pieces, uses = stages[-1]
        keep, send = call(
            functools.partial(down_place_kernel, starts_of(uses), [use[:3] for use in uses]),
            [array(2 * count + 8, f32)] * 2, "down_place_rows", *rows, place, *sums, *pieces, flops=2**26,
        )
        came = swap(send, c=1)
        block = array(count)
        draft_latent, stay, send = call(
            route_kernel, [array(8, f32), block, block], "route_rows", keep, came,
            scratch_shapes=[pltpu.VMEM((2 * count + 8, width), f32)],
        )
        came = swap(send, y=1)
        stay, send = call(functools.partial(mix_kernel, 2), [block, block], "mix_rows", stay, came)
        came = swap(send, z=2)
        stay, send = call(functools.partial(mix_kernel, 1), [block, block], "mix_rows", stay, came)
        return draft_latent, [stay, swap(send, z=1)]

    return limit, column_slot, finish


def deliver_plain(prompt_hidden, draft_hidden, shard, row_target, context_len, held):
    wide_size = lax.axis_size("wide")
    row_count = prompt_hidden.shape[0]
    slot_count, draft_count, _ = draft_hidden.shape
    latent_width = shard.shape[1]
    most_rows = 2 * ((row_count + wide_size - 1) // wide_size)
    arrived = wide_size * most_rows
    weight = lax.all_gather(shard, "wide", axis=0, tiled=True)
    index = jnp.arange(row_count, dtype=jnp.int32)
    same = (row_target[:, None] == row_target[None, :]) & (index[None, :] < index[:, None])
    rank = jnp.sum(same.astype(jnp.int32), 1)
    front = row_target % slot_count == 0
    place = row_target // slot_count * most_rows + jnp.where(front, rank, most_rows - 1 - rank)
    request = jnp.arange(wide_size * slot_count, dtype=jnp.int32)
    counts = jnp.sum((row_target[None, :] == request[:, None]).astype(jnp.int32), 1)
    counts = lax.all_to_all(counts.reshape(wide_size, slot_count), "wide", split_axis=0, concat_axis=0, tiled=True)
    limit = jnp.broadcast_to((context_len - jnp.sum(counts, 0))[:, None], (slot_count, 128))
    spot = jnp.arange(most_rows, dtype=jnp.int32)[None, :]
    column_slot = jnp.where(
        spot < counts[:, 0:1], 0, jnp.where(spot >= most_rows - counts[:, 1:2], 1, -1)
    ).reshape(1, arrived)

    tile = slot_count * draft_count
    draft_flat = jnp.pad(draft_hidden.reshape(tile, draft_hidden.shape[2]), ((0, 16 - tile), (0, 0)))

    def finish():
        outgoing, draft_latent = pl.pallas_call(
            plain_down_kernel,
            out_shape=[
                jax.ShapeDtypeStruct((arrived, latent_width), jnp.bfloat16),
                jax.ShapeDtypeStruct((slot_count * draft_count, latent_width), jnp.float32),
            ],
            in_specs=[WHOLE] * 4,
            out_specs=[WHOLE] * 2,
            compiler_params=params(24),
            name="down_rows",
        )(place.reshape(1, row_count), prompt_hidden, draft_flat, weight)
        incoming = lax.all_to_all(
            outgoing.reshape(wide_size, most_rows, latent_width), "wide", split_axis=0, concat_axis=0, tiled=True
        )
        return draft_latent, [incoming.reshape(arrived, latent_width)]

    return limit, column_slot, finish


def local(
    prompt_hidden,
    resident_latent,
    row_target,
    row_offset,
    context_len,
    draft_hidden,
    draft_query_heads,
    down_weight,
    key_up_weight,
    value_up_weight,
):
    f32, bf16 = jnp.float32, jnp.bfloat16
    slot_count, span_rows, latent_width = resident_latent.shape
    draft_count = draft_hidden.shape[1]
    rows = QUERY_HEADS * draft_count
    wide_size, row_count = lax.axis_size("wide"), prompt_hidden.shape[0]
    arrived = 2 * ((row_count + wide_size - 1) // wide_size) * wide_size
    window = min(arrived + 128, span_rows)
    hbm = pl.BlockSpec(memory_space=pltpu.HBM)
    stats = [
        jax.ShapeDtypeStruct((slot_count, rows, 1), f32),
        jax.ShapeDtypeStruct((slot_count, rows, 1), f32),
        jax.ShapeDtypeStruct((slot_count, rows, latent_width), f32),
    ]
    turned, peak, total, mixed, edge = pl.pallas_call(
        functools.partial(held_kernel, arrived),
        out_shape=[
            jax.ShapeDtypeStruct((slot_count, 2 * rows, latent_width), bf16),
            *stats,
            jax.ShapeDtypeStruct((slot_count, window, latent_width), bf16),
        ],
        in_specs=[SCALARS, hbm, hbm, hbm],
        out_specs=[WHOLE] * 5,
        scratch_shapes=[
            pltpu.VMEM(draft_query_heads.shape, bf16),
            pltpu.VMEM(key_up_weight.shape, bf16),
            pltpu.VMEM(resident_latent.shape, bf16),
            pltpu.VMEM((slot_count, rows, latent_width), f32),
            pltpu.VMEM((rows, span_rows), f32),
            pltpu.SemaphoreType.DMA((3,)),
        ],
        compiler_params=params(16),
        cost_estimate=pl.CostEstimate(flops=2**31, bytes_accessed=2**21, transcendentals=0),
        name="held_rows",
    )(context_len, *(pltpu.with_memory_space_constraint(x, pltpu.HBM) for x in (draft_query_heads, key_up_weight, resident_latent)))
    known = wide_size == 16 and lax.axis_size("rep") == 2
    limit, column_slot, finish = (deliver if known else deliver_plain)(
        prompt_hidden, draft_hidden, down_weight, row_target, context_len, peak
    )
    draft_latent, incoming = finish()
    peak, total, mixed = pl.pallas_call(
        functools.partial(window_kernel, arrived, span_rows, draft_count),
        out_shape=stats,
        in_specs=[SCALARS] + [WHOLE] * 7,
        out_specs=[WHOLE] * 3,
        compiler_params=params(16),
        cost_estimate=pl.CostEstimate(flops=2**30, bytes_accessed=2**16, transcendentals=0),
        name="window_rows",
    )(context_len, limit, turned, peak, total, mixed, edge, draft_latent)
    return pl.pallas_call(
        late_kernel,
        out_shape=jax.ShapeDtypeStruct((slot_count, draft_count, QUERY_HEADS * HEAD_SIZE), bf16),
        in_specs=[WHOLE] * (6 + len(incoming)),
        out_specs=WHOLE,
        scratch_shapes=[
            pltpu.VMEM((arrived, latent_width), bf16),
            pltpu.VMEM((slot_count, 2 * rows, latent_width), bf16),
        ],
        compiler_params=params(16),
        name="late_rows",
    )(column_slot, turned, peak, total, mixed, value_up_weight, *incoming)


def solution(mesh):
    placed = (
        P(("rep", "wide"), None),
        P(("rep", "wide"), None, None),
        P(("rep", "wide")),
        P(("rep", "wide")),
        P(("rep", "wide")),
        P(("rep", "wide"), None, None),
        P(("rep", "wide"), None, None),
        P("wide", None),
        P(),
        P(),
    )
    return jax.shard_map(
        local, mesh=mesh, in_specs=placed, out_specs=P(("rep", "wide"), None, None), check_vma=False
    )
```

```python
import functools
import math

import jax
import jax.numpy as jnp
from jax import lax
from jax.experimental import pallas as pl
from jax.experimental.pallas import tpu as pltpu
from jax.sharding import PartitionSpec as P

QUERY_HEADS = 64
HEAD_SIZE = 128
FAR = -1e30
NT = (((1,), (1,)), ((), ()))
WHOLE = pl.BlockSpec(memory_space=pltpu.VMEM)
SCALARS = pl.BlockSpec(memory_space=pltpu.SMEM)
UNREAD = pl.BlockSpec(memory_space=pl.ANY)


def params(mib):
    return pltpu.CompilerParams(vmem_limit_bytes=mib * 1024 * 1024)


def split_rows(x):
    top = x.astype(jnp.bfloat16)
    rest = (x - top.astype(jnp.float32)).astype(jnp.bfloat16)
    return jnp.concatenate([top, rest], 0)


def join_rows(x):
    half = x.shape[0] // 2
    return x[:half] + x[half:]


def held_kernel(
    arrived, context_ref, query_hbm, key_up_hbm, cache_hbm, turned_ref, peak_ref, total_ref, mixed_ref, window_ref,
    query_ref, key_up_ref, cache_ref, float_ref, scores_ref, sems,
):
    copies = [
        pltpu.make_async_copy(source, target, sems.at[n])
        for n, (source, target) in enumerate(
            [(query_hbm, query_ref), (key_up_hbm, key_up_ref), (cache_hbm, cache_ref)]
        )
    ]
    for copy in copies:
        copy.start()
    slot_count, span_rows, _ = cache_ref.shape
    draft_count = query_ref.shape[1]
    heads_kv = key_up_ref.shape[1] // HEAD_SIZE
    group_size = QUERY_HEADS // heads_kv
    rows = group_size * draft_count
    scale = math.log2(math.e) / math.sqrt(HEAD_SIZE)
    step = 256
    copies[0].wait()
    copies[1].wait()
    for k in range(heads_kv):
        pieces = []
        for b in range(slot_count):
            for g in range(group_size):
                lane = (k * group_size + g) * HEAD_SIZE
                pieces.append(query_ref[b, :, lane : lane + HEAD_SIZE].astype(jnp.float32))
        query = jnp.concatenate(pieces, 0).astype(jnp.bfloat16)
        key_up = key_up_ref[:, k * HEAD_SIZE : (k + 1) * HEAD_SIZE]
        turned = lax.dot_general(query, key_up, NT, preferred_element_type=jnp.float32) * scale
        for b in range(slot_count):
            float_ref[b, k * rows : (k + 1) * rows, :] = turned[b * rows : (b + 1) * rows]
    copies[2].wait()
    for b in range(slot_count):
        first = pl.multiple_of(window_start(context_ref[b], arrived, window_ref.shape[1], span_rows), 128)
        window_ref[b] = cache_ref[b, pl.ds(first, window_ref.shape[1]), :]
        turned_ref[b] = split_rows(float_ref[b])
        peak = None
        for c in range(0, span_rows, step):
            scores = join_rows(
                lax.dot_general(turned_ref[b], cache_ref[b, c : c + step], NT, preferred_element_type=jnp.float32)
            )
            column = lax.broadcasted_iota(jnp.int32, (1, step), 1) + c
            scores = jnp.where(column < context_ref[b] - arrived, scores, FAR)
            scores_ref[:, c : c + step] = scores
            top = jnp.max(scores, 1, keepdims=True)
            peak = top if peak is None else jnp.maximum(peak, top)
        peak_ref[b] = peak
        total = jnp.zeros_like(peak)
        mixed = jnp.zeros(mixed_ref.shape[1:], jnp.float32)
        for c in range(0, span_rows, step):
            weights = jnp.exp2(scores_ref[:, c : c + step] - peak)
            total += jnp.sum(weights, 1, keepdims=True)
            mixed += join_rows(
                jnp.dot(split_rows(weights), cache_ref[b, c : c + step], preferred_element_type=jnp.float32)
            )
        total_ref[b] = total
        mixed_ref[b] = mixed


def window_start(context, arrived, size, span_rows):
    return jnp.clip((context - arrived) // 128 * 128, 0, span_rows - size)


def window_kernel(
    arrived, span_rows, draft_count, context_ref, limit_ref, turned_ref, peak_ref, total_ref, mixed_ref, window_ref,
    draft_latent_ref, new_peak_ref, new_total_ref, new_mixed_ref,
):
    slot_count, size, width = window_ref.shape
    rows = peak_ref.shape[1]
    drafts = draft_latent_ref[...]
    drafts = jnp.concatenate([drafts, jnp.zeros((128 - drafts.shape[0], width), jnp.float32)], 0).astype(jnp.bfloat16)
    token = lax.broadcasted_iota(jnp.int32, (rows, 1), 0) % draft_count
    spot = lax.broadcasted_iota(jnp.int32, (rows, 128), 1)
    for b in range(slot_count):
        first = window_start(context_ref[b], arrived, size, span_rows)
        scores = join_rows(lax.dot_general(turned_ref[b], window_ref[b], NT, preferred_element_type=jnp.float32))
        column = lax.broadcasted_iota(jnp.int32, (1, size), 1) + first
        seen = (column >= context_ref[b] - arrived) & (column < limit_ref[b : b + 1, 0:1])
        scores = jnp.where(seen, scores, FAR)
        draft_scores = join_rows(lax.dot_general(turned_ref[b], drafts, NT, preferred_element_type=jnp.float32))
        draft_seen = (spot >= b * draft_count) & (spot <= b * draft_count + token)
        draft_scores = jnp.where(draft_seen, draft_scores, FAR)
        peak = jnp.maximum(jnp.max(scores, 1, keepdims=True), jnp.max(draft_scores, 1, keepdims=True))
        peak = jnp.maximum(peak, peak_ref[b])
        weights, draft_weights = jnp.exp2(scores - peak), jnp.exp2(draft_scores - peak)
        fade = jnp.exp2(peak_ref[b] - peak)
        new_peak_ref[b] = peak
        total = jnp.sum(weights, 1, keepdims=True) + jnp.sum(draft_weights, 1, keepdims=True)
        new_total_ref[b] = total_ref[b] * fade + total
        mixed = jnp.dot(split_rows(weights), window_ref[b], preferred_element_type=jnp.float32)
        mixed += jnp.dot(split_rows(draft_weights), drafts, preferred_element_type=jnp.float32)
        new_mixed_ref[b] = mixed_ref[b] * fade + join_rows(mixed)


def piece_sums(starts, spans, row_refs, refs):
    total = None
    for start, (n, first, depth) in zip(starts, spans):
        lanes = pl.ds(pl.multiple_of(start, HEAD_SIZE), depth)
        rows = [ref[:, lanes] for ref in row_refs]
        piece = refs[n][first : first + depth, :]
        product = jnp.dot(jnp.concatenate(rows, 0), piece, preferred_element_type=jnp.float32)
        total = product if total is None else total + product
    return total


def down_kernel(starts_of, spans, first, *refs):
    row_refs, refs, out_ref = refs[:4], refs[4:-1], refs[-1]
    total = piece_sums(starts_of(), spans, row_refs, refs)
    out_ref[...] = total if first else total + refs[-1][...]


def down_place_kernel(starts_of, spans, *refs):
    row_refs, refs, (keep_ref, send_ref) = refs[:4], refs[4:-2], refs[-2:]
    place_ref, sum_ref, refs = refs[0], refs[1], refs[2:]
    total = piece_sums(starts_of(), spans, row_refs, refs) + sum_ref[...]
    slots, width = keep_ref.shape[0] - 8, keep_ref.shape[1]
    count = place_ref.shape[1]
    parts = []
    left = total[:count]
    for _ in range(3):
        part = left.astype(jnp.bfloat16)
        parts.append(part)
        left = left - part.astype(jnp.float32)
    parts = jnp.concatenate(parts, 1)
    core = lax.axis_index("wide") % 2
    spot = lax.broadcasted_iota(jnp.int32, (slots, count), 0)
    for ref, target, draft in ((keep_ref, core, count), (send_ref, 1 - core, count + 16)):
        chosen = jnp.where(spot + target * slots == place_ref[...], 1.0, 0.0).astype(jnp.bfloat16)
        moved = jnp.dot(chosen, parts, preferred_element_type=jnp.float32)
        ref[:slots, :] = moved[:, :width] + moved[:, width : 2 * width] + moved[:, 2 * width :]
        ref[slots:, :] = total[draft : draft + 8]


def route_kernel(keep_ref, came_ref, draft_latent_ref, stay_ref, send_ref, float_ref):
    float_ref[...] = keep_ref[...] + came_ref[...]
    slots = float_ref.shape[0] - 8
    draft_latent_ref[...] = float_ref[slots:, :].astype(jnp.bfloat16).astype(jnp.float32)
    size = slots // 8
    wide = lax.axis_index("wide")
    z, y = wide // 4, wide // 2 % 2
    for other, ref in ((0, stay_ref), (1, send_ref)):
        for n, (high, low) in enumerate(((0, 0), (0, 1), (1, 0), (1, 1))):
            there = (z // 2 + high) % 2 * 2 + (z + low) % 2
            block = there * 2 + (y + other) % 2
            rows = pl.ds(pl.multiple_of(block * size, size), size)
            ref[n * size : (n + 1) * size, :] = float_ref[rows, :].astype(jnp.bfloat16)


def mix_kernel(outer, keep_ref, came_ref, stay_ref, send_ref):
    half = keep_ref.shape[0] // 2
    size = half // outer
    for ref, first in ((stay_ref, 0), (send_ref, half)):
        for n in range(outer):
            for m, source in enumerate((keep_ref, came_ref)):
                spot = (n * 2 + m) * size
                ref[spot : spot + size, :] = source[first + n * size : first + (n + 1) * size, :]


def start_kernel(target_hbm, shard_hbm, draft_hbm, half_ref, full_ref, rows_ref, target_ref, draft_ref, sems):
    half_rows, shard_rows = half_ref.shape[0] - 16, full_ref.shape[0] - 16
    mine = pl.ds(pl.multiple_of(lax.axis_index("rep") * half_rows, half_rows), half_rows)
    copies = [
        pltpu.make_async_copy(target_hbm, target_ref, sems.at[0]),
        pltpu.make_async_copy(shard_hbm.at[mine], half_ref.at[:half_rows], sems.at[1]),
        pltpu.make_async_copy(shard_hbm, full_ref.at[:shard_rows], sems.at[2]),
        pltpu.make_async_copy(draft_hbm, draft_ref, sems.at[3]),
    ]
    for copy in copies:
        copy.start()
    width, count = half_ref.shape[1], target_ref.shape[1]
    copies[0].wait()
    hit = lax.broadcasted_iota(jnp.int32, (width, count), 0) == target_ref[...]
    hit = jnp.where(hit, 1.0, 0.0).astype(jnp.bfloat16)
    block = lax.dot_general(jnp.ones((16, count), jnp.bfloat16), hit, NT, preferred_element_type=jnp.float32)
    half_ref[half_rows:, :] = block.astype(jnp.bfloat16)
    full_ref[shard_rows:, :] = block.astype(jnp.bfloat16)
    copies[3].wait()
    rows = [draft_ref[b].astype(jnp.float32) for b in range(draft_ref.shape[0])]
    target = jnp.broadcast_to(target_ref[...].astype(jnp.float32), (8, count))
    rows.append(jnp.concatenate([target, jnp.zeros((8, rows_ref.shape[1] - count), jnp.float32)], 1))
    rows_ref[...] = jnp.concatenate(rows, 0).astype(jnp.bfloat16)
    for copy in copies[1:3]:
        copy.wait()


def join_kernel(one_ref, two_ref, *refs):
    rows, (out_ref, bare_ref) = one_ref.shape[0], refs[-2:]
    out_ref[:rows, :] = one_ref[...]
    out_ref[rows:, :] = two_ref[...]
    bare_ref[: rows - 16, :] = one_ref[: rows - 16, :]
    bare_ref[rows - 16 :, :] = two_ref[: rows - 16, :]


def copy_kernel(spans, one_ref, *refs):
    done = 0
    for first, count in spans:
        refs[-1][done : done + count, :] = one_ref[first : first + count, :]
        done += count


def other_half_kernel(shard_ref, out_ref):
    rows = out_ref.shape[0]
    first = pl.multiple_of((1 - lax.axis_index("rep")) * rows, rows)
    out_ref[...] = shard_ref[pl.ds(first, rows), :]


def pack_kernel(spans, *refs):
    out_ref, width = refs[-1], refs[0].shape[1]
    for m, (n, first) in enumerate(spans):
        out_ref[:, m * width : (m + 1) * width] = refs[n][first : first + 16, :]


def count_kernel(most_rows, context_ref, mine_ref, other_ref, limit_ref, column_slot_ref):
    f32 = jnp.float32
    width = mine_ref.shape[1] // 8
    wide = lax.axis_index("wide")
    core = wide % 2
    mine, other = mine_ref[...].astype(f32), other_ref[...].astype(f32)
    low = jnp.where(core == 0, mine[:1], other[:1])
    high = jnp.where(core == 0, other[:1], mine[:1])
    counts = []
    for n in range(8):
        counts += [low[:, n * width : (n + 1) * width], high[:, n * width : (n + 1) * width]]
    counts = jnp.concatenate(counts, 0)
    lane = lax.broadcasted_iota(jnp.int32, counts.shape, 1)
    row = lax.broadcasted_iota(jnp.int32, counts.shape, 0)
    spread = []
    for b in range(2):
        number = jnp.sum(jnp.where(lane == wide * 2 + b, counts, 0.0), 1, keepdims=True)
        limit = context_ref[b] - jnp.sum(number, 0, keepdims=True).astype(jnp.int32)
        limit_ref[b : b + 1, :] = jnp.broadcast_to(limit, (1, limit_ref.shape[1]))
        spread.append(jnp.sum(jnp.where(lane // most_rows == row, number, 0.0), 0, keepdims=True).astype(jnp.int32))
    spot = lax.broadcasted_iota(jnp.int32, column_slot_ref.shape, 1) % most_rows
    column_slot_ref[...] = jnp.where(spot < spread[0], 0, jnp.where(spot >= most_rows - spread[1], 1, -1))


def place_kernel(most_rows, mine_ref, other_ref, place_ref):
    f32, bf16 = jnp.float32, jnp.bfloat16
    count = place_ref.shape[1] // 2
    core = lax.axis_index("wide") % 2
    earlier = lax.broadcasted_iota(jnp.int32, (count, count), 0) < lax.broadcasted_iota(jnp.int32, (count, count), 1)
    earlier = jnp.where(earlier, 1.0, 0.0).astype(bf16)
    for n, (ref, owner) in enumerate(((mine_ref, core), (other_ref, 1 - core))):
        target = ref[:, :count].astype(f32)[8:9].astype(jnp.int32)
        hit = jnp.where(lax.broadcasted_iota(jnp.int32, (64, count), 0) == target, 1.0, 0.0)
        before = jnp.dot(hit.astype(bf16), earlier, preferred_element_type=f32)
        rank = jnp.sum(hit * before, 0, keepdims=True).astype(jnp.int32)
        spot = jnp.where(target % 2 == 0, rank, most_rows - 1 - rank)
        chip, side = target // 4, target // 2 % 2
        place_ref[:, n * count : (n + 1) * count] = side * 2 * count + (chip * 2 + owner) * most_rows + spot


def plain_down_kernel(place_ref, prompt_ref, draft_ref, weight_ref, outgoing_ref, draft_latent_ref):
    count = prompt_ref.shape[0]
    rows = jnp.concatenate([prompt_ref[...], draft_ref[...]], 0)
    total = jnp.dot(rows, weight_ref[...], preferred_element_type=jnp.float32)
    draft_latent_ref[...] = total[count : count + 8].astype(jnp.bfloat16).astype(jnp.float32)
    spot = lax.broadcasted_iota(jnp.int32, (outgoing_ref.shape[0], count), 0)
    chosen = jnp.where(spot == place_ref[...], 1.0, 0.0).astype(jnp.bfloat16)
    latent = total[:count].astype(jnp.bfloat16)
    outgoing_ref[...] = jnp.dot(chosen, latent, preferred_element_type=jnp.float32).astype(jnp.bfloat16)


def late_kernel(column_slot_ref, turned_ref, peak_ref, total_ref, mixed_ref, value_up_ref, *refs):
    incoming_refs, (out_ref, rows_ref, parted_ref) = refs[:-3], refs[-3:]
    slot_count, draft_count, _ = out_ref.shape
    heads_kv = value_up_ref.shape[1] // HEAD_SIZE
    group_size = QUERY_HEADS // heads_kv
    head_rows = group_size * draft_count
    rows = peak_ref.shape[1]
    block = incoming_refs[0].shape[0]
    for n, ref in enumerate(incoming_refs):
        rows_ref[n * block : (n + 1) * block, :] = ref[...]
    for b in range(slot_count):
        scores = join_rows(lax.dot_general(turned_ref[b], rows_ref[...], NT, preferred_element_type=jnp.float32))
        scores = jnp.where(column_slot_ref[...] == b, scores, FAR)
        peak = jnp.maximum(jnp.max(scores, 1, keepdims=True), peak_ref[b])
        weights = jnp.exp2(scores - peak)
        fade = jnp.exp2(peak_ref[b] - peak)
        total = total_ref[b] * fade + jnp.sum(weights, 1, keepdims=True)
        mixed = join_rows(jnp.dot(split_rows(weights), rows_ref[...], preferred_element_type=jnp.float32))
        parted_ref[b] = split_rows((mixed_ref[b] * fade + mixed) / total)
    for k in range(heads_kv):
        part = []
        for b in range(slot_count):
            part.append(parted_ref[b, k * head_rows : (k + 1) * head_rows, :])
            part.append(parted_ref[b, rows + k * head_rows : rows + (k + 1) * head_rows, :])
        value_up = value_up_ref[:, k * HEAD_SIZE : (k + 1) * HEAD_SIZE]
        both = jnp.dot(jnp.concatenate(part, 0), value_up, preferred_element_type=jnp.float32)
        for b in range(slot_count):
            result = join_rows(both[b * 2 * head_rows : (b + 1) * 2 * head_rows])
            wide = jnp.concatenate(
                [result[g * draft_count : (g + 1) * draft_count] for g in range(group_size)], 1
            )
            out_ref[b, :, k * group_size * HEAD_SIZE : (k + 1) * group_size * HEAD_SIZE] = wide.astype(jnp.bfloat16)


def deliver(prompt_hidden, draft_hidden, shard, row_target, context_len, held):
    shard_rows, width = shard.shape
    count = prompt_hidden.shape[0]
    spots = [(r, z, y, c) for r in range(2) for z in range(4) for y in range(2) for c in range(2)]
    most_rows = count // 8
    f32, bf16 = jnp.float32, jnp.bfloat16

    def flat(spot):
        return ((spot[0] * 4 + spot[1]) * 2 + spot[2]) * 2 + spot[3]

    def swap(x, r=0, z=0, y=0, c=0):
        pairs = [(flat(spot), flat([a ^ b for a, b in zip(spot, (r, z, y, c))])) for spot in spots]
        return lax.ppermute(x, ("rep", "wide"), pairs)

    def array(rows, dtype=bf16):
        return jax.ShapeDtypeStruct((rows, width), dtype)

    def call(kernel, out_shape, name, *operands, specs=None, flops=2**20, **more):
        return pl.pallas_call(
            kernel,
            out_shape=out_shape,
            in_specs=specs or [WHOLE] * len(operands),
            out_specs=[WHOLE] * len(out_shape) if isinstance(out_shape, list) else WHOLE,
            compiler_params=params(16),
            cost_estimate=pl.CostEstimate(flops=flops, bytes_accessed=2**16, transcendentals=0),
            name=name,
            **more,
        )(*operands)

    hbm = pl.BlockSpec(memory_space=pltpu.HBM)
    half_rows = shard_rows // 2
    ext = half_rows + 16
    half, full, draft_rows = call(
        start_kernel,
        [
            array(ext),
            array(shard_rows + 16),
            jax.ShapeDtypeStruct((16, draft_hidden.shape[2]), bf16),
        ],
        "start_rows",
        *(pltpu.with_memory_space_constraint(x, pltpu.HBM) for x in (row_target.reshape(1, count), shard, draft_hidden)),
        specs=[hbm] * 3,
        scratch_shapes=[
            pltpu.VMEM((1, count), jnp.int32), pltpu.VMEM(draft_hidden.shape, bf16), pltpu.SemaphoreType.DMA((4,))
        ],
    )
    za, zb = swap(half, z=1), swap(half, z=2)
    y0 = swap(full, y=1)
    other_prompt, other_drafts = swap(prompt_hidden, c=1), swap(draft_rows, c=1)

    def copy(x, spans, *ties):
        return call(
            functools.partial(copy_kernel, spans), array(sum(rows for _, rows in spans)), "copy_piece", x, *ties,
            specs=[WHOLE] + [UNREAD] * len(ties),
        )

    rest = call(other_half_kernel, array(half_rows), "other_half", y0)
    db = swap(rest, z=2)
    zab, bare = call(
        join_kernel, [array(2 * ext), array(2 * half_rows)], "join_pieces", za, zb, other_drafts, held,
        specs=[WHOLE] * 2 + [UNREAD] * 2,
    )
    yab, xab = swap(zab, y=1), swap(bare, r=1)
    zc, dc = swap(zb, z=1), swap(db, z=1)
    xc = swap(copy(zc, [(0, half_rows)]), r=1)
    xya = swap(copy(yab, [(0, half_rows)]), r=1)
    yc = swap(copy(zc, [(0, ext)], yab), y=1)

    order = [
        (half, half_rows), (y0, shard_rows), (zab, ext + half_rows), (yab, ext + half_rows),
        (zab, half_rows), (yab, half_rows), (zc, half_rows), (yc, half_rows),
    ]
    pack = call(
        functools.partial(pack_kernel, [(n, first) for n, (_, first) in enumerate(order)]),
        jax.ShapeDtypeStruct((16, len(order) * width), bf16), "pack_rows", *(x for x, _ in order),
    )
    other_pack = swap(pack, c=1)
    limit, column_slot = call(
        functools.partial(count_kernel, most_rows),
        [jax.ShapeDtypeStruct((2, 128), jnp.int32), jax.ShapeDtypeStruct((1, 2 * count), jnp.int32)],
        "count_rows", context_len, pack, other_pack,
        specs=[SCALARS, WHOLE, WHOLE],
    )
    place = call(
        functools.partial(place_kernel, most_rows), jax.ShapeDtypeStruct((1, 2 * count), jnp.int32), "place_rows",
        draft_rows, other_drafts,
    )

    def starts_of(uses):
        def starts():
            rep, wide = lax.axis_index("rep"), lax.axis_index("wide")
            z, y, c = wide // 4, wide // 2 % 2, wide % 2
            found = []
            for _, _, _, (x_step, z_step, y_step), *further in uses:
                owner_z = (z // 2 + z_step // 2) % 2 * 2 + (z + z_step) % 2
                owner = (owner_z * 2 + (y + y_step) % 2) * 2 + c
                start = owner * shard_rows + (0 if x_step is None else (rep + x_step) % 2 * half_rows)
                found.append(start + sum(further))
            return found

        return starts

    rows = [prompt_hidden, other_prompt, draft_rows, other_drafts]
    stages = [
        ([full, y0], [(0, 0, shard_rows, (None, 0, 0)), (1, 0, shard_rows, (None, 0, 1))]),
        (
            [zab, yab],
            [(0, 0, half_rows, (0, 1, 0)), (0, ext, half_rows, (0, 2, 0)),
             (1, 0, half_rows, (0, 1, 1)), (1, ext, half_rows, (0, 2, 1))],
        ),
        (
            [xab, zc],
            [(0, 0, half_rows, (1, 1, 0)), (0, half_rows, half_rows, (1, 2, 0)), (1, 0, half_rows, (0, 3, 0))],
        ),
        (
            [xc, yc, xya, db, dc],
            [(0, 0, half_rows, (1, 3, 0)), (1, 0, half_rows, (0, 3, 1)), (2, 0, half_rows, (1, 1, 1)),
             (3, 0, half_rows, (1, 2, 1)), (4, 0, half_rows, (1, 3, 1))],
        ),
    ]
    sums = []
    total_rows = 2 * count + 32
    for n, (pieces, uses) in enumerate(stages[:-1]):
        sums = [
            call(
                functools.partial(down_kernel, starts_of(uses), [use[:3] for use in uses], n == 0),
                array(total_rows, f32), "down_rows", *rows, *pieces, *sums, flops=2**26,
            )
        ]

    def finish():
        pieces, uses = stages[-1]
        keep, send = call(
            functools.partial(down_place_kernel, starts_of(uses), [use[:3] for use in uses]),
            [array(2 * count + 8, f32)] * 2, "down_place_rows", *rows, place, *sums, *pieces, flops=2**26,
        )
        came = swap(send, c=1)
        block = array(count)
        draft_latent, stay, send = call(
            route_kernel, [array(8, f32), block, block], "route_rows", keep, came,
            scratch_shapes=[pltpu.VMEM((2 * count + 8, width), f32)],
        )
        came = swap(send, y=1)
        stay, send = call(functools.partial(mix_kernel, 2), [block, block], "mix_rows", stay, came)
        came = swap(send, z=2)
        stay, send = call(functools.partial(mix_kernel, 1), [block, block], "mix_rows", stay, came)
        return draft_latent, [stay, swap(send, z=1)]

    return limit, column_slot, finish


def deliver_plain(prompt_hidden, draft_hidden, shard, row_target, context_len, held):
    wide_size = lax.axis_size("wide")
    row_count = prompt_hidden.shape[0]
    slot_count, draft_count, _ = draft_hidden.shape
    latent_width = shard.shape[1]
    most_rows = 2 * ((row_count + wide_size - 1) // wide_size)
    arrived = wide_size * most_rows
    weight = lax.all_gather(shard, "wide", axis=0, tiled=True)
    index = jnp.arange(row_count, dtype=jnp.int32)
    same = (row_target[:, None] == row_target[None, :]) & (index[None, :] < index[:, None])
    rank = jnp.sum(same.astype(jnp.int32), 1)
    front = row_target % slot_count == 0
    place = row_target // slot_count * most_rows + jnp.where(front, rank, most_rows - 1 - rank)
    request = jnp.arange(wide_size * slot_count, dtype=jnp.int32)
    counts = jnp.sum((row_target[None, :] == request[:, None]).astype(jnp.int32), 1)
    counts = lax.all_to_all(counts.reshape(wide_size, slot_count), "wide", split_axis=0, concat_axis=0, tiled=True)
    limit = jnp.broadcast_to((context_len - jnp.sum(counts, 0))[:, None], (slot_count, 128))
    spot = jnp.arange(most_rows, dtype=jnp.int32)[None, :]
    column_slot = jnp.where(
        spot < counts[:, 0:1], 0, jnp.where(spot >= most_rows - counts[:, 1:2], 1, -1)
    ).reshape(1, arrived)

    tile = slot_count * draft_count
    draft_flat = jnp.pad(draft_hidden.reshape(tile, draft_hidden.shape[2]), ((0, 16 - tile), (0, 0)))

    def finish():
        outgoing, draft_latent = pl.pallas_call(
            plain_down_kernel,
            out_shape=[
                jax.ShapeDtypeStruct((arrived, latent_width), jnp.bfloat16),
                jax.ShapeDtypeStruct((slot_count * draft_count, latent_width), jnp.float32),
            ],
            in_specs=[WHOLE] * 4,
            out_specs=[WHOLE] * 2,
            compiler_params=params(24),
            name="down_rows",
        )(place.reshape(1, row_count), prompt_hidden, draft_flat, weight)
        incoming = lax.all_to_all(
            outgoing.reshape(wide_size, most_rows, latent_width), "wide", split_axis=0, concat_axis=0, tiled=True
        )
        return draft_latent, [incoming.reshape(arrived, latent_width)]

    return limit, column_slot, finish


def local(
    prompt_hidden,
    resident_latent,
    row_target,
    row_offset,
    context_len,
    draft_hidden,
    draft_query_heads,
    down_weight,
    key_up_weight,
    value_up_weight,
):
    f32, bf16 = jnp.float32, jnp.bfloat16
    slot_count, span_rows, latent_width = resident_latent.shape
    draft_count = draft_hidden.shape[1]
    rows = QUERY_HEADS * draft_count
    wide_size, row_count = lax.axis_size("wide"), prompt_hidden.shape[0]
    arrived = 2 * ((row_count + wide_size - 1) // wide_size) * wide_size
    window = min(arrived + 128, span_rows)
    hbm = pl.BlockSpec(memory_space=pltpu.HBM)
    stats = [
        jax.ShapeDtypeStruct((slot_count, rows, 1), f32),
        jax.ShapeDtypeStruct((slot_count, rows, 1), f32),
        jax.ShapeDtypeStruct((slot_count, rows, latent_width), f32),
    ]
    turned, peak, total, mixed, edge = pl.pallas_call(
        functools.partial(held_kernel, arrived),
        out_shape=[
            jax.ShapeDtypeStruct((slot_count, 2 * rows, latent_width), bf16),
            *stats,
            jax.ShapeDtypeStruct((slot_count, window, latent_width), bf16),
        ],
        in_specs=[SCALARS, hbm, hbm, hbm],
        out_specs=[WHOLE] * 5,
        scratch_shapes=[
            pltpu.VMEM(draft_query_heads.shape, bf16),
            pltpu.VMEM(key_up_weight.shape, bf16),
            pltpu.VMEM(resident_latent.shape, bf16),
            pltpu.VMEM((slot_count, rows, latent_width), f32),
            pltpu.VMEM((rows, span_rows), f32),
            pltpu.SemaphoreType.DMA((3,)),
        ],
        compiler_params=params(16),
        cost_estimate=pl.CostEstimate(flops=2**31, bytes_accessed=2**21, transcendentals=0),
        name="held_rows",
    )(context_len, *(pltpu.with_memory_space_constraint(x, pltpu.HBM) for x in (draft_query_heads, key_up_weight, resident_latent)))
    known = wide_size == 16 and lax.axis_size("rep") == 2
    limit, column_slot, finish = (deliver if known else deliver_plain)(
        prompt_hidden, draft_hidden, down_weight, row_target, context_len, peak
    )
    draft_latent, incoming = finish()
    peak, total, mixed = pl.pallas_call(
        functools.partial(window_kernel, arrived, span_rows, draft_count),
        out_shape=stats,
        in_specs=[SCALARS] + [WHOLE] * 7,
        out_specs=[WHOLE] * 3,
        compiler_params=params(16),
        cost_estimate=pl.CostEstimate(flops=2**30, bytes_accessed=2**16, transcendentals=0),
        name="window_rows",
    )(context_len, limit, turned, peak, total, mixed, edge, draft_latent)
    return pl.pallas_call(
        late_kernel,
        out_shape=jax.ShapeDtypeStruct((slot_count, draft_count, QUERY_HEADS * HEAD_SIZE), bf16),
        in_specs=[WHOLE] * (6 + len(incoming)),
        out_specs=WHOLE,
        scratch_shapes=[
            pltpu.VMEM((arrived, latent_width), bf16),
            pltpu.VMEM((slot_count, 2 * rows, latent_width), bf16),
        ],
        compiler_params=params(16),
        name="late_rows",
    )(column_slot, turned, peak, total, mixed, value_up_weight, *incoming)


def solution(mesh):
    placed = (
        P(("rep", "wide"), None),
        P(("rep", "wide"), None, None),
        P(("rep", "wide")),
        P(("rep", "wide")),
        P(("rep", "wide")),
        P(("rep", "wide"), None, None),
        P(("rep", "wide"), None, None),
        P("wide", None),
        P(),
        P(),
    )
    return jax.shard_map(
        local, mesh=mesh, in_specs=placed, out_specs=P(("rep", "wide"), None, None), check_vma=False
    )
```

```python
import functools
import math

import jax
import jax.numpy as jnp
from jax import lax
from jax.experimental import pallas as pl
from jax.experimental.pallas import tpu as pltpu
from jax.sharding import PartitionSpec as P

QUERY_HEADS = 64
HEAD_SIZE = 128
FAR = -1e30
NT = (((1,), (1,)), ((), ()))
WHOLE = pl.BlockSpec(memory_space=pltpu.VMEM)
SCALARS = pl.BlockSpec(memory_space=pltpu.SMEM)
UNREAD = pl.BlockSpec(memory_space=pl.ANY)


def params(mib):
    return pltpu.CompilerParams(vmem_limit_bytes=mib * 1024 * 1024)


def split_rows(x):
    top = x.astype(jnp.bfloat16)
    rest = (x - top.astype(jnp.float32)).astype(jnp.bfloat16)
    return jnp.concatenate([top, rest], 0)


def join_rows(x):
    half = x.shape[0] // 2
    return x[:half] + x[half:]


def held_kernel(
    arrived, context_ref, query_hbm, key_up_hbm, cache_hbm, turned_ref, peak_ref, total_ref, mixed_ref, window_ref,
    query_ref, key_up_ref, cache_ref, float_ref, scores_ref, sems,
):
    copies = [
        pltpu.make_async_copy(source, target, sems.at[n])
        for n, (source, target) in enumerate(
            [(query_hbm, query_ref), (key_up_hbm, key_up_ref), (cache_hbm, cache_ref)]
        )
    ]
    for copy in copies:
        copy.start()
    slot_count, span_rows, _ = cache_ref.shape
    draft_count = query_ref.shape[1]
    heads_kv = key_up_ref.shape[1] // HEAD_SIZE
    group_size = QUERY_HEADS // heads_kv
    rows = group_size * draft_count
    scale = math.log2(math.e) / math.sqrt(HEAD_SIZE)
    step = 256
    copies[0].wait()
    copies[1].wait()
    for k in range(heads_kv):
        pieces = []
        for b in range(slot_count):
            for g in range(group_size):
                lane = (k * group_size + g) * HEAD_SIZE
                pieces.append(query_ref[b, :, lane : lane + HEAD_SIZE].astype(jnp.float32))
        query = jnp.concatenate(pieces, 0).astype(jnp.bfloat16)
        key_up = key_up_ref[:, k * HEAD_SIZE : (k + 1) * HEAD_SIZE]
        turned = lax.dot_general(query, key_up, NT, preferred_element_type=jnp.float32) * scale
        for b in range(slot_count):
            float_ref[b, k * rows : (k + 1) * rows, :] = turned[b * rows : (b + 1) * rows]
    copies[2].wait()
    for b in range(slot_count):
        first = pl.multiple_of(window_start(context_ref[b], arrived, window_ref.shape[1], span_rows), 128)
        window_ref[b] = cache_ref[b, pl.ds(first, window_ref.shape[1]), :]
        turned_ref[b] = split_rows(float_ref[b])
        peak = None
        for c in range(0, span_rows, step):
            scores = join_rows(
                lax.dot_general(turned_ref[b], cache_ref[b, c : c + step], NT, preferred_element_type=jnp.float32)
            )
            column = lax.broadcasted_iota(jnp.int32, (1, step), 1) + c
            scores = jnp.where(column < context_ref[b] - arrived, scores, FAR)
            scores_ref[:, c : c + step] = scores
            top = jnp.max(scores, 1, keepdims=True)
            peak = top if peak is None else jnp.maximum(peak, top)
        peak_ref[b] = peak
        total = jnp.zeros_like(peak)
        mixed = jnp.zeros(mixed_ref.shape[1:], jnp.float32)
        for c in range(0, span_rows, step):
            weights = jnp.exp2(scores_ref[:, c : c + step] - peak)
            total += jnp.sum(weights, 1, keepdims=True)
            mixed += join_rows(
                jnp.dot(split_rows(weights), cache_ref[b, c : c + step], preferred_element_type=jnp.float32)
            )
        total_ref[b] = total
        mixed_ref[b] = mixed


def window_start(context, arrived, size, span_rows):
    return jnp.clip((context - arrived) // 128 * 128, 0, span_rows - size)


def window_kernel(
    arrived, span_rows, draft_count, context_ref, limit_ref, turned_ref, peak_ref, total_ref, mixed_ref, window_ref,
    draft_latent_ref, new_peak_ref, new_total_ref, new_mixed_ref,
):
    slot_count, size, width = window_ref.shape
    rows = peak_ref.shape[1]
    drafts = draft_latent_ref[...]
    drafts = jnp.concatenate([drafts, jnp.zeros((128 - drafts.shape[0], width), jnp.float32)], 0).astype(jnp.bfloat16)
    token = lax.broadcasted_iota(jnp.int32, (rows, 1), 0) % draft_count
    spot = lax.broadcasted_iota(jnp.int32, (rows, 128), 1)
    for b in range(slot_count):
        first = window_start(context_ref[b], arrived, size, span_rows)
        scores = join_rows(lax.dot_general(turned_ref[b], window_ref[b], NT, preferred_element_type=jnp.float32))
        column = lax.broadcasted_iota(jnp.int32, (1, size), 1) + first
        seen = (column >= context_ref[b] - arrived) & (column < limit_ref[b : b + 1, 0:1])
        scores = jnp.where(seen, scores, FAR)
        draft_scores = join_rows(lax.dot_general(turned_ref[b], drafts, NT, preferred_element_type=jnp.float32))
        draft_seen = (spot >= b * draft_count) & (spot <= b * draft_count + token)
        draft_scores = jnp.where(draft_seen, draft_scores, FAR)
        peak = jnp.maximum(jnp.max(scores, 1, keepdims=True), jnp.max(draft_scores, 1, keepdims=True))
        peak = jnp.maximum(peak, peak_ref[b])
        weights, draft_weights = jnp.exp2(scores - peak), jnp.exp2(draft_scores - peak)
        fade = jnp.exp2(peak_ref[b] - peak)
        new_peak_ref[b] = peak
        total = jnp.sum(weights, 1, keepdims=True) + jnp.sum(draft_weights, 1, keepdims=True)
        new_total_ref[b] = total_ref[b] * fade + total
        mixed = jnp.dot(split_rows(weights), window_ref[b], preferred_element_type=jnp.float32)
        mixed += jnp.dot(split_rows(draft_weights), drafts, preferred_element_type=jnp.float32)
        new_mixed_ref[b] = mixed_ref[b] * fade + join_rows(mixed)


def piece_sums(starts, spans, row_refs, refs):
    total = None
    for start, (n, first, depth) in zip(starts, spans):
        lanes = pl.ds(pl.multiple_of(start, HEAD_SIZE), depth)
        rows = [ref[:, lanes] for ref in row_refs]
        piece = refs[n][first : first + depth, :]
        product = jnp.dot(jnp.concatenate(rows, 0), piece, preferred_element_type=jnp.float32)
        total = product if total is None else total + product
    return total


def down_kernel(starts_of, spans, first, *refs):
    row_refs, refs, out_ref = refs[:4], refs[4:-1], refs[-1]
    total = piece_sums(starts_of(), spans, row_refs, refs)
    out_ref[...] = total if first else total + refs[-1][...]


def down_place_kernel(starts_of, spans, *refs):
    row_refs, refs, (keep_ref, send_ref) = refs[:4], refs[4:-2], refs[-2:]
    place_ref, sum_ref, refs = refs[0], refs[1], refs[2:]
    total = piece_sums(starts_of(), spans, row_refs, refs) + sum_ref[...]
    slots, width = keep_ref.shape[0] - 8, keep_ref.shape[1]
    count = place_ref.shape[1]
    parts = []
    left = total[:count]
    for _ in range(3):
        part = left.astype(jnp.bfloat16)
        parts.append(part)
        left = left - part.astype(jnp.float32)
    parts = jnp.concatenate(parts, 1)
    core = lax.axis_index("wide") % 2
    spot = lax.broadcasted_iota(jnp.int32, (slots, count), 0)
    for ref, target, draft in ((keep_ref, core, count), (send_ref, 1 - core, count + 16)):
        chosen = jnp.where(spot + target * slots == place_ref[...], 1.0, 0.0).astype(jnp.bfloat16)
        moved = jnp.dot(chosen, parts, preferred_element_type=jnp.float32)
        ref[:slots, :] = moved[:, :width] + moved[:, width : 2 * width] + moved[:, 2 * width :]
        ref[slots:, :] = total[draft : draft + 8]


def route_kernel(keep_ref, came_ref, draft_latent_ref, out_ref):
    slots = out_ref.shape[0]
    out_ref[...] = (keep_ref[:slots, :] + came_ref[:slots, :]).astype(jnp.bfloat16)
    drafts = keep_ref[slots:, :] + came_ref[slots:, :]
    draft_latent_ref[...] = drafts.astype(jnp.bfloat16).astype(jnp.float32)


def start_kernel(target_hbm, shard_hbm, draft_hbm, half_ref, full_ref, rows_ref, target_ref, draft_ref, sems):
    half_rows, shard_rows = half_ref.shape[0] - 16, full_ref.shape[0] - 16
    mine = pl.ds(pl.multiple_of(lax.axis_index("rep") * half_rows, half_rows), half_rows)
    copies = [
        pltpu.make_async_copy(target_hbm, target_ref, sems.at[0]),
        pltpu.make_async_copy(shard_hbm.at[mine], half_ref.at[:half_rows], sems.at[1]),
        pltpu.make_async_copy(shard_hbm, full_ref.at[:shard_rows], sems.at[2]),
        pltpu.make_async_copy(draft_hbm, draft_ref, sems.at[3]),
    ]
    for copy in copies:
        copy.start()
    width, count = half_ref.shape[1], target_ref.shape[1]
    copies[0].wait()
    hit = lax.broadcasted_iota(jnp.int32, (width, count), 0) == target_ref[...]
    hit = jnp.where(hit, 1.0, 0.0).astype(jnp.bfloat16)
    block = lax.dot_general(jnp.ones((16, count), jnp.bfloat16), hit, NT, preferred_element_type=jnp.float32)
    half_ref[half_rows:, :] = block.astype(jnp.bfloat16)
    full_ref[shard_rows:, :] = block.astype(jnp.bfloat16)
    copies[3].wait()
    rows = [draft_ref[b].astype(jnp.float32) for b in range(draft_ref.shape[0])]
    target = jnp.broadcast_to(target_ref[...].astype(jnp.float32), (8, count))
    rows.append(jnp.concatenate([target, jnp.zeros((8, rows_ref.shape[1] - count), jnp.float32)], 1))
    rows_ref[...] = jnp.concatenate(rows, 0).astype(jnp.bfloat16)
    for copy in copies[1:3]:
        copy.wait()


def join_kernel(one_ref, two_ref, *refs):
    rows, (out_ref, bare_ref) = one_ref.shape[0], refs[-2:]
    out_ref[:rows, :] = one_ref[...]
    out_ref[rows:, :] = two_ref[...]
    bare_ref[: rows - 16, :] = one_ref[: rows - 16, :]
    bare_ref[rows - 16 :, :] = two_ref[: rows - 16, :]


def copy_kernel(spans, one_ref, *refs):
    done = 0
    for first, count in spans:
        refs[-1][done : done + count, :] = one_ref[first : first + count, :]
        done += count


def other_half_kernel(shard_ref, out_ref):
    rows = out_ref.shape[0]
    first = pl.multiple_of((1 - lax.axis_index("rep")) * rows, rows)
    out_ref[...] = shard_ref[pl.ds(first, rows), :]


def pack_kernel(spans, *refs):
    out_ref, width = refs[-1], refs[0].shape[1]
    for m, (n, first) in enumerate(spans):
        out_ref[:, m * width : (m + 1) * width] = refs[n][first : first + 16, :]


def count_kernel(most_rows, context_ref, mine_ref, other_ref, limit_ref, column_slot_ref):
    f32 = jnp.float32
    width = mine_ref.shape[1] // 8
    wide = lax.axis_index("wide")
    core = wide % 2
    mine, other = mine_ref[...].astype(f32), other_ref[...].astype(f32)
    low = jnp.where(core == 0, mine[:1], other[:1])
    high = jnp.where(core == 0, other[:1], mine[:1])
    counts = []
    for n in range(8):
        counts += [low[:, n * width : (n + 1) * width], high[:, n * width : (n + 1) * width]]
    counts = jnp.concatenate(counts, 0)
    lane = lax.broadcasted_iota(jnp.int32, counts.shape, 1)
    row = lax.broadcasted_iota(jnp.int32, counts.shape, 0)
    z, y = wide // 4, wide // 2 % 2
    chip = lane // (2 * most_rows)
    near, far, side = (chip // 2 + z) % 2, (chip // 4 + z // 2) % 2, (chip + y) % 2
    source = (near * 4 + far * 2 + side) * 2 + lane // most_rows % 2
    spread = []
    for b in range(2):
        number = jnp.sum(jnp.where(lane == wide * 2 + b, counts, 0.0), 1, keepdims=True)
        limit = context_ref[b] - jnp.sum(number, 0, keepdims=True).astype(jnp.int32)
        limit_ref[b : b + 1, :] = jnp.broadcast_to(limit, (1, limit_ref.shape[1]))
        spread.append(jnp.sum(jnp.where(source == row, number, 0.0), 0, keepdims=True).astype(jnp.int32))
    spot = lax.broadcasted_iota(jnp.int32, column_slot_ref.shape, 1) % most_rows
    column_slot_ref[...] = jnp.where(spot < spread[0], 0, jnp.where(spot >= most_rows - spread[1], 1, -1))


def place_kernel(most_rows, mine_ref, other_ref, place_ref):
    f32, bf16 = jnp.float32, jnp.bfloat16
    count = place_ref.shape[1] // 2
    core = lax.axis_index("wide") % 2
    earlier = lax.broadcasted_iota(jnp.int32, (count, count), 0) < lax.broadcasted_iota(jnp.int32, (count, count), 1)
    earlier = jnp.where(earlier, 1.0, 0.0).astype(bf16)
    for n, (ref, owner) in enumerate(((mine_ref, core), (other_ref, 1 - core))):
        target = ref[:, :count].astype(f32)[8:9].astype(jnp.int32)
        hit = jnp.where(lax.broadcasted_iota(jnp.int32, (64, count), 0) == target, 1.0, 0.0)
        before = jnp.dot(hit.astype(bf16), earlier, preferred_element_type=f32)
        rank = jnp.sum(hit * before, 0, keepdims=True).astype(jnp.int32)
        spot = jnp.where(target % 2 == 0, rank, most_rows - 1 - rank)
        chip, side = target // 4, target // 2 % 2
        place_ref[:, n * count : (n + 1) * count] = side * 2 * count + (chip * 2 + owner) * most_rows + spot


def plain_down_kernel(place_ref, prompt_ref, draft_ref, weight_ref, outgoing_ref, draft_latent_ref):
    count = prompt_ref.shape[0]
    rows = jnp.concatenate([prompt_ref[...], draft_ref[...]], 0)
    total = jnp.dot(rows, weight_ref[...], preferred_element_type=jnp.float32)
    draft_latent_ref[...] = total[count : count + 8].astype(jnp.bfloat16).astype(jnp.float32)
    spot = lax.broadcasted_iota(jnp.int32, (outgoing_ref.shape[0], count), 0)
    chosen = jnp.where(spot == place_ref[...], 1.0, 0.0).astype(jnp.bfloat16)
    latent = total[:count].astype(jnp.bfloat16)
    outgoing_ref[...] = jnp.dot(chosen, latent, preferred_element_type=jnp.float32).astype(jnp.bfloat16)


def late_kernel(column_slot_ref, turned_ref, peak_ref, total_ref, mixed_ref, value_up_ref, *refs):
    incoming_refs, (out_ref, rows_ref, parted_ref) = refs[:-3], refs[-3:]
    slot_count, draft_count, _ = out_ref.shape
    heads_kv = value_up_ref.shape[1] // HEAD_SIZE
    group_size = QUERY_HEADS // heads_kv
    head_rows = group_size * draft_count
    rows = peak_ref.shape[1]
    block = incoming_refs[0].shape[0]
    for n, ref in enumerate(incoming_refs):
        rows_ref[n * block : (n + 1) * block, :] = ref[...]
    for b in range(slot_count):
        scores = join_rows(lax.dot_general(turned_ref[b], rows_ref[...], NT, preferred_element_type=jnp.float32))
        scores = jnp.where(column_slot_ref[...] == b, scores, FAR)
        peak = jnp.maximum(jnp.max(scores, 1, keepdims=True), peak_ref[b])
        weights = jnp.exp2(scores - peak)
        fade = jnp.exp2(peak_ref[b] - peak)
        total = total_ref[b] * fade + jnp.sum(weights, 1, keepdims=True)
        mixed = join_rows(jnp.dot(split_rows(weights), rows_ref[...], preferred_element_type=jnp.float32))
        parted_ref[b] = split_rows((mixed_ref[b] * fade + mixed) / total)
    for k in range(heads_kv):
        part = []
        for b in range(slot_count):
            part.append(parted_ref[b, k * head_rows : (k + 1) * head_rows, :])
            part.append(parted_ref[b, rows + k * head_rows : rows + (k + 1) * head_rows, :])
        value_up = value_up_ref[:, k * HEAD_SIZE : (k + 1) * HEAD_SIZE]
        both = jnp.dot(jnp.concatenate(part, 0), value_up, preferred_element_type=jnp.float32)
        for b in range(slot_count):
            result = join_rows(both[b * 2 * head_rows : (b + 1) * 2 * head_rows])
            wide = jnp.concatenate(
                [result[g * draft_count : (g + 1) * draft_count] for g in range(group_size)], 1
            )
            out_ref[b, :, k * group_size * HEAD_SIZE : (k + 1) * group_size * HEAD_SIZE] = wide.astype(jnp.bfloat16)


def deliver(prompt_hidden, draft_hidden, shard, row_target, context_len, held):
    shard_rows, width = shard.shape
    count = prompt_hidden.shape[0]
    spots = [(r, z, y, c) for r in range(2) for z in range(4) for y in range(2) for c in range(2)]
    most_rows = count // 8
    f32, bf16 = jnp.float32, jnp.bfloat16

    def flat(spot):
        return ((spot[0] * 4 + spot[1]) * 2 + spot[2]) * 2 + spot[3]

    def swap(x, r=0, z=0, y=0, c=0):
        pairs = [(flat(spot), flat([a ^ b for a, b in zip(spot, (r, z, y, c))])) for spot in spots]
        return lax.ppermute(x, ("rep", "wide"), pairs)

    def array(rows, dtype=bf16):
        return jax.ShapeDtypeStruct((rows, width), dtype)

    def call(kernel, out_shape, name, *operands, specs=None, flops=2**20, **more):
        return pl.pallas_call(
            kernel,
            out_shape=out_shape,
            in_specs=specs or [WHOLE] * len(operands),
            out_specs=[WHOLE] * len(out_shape) if isinstance(out_shape, list) else WHOLE,
            compiler_params=params(16),
            cost_estimate=pl.CostEstimate(flops=flops, bytes_accessed=2**16, transcendentals=0),
            name=name,
            **more,
        )(*operands)

    hbm = pl.BlockSpec(memory_space=pltpu.HBM)
    half_rows = shard_rows // 2
    ext = half_rows + 16
    half, full, draft_rows = call(
        start_kernel,
        [
            array(ext),
            array(shard_rows + 16),
            jax.ShapeDtypeStruct((16, draft_hidden.shape[2]), bf16),
        ],
        "start_rows",
        *(pltpu.with_memory_space_constraint(x, pltpu.HBM) for x in (row_target.reshape(1, count), shard, draft_hidden)),
        specs=[hbm] * 3,
        scratch_shapes=[
            pltpu.VMEM((1, count), jnp.int32), pltpu.VMEM(draft_hidden.shape, bf16), pltpu.SemaphoreType.DMA((4,))
        ],
    )
    za, zb = swap(half, z=1), swap(half, z=2)
    y0 = swap(full, y=1)
    other_prompt, other_drafts = swap(prompt_hidden, c=1), swap(draft_rows, c=1)

    def copy(x, spans, *ties):
        return call(
            functools.partial(copy_kernel, spans), array(sum(rows for _, rows in spans)), "copy_piece", x, *ties,
            specs=[WHOLE] + [UNREAD] * len(ties),
        )

    rest = call(other_half_kernel, array(half_rows), "other_half", y0)
    db = swap(rest, z=2)
    zab, bare = call(
        join_kernel, [array(2 * ext), array(2 * half_rows)], "join_pieces", za, zb, other_drafts, held,
        specs=[WHOLE] * 2 + [UNREAD] * 2,
    )
    yab, xab = swap(zab, y=1), swap(bare, r=1)
    zc, dc = swap(zb, z=1), swap(db, z=1)
    xc = swap(copy(zc, [(0, half_rows)]), r=1)
    xya = swap(copy(yab, [(0, half_rows)]), r=1)
    yc = swap(copy(zc, [(0, ext)], yab), y=1)

    order = [
        (half, half_rows), (y0, shard_rows), (zab, ext + half_rows), (yab, ext + half_rows),
        (zab, half_rows), (yab, half_rows), (zc, half_rows), (yc, half_rows),
    ]
    pack = call(
        functools.partial(pack_kernel, [(n, first) for n, (_, first) in enumerate(order)]),
        jax.ShapeDtypeStruct((16, len(order) * width), bf16), "pack_rows", *(x for x, _ in order),
    )
    other_pack = swap(pack, c=1)
    limit, column_slot = call(
        functools.partial(count_kernel, most_rows),
        [jax.ShapeDtypeStruct((2, 128), jnp.int32), jax.ShapeDtypeStruct((1, 2 * count), jnp.int32)],
        "count_rows", context_len, pack, other_pack,
        specs=[SCALARS, WHOLE, WHOLE],
    )
    place = call(
        functools.partial(place_kernel, most_rows), jax.ShapeDtypeStruct((1, 2 * count), jnp.int32), "place_rows",
        draft_rows, other_drafts,
    )

    def starts_of(uses):
        def starts():
            rep, wide = lax.axis_index("rep"), lax.axis_index("wide")
            z, y, c = wide // 4, wide // 2 % 2, wide % 2
            found = []
            for _, _, _, (x_step, z_step, y_step), *further in uses:
                owner_z = (z // 2 + z_step // 2) % 2 * 2 + (z + z_step) % 2
                owner = (owner_z * 2 + (y + y_step) % 2) * 2 + c
                start = owner * shard_rows + (0 if x_step is None else (rep + x_step) % 2 * half_rows)
                found.append(start + sum(further))
            return found

        return starts

    rows = [prompt_hidden, other_prompt, draft_rows, other_drafts]
    stages = [
        ([full, y0], [(0, 0, shard_rows, (None, 0, 0)), (1, 0, shard_rows, (None, 0, 1))]),
        (
            [zab, yab],
            [(0, 0, half_rows, (0, 1, 0)), (0, ext, half_rows, (0, 2, 0)),
             (1, 0, half_rows, (0, 1, 1)), (1, ext, half_rows, (0, 2, 1))],
        ),
        (
            [xab, zc],
            [(0, 0, half_rows, (1, 1, 0)), (0, half_rows, half_rows, (1, 2, 0)), (1, 0, half_rows, (0, 3, 0))],
        ),
        (
            [xc, yc, xya, db, dc],
            [(0, 0, half_rows, (1, 3, 0)), (1, 0, half_rows, (0, 3, 1)), (2, 0, half_rows, (1, 1, 1)),
             (3, 0, half_rows, (1, 2, 1)), (4, 0, half_rows, (1, 3, 1))],
        ),
    ]
    sums = []
    total_rows = 2 * count + 32
    for n, (pieces, uses) in enumerate(stages[:-1]):
        sums = [
            call(
                functools.partial(down_kernel, starts_of(uses), [use[:3] for use in uses], n == 0),
                array(total_rows, f32), "down_rows", *rows, *pieces, *sums, flops=2**26,
            )
        ]

    def finish():
        pieces, uses = stages[-1]
        keep, send = call(
            functools.partial(down_place_kernel, starts_of(uses), [use[:3] for use in uses]),
            [array(2 * count + 8, f32)] * 2, "down_place_rows", *rows, place, *sums, *pieces, flops=2**26,
        )
        came = swap(send, c=1)
        draft_latent, outgoing = call(route_kernel, [array(8, f32), array(2 * count)], "route_rows", keep, came)
        incoming = lax.all_to_all(
            outgoing.reshape(8, 2 * most_rows, width), "wide", split_axis=0, concat_axis=0, tiled=True,
            axis_index_groups=[list(range(c, 16, 2)) for c in range(2)],
        )
        return draft_latent, [incoming.reshape(2 * count, width)]

    return limit, column_slot, finish


def deliver_plain(prompt_hidden, draft_hidden, shard, row_target, context_len, held):
    wide_size = lax.axis_size("wide")
    row_count = prompt_hidden.shape[0]
    slot_count, draft_count, _ = draft_hidden.shape
    latent_width = shard.shape[1]
    most_rows = 2 * ((row_count + wide_size - 1) // wide_size)
    arrived = wide_size * most_rows
    weight = lax.all_gather(shard, "wide", axis=0, tiled=True)
    index = jnp.arange(row_count, dtype=jnp.int32)
    same = (row_target[:, None] == row_target[None, :]) & (index[None, :] < index[:, None])
    rank = jnp.sum(same.astype(jnp.int32), 1)
    front = row_target % slot_count == 0
    place = row_target // slot_count * most_rows + jnp.where(front, rank, most_rows - 1 - rank)
    request = jnp.arange(wide_size * slot_count, dtype=jnp.int32)
    counts = jnp.sum((row_target[None, :] == request[:, None]).astype(jnp.int32), 1)
    counts = lax.all_to_all(counts.reshape(wide_size, slot_count), "wide", split_axis=0, concat_axis=0, tiled=True)
    limit = jnp.broadcast_to((context_len - jnp.sum(counts, 0))[:, None], (slot_count, 128))
    spot = jnp.arange(most_rows, dtype=jnp.int32)[None, :]
    column_slot = jnp.where(
        spot < counts[:, 0:1], 0, jnp.where(spot >= most_rows - counts[:, 1:2], 1, -1)
    ).reshape(1, arrived)

    tile = slot_count * draft_count
    draft_flat = jnp.pad(draft_hidden.reshape(tile, draft_hidden.shape[2]), ((0, 16 - tile), (0, 0)))

    def finish():
        outgoing, draft_latent = pl.pallas_call(
            plain_down_kernel,
            out_shape=[
                jax.ShapeDtypeStruct((arrived, latent_width), jnp.bfloat16),
                jax.ShapeDtypeStruct((slot_count * draft_count, latent_width), jnp.float32),
            ],
            in_specs=[WHOLE] * 4,
            out_specs=[WHOLE] * 2,
            compiler_params=params(24),
            name="down_rows",
        )(place.reshape(1, row_count), prompt_hidden, draft_flat, weight)
        incoming = lax.all_to_all(
            outgoing.reshape(wide_size, most_rows, latent_width), "wide", split_axis=0, concat_axis=0, tiled=True
        )
        return draft_latent, [incoming.reshape(arrived, latent_width)]

    return limit, column_slot, finish


def local(
    prompt_hidden,
    resident_latent,
    row_target,
    row_offset,
    context_len,
    draft_hidden,
    draft_query_heads,
    down_weight,
    key_up_weight,
    value_up_weight,
):
    f32, bf16 = jnp.float32, jnp.bfloat16
    slot_count, span_rows, latent_width = resident_latent.shape
    draft_count = draft_hidden.shape[1]
    rows = QUERY_HEADS * draft_count
    wide_size, row_count = lax.axis_size("wide"), prompt_hidden.shape[0]
    arrived = 2 * ((row_count + wide_size - 1) // wide_size) * wide_size
    window = min(arrived + 128, span_rows)
    hbm = pl.BlockSpec(memory_space=pltpu.HBM)
    stats = [
        jax.ShapeDtypeStruct((slot_count, rows, 1), f32),
        jax.ShapeDtypeStruct((slot_count, rows, 1), f32),
        jax.ShapeDtypeStruct((slot_count, rows, latent_width), f32),
    ]
    turned, peak, total, mixed, edge = pl.pallas_call(
        functools.partial(held_kernel, arrived),
        out_shape=[
            jax.ShapeDtypeStruct((slot_count, 2 * rows, latent_width), bf16),
            *stats,
            jax.ShapeDtypeStruct((slot_count, window, latent_width), bf16),
        ],
        in_specs=[SCALARS, hbm, hbm, hbm],
        out_specs=[WHOLE] * 5,
        scratch_shapes=[
            pltpu.VMEM(draft_query_heads.shape, bf16),
            pltpu.VMEM(key_up_weight.shape, bf16),
            pltpu.VMEM(resident_latent.shape, bf16),
            pltpu.VMEM((slot_count, rows, latent_width), f32),
            pltpu.VMEM((rows, span_rows), f32),
            pltpu.SemaphoreType.DMA((3,)),
        ],
        compiler_params=params(16),
        cost_estimate=pl.CostEstimate(flops=2**31, bytes_accessed=2**21, transcendentals=0),
        name="held_rows",
    )(context_len, *(pltpu.with_memory_space_constraint(x, pltpu.HBM) for x in (draft_query_heads, key_up_weight, resident_latent)))
    known = wide_size == 16 and lax.axis_size("rep") == 2
    limit, column_slot, finish = (deliver if known else deliver_plain)(
        prompt_hidden, draft_hidden, down_weight, row_target, context_len, peak
    )
    draft_latent, incoming = finish()
    peak, total, mixed = pl.pallas_call(
        functools.partial(window_kernel, arrived, span_rows, draft_count),
        out_shape=stats,
        in_specs=[SCALARS] + [WHOLE] * 7,
        out_specs=[WHOLE] * 3,
        compiler_params=params(16),
        cost_estimate=pl.CostEstimate(flops=2**30, bytes_accessed=2**16, transcendentals=0),
        name="window_rows",
    )(context_len, limit, turned, peak, total, mixed, edge, draft_latent)
    return pl.pallas_call(
        late_kernel,
        out_shape=jax.ShapeDtypeStruct((slot_count, draft_count, QUERY_HEADS * HEAD_SIZE), bf16),
        in_specs=[WHOLE] * (6 + len(incoming)),
        out_specs=WHOLE,
        scratch_shapes=[
            pltpu.VMEM((arrived, latent_width), bf16),
            pltpu.VMEM((slot_count, 2 * rows, latent_width), bf16),
        ],
        compiler_params=params(16),
        name="late_rows",
    )(column_slot, turned, peak, total, mixed, value_up_weight, *incoming)


def solution(mesh):
    placed = (
        P(("rep", "wide"), None),
        P(("rep", "wide"), None, None),
        P(("rep", "wide")),
        P(("rep", "wide")),
        P(("rep", "wide")),
        P(("rep", "wide"), None, None),
        P(("rep", "wide"), None, None),
        P("wide", None),
        P(),
        P(),
    )
    return jax.shard_map(
        local, mesh=mesh, in_specs=placed, out_specs=P(("rep", "wide"), None, None), check_vma=False
    )
```

```python
import functools
import math

import jax
import jax.numpy as jnp
from jax import lax
from jax.experimental import pallas as pl
from jax.experimental.pallas import tpu as pltpu
from jax.sharding import PartitionSpec as P

QUERY_HEADS = 64
HEAD_SIZE = 128
FAR = -1e30
NT = (((1,), (1,)), ((), ()))
WHOLE = pl.BlockSpec(memory_space=pltpu.VMEM)
SCALARS = pl.BlockSpec(memory_space=pltpu.SMEM)
UNREAD = pl.BlockSpec(memory_space=pl.ANY)


def params(mib):
    return pltpu.CompilerParams(vmem_limit_bytes=mib * 1024 * 1024)


def split_rows(x):
    top = x.astype(jnp.bfloat16)
    rest = (x - top.astype(jnp.float32)).astype(jnp.bfloat16)
    return jnp.concatenate([top, rest], 0)


def join_rows(x):
    half = x.shape[0] // 2
    return x[:half] + x[half:]


def held_kernel(
    arrived, context_ref, query_hbm, key_up_hbm, cache_hbm, turned_ref, peak_ref, total_ref, mixed_ref, window_ref,
    query_ref, key_up_ref, cache_ref, float_ref, scores_ref, sems,
):
    copies = [
        pltpu.make_async_copy(source, target, sems.at[n])
        for n, (source, target) in enumerate(
            [(query_hbm, query_ref), (key_up_hbm, key_up_ref), (cache_hbm, cache_ref)]
        )
    ]
    for copy in copies:
        copy.start()
    slot_count, span_rows, _ = cache_ref.shape
    draft_count = query_ref.shape[1]
    heads_kv = key_up_ref.shape[1] // HEAD_SIZE
    group_size = QUERY_HEADS // heads_kv
    rows = group_size * draft_count
    scale = math.log2(math.e) / math.sqrt(HEAD_SIZE)
    step = 256
    copies[0].wait()
    copies[1].wait()
    for k in range(heads_kv):
        pieces = []
        for b in range(slot_count):
            for g in range(group_size):
                lane = (k * group_size + g) * HEAD_SIZE
                pieces.append(query_ref[b, :, lane : lane + HEAD_SIZE].astype(jnp.float32))
        query = jnp.concatenate(pieces, 0).astype(jnp.bfloat16)
        key_up = key_up_ref[:, k * HEAD_SIZE : (k + 1) * HEAD_SIZE]
        turned = lax.dot_general(query, key_up, NT, preferred_element_type=jnp.float32) * scale
        for b in range(slot_count):
            float_ref[b, k * rows : (k + 1) * rows, :] = turned[b * rows : (b + 1) * rows]
    copies[2].wait()
    for b in range(slot_count):
        first = pl.multiple_of(window_start(context_ref[b], arrived, window_ref.shape[1], span_rows), 128)
        window_ref[b] = cache_ref[b, pl.ds(first, window_ref.shape[1]), :]
        turned_ref[b] = split_rows(float_ref[b])
        peak = None
        for c in range(0, span_rows, step):
            scores = join_rows(
                lax.dot_general(turned_ref[b], cache_ref[b, c : c + step], NT, preferred_element_type=jnp.float32)
            )
            column = lax.broadcasted_iota(jnp.int32, (1, step), 1) + c
            scores = jnp.where(column < context_ref[b] - arrived, scores, FAR)
            scores_ref[:, c : c + step] = scores
            top = jnp.max(scores, 1, keepdims=True)
            peak = top if peak is None else jnp.maximum(peak, top)
        peak_ref[b] = peak
        total = jnp.zeros_like(peak)
        mixed = jnp.zeros(mixed_ref.shape[1:], jnp.float32)
        for c in range(0, span_rows, step):
            weights = jnp.exp2(scores_ref[:, c : c + step] - peak)
            total += jnp.sum(weights, 1, keepdims=True)
            mixed += join_rows(
                jnp.dot(split_rows(weights), cache_ref[b, c : c + step], preferred_element_type=jnp.float32)
            )
        total_ref[b] = total
        mixed_ref[b] = mixed


def window_start(context, arrived, size, span_rows):
    return jnp.clip((context - arrived) // 128 * 128, 0, span_rows - size)


def window_kernel(
    arrived, span_rows, draft_count, context_ref, limit_ref, turned_ref, peak_ref, total_ref, mixed_ref, window_ref,
    draft_latent_ref, new_peak_ref, new_total_ref, new_mixed_ref,
):
    slot_count, size, width = window_ref.shape
    rows = peak_ref.shape[1]
    drafts = draft_latent_ref[...]
    drafts = jnp.concatenate([drafts, jnp.zeros((128 - drafts.shape[0], width), jnp.float32)], 0).astype(jnp.bfloat16)
    token = lax.broadcasted_iota(jnp.int32, (rows, 1), 0) % draft_count
    spot = lax.broadcasted_iota(jnp.int32, (rows, 128), 1)
    for b in range(slot_count):
        first = window_start(context_ref[b], arrived, size, span_rows)
        scores = join_rows(lax.dot_general(turned_ref[b], window_ref[b], NT, preferred_element_type=jnp.float32))
        column = lax.broadcasted_iota(jnp.int32, (1, size), 1) + first
        seen = (column >= context_ref[b] - arrived) & (column < limit_ref[b : b + 1, 0:1])
        scores = jnp.where(seen, scores, FAR)
        draft_scores = join_rows(lax.dot_general(turned_ref[b], drafts, NT, preferred_element_type=jnp.float32))
        draft_seen = (spot >= b * draft_count) & (spot <= b * draft_count + token)
        draft_scores = jnp.where(draft_seen, draft_scores, FAR)
        peak = jnp.maximum(jnp.max(scores, 1, keepdims=True), jnp.max(draft_scores, 1, keepdims=True))
        peak = jnp.maximum(peak, peak_ref[b])
        weights, draft_weights = jnp.exp2(scores - peak), jnp.exp2(draft_scores - peak)
        fade = jnp.exp2(peak_ref[b] - peak)
        new_peak_ref[b] = peak
        total = jnp.sum(weights, 1, keepdims=True) + jnp.sum(draft_weights, 1, keepdims=True)
        new_total_ref[b] = total_ref[b] * fade + total
        mixed = jnp.dot(split_rows(weights), window_ref[b], preferred_element_type=jnp.float32)
        mixed += jnp.dot(split_rows(draft_weights), drafts, preferred_element_type=jnp.float32)
        new_mixed_ref[b] = mixed_ref[b] * fade + join_rows(mixed)


def piece_sums(starts, spans, row_refs, refs):
    total = None
    for start, (n, first, depth) in zip(starts, spans):
        lanes = pl.ds(pl.multiple_of(start, HEAD_SIZE), depth)
        rows = [ref[:, lanes] for ref in row_refs]
        piece = refs[n][first : first + depth, :]
        product = jnp.dot(jnp.concatenate(rows, 0), piece, preferred_element_type=jnp.float32)
        total = product if total is None else total + product
    return total


def down_kernel(starts_of, spans, first, *refs):
    row_refs, refs, out_ref = refs[:4], refs[4:-1], refs[-1]
    total = piece_sums(starts_of(), spans, row_refs, refs)
    out_ref[...] = total if first else total + refs[-1][...]


def down_place_kernel(starts_of, spans, *refs):
    row_refs, refs, (keep_ref, send_ref) = refs[:4], refs[4:-2], refs[-2:]
    place_ref, sum_ref, refs = refs[0], refs[1], refs[2:]
    total = piece_sums(starts_of(), spans, row_refs, refs) + sum_ref[...]
    slots, width = keep_ref.shape[0] - 8, keep_ref.shape[1]
    count = place_ref.shape[1]
    parts = []
    left = total[:count]
    for _ in range(3):
        part = left.astype(jnp.bfloat16)
        parts.append(part)
        left = left - part.astype(jnp.float32)
    parts = jnp.concatenate(parts, 1)
    core = lax.axis_index("wide") % 2
    spot = lax.broadcasted_iota(jnp.int32, (slots, count), 0)
    for ref, target, draft in ((keep_ref, core, count), (send_ref, 1 - core, count + 16)):
        chosen = jnp.where(spot + target * slots == place_ref[...], 1.0, 0.0).astype(jnp.bfloat16)
        moved = jnp.dot(chosen, parts, preferred_element_type=jnp.float32)
        ref[:slots, :] = moved[:, :width] + moved[:, width : 2 * width] + moved[:, 2 * width :]
        ref[slots:, :] = total[draft : draft + 8]


def route_kernel(keep_ref, came_ref, draft_latent_ref, out_ref):
    slots = out_ref.shape[0]
    out_ref[...] = (keep_ref[:slots, :] + came_ref[:slots, :]).astype(jnp.bfloat16)
    drafts = keep_ref[slots:, :] + came_ref[slots:, :]
    draft_latent_ref[...] = drafts.astype(jnp.bfloat16).astype(jnp.float32)


def start_kernel(target_hbm, shard_hbm, draft_hbm, half_ref, full_ref, rows_ref, target_ref, draft_ref, sems):
    half_rows, shard_rows = half_ref.shape[0] - 16, full_ref.shape[0] - 16
    mine = pl.ds(pl.multiple_of(lax.axis_index("rep") * half_rows, half_rows), half_rows)
    copies = [
        pltpu.make_async_copy(target_hbm, target_ref, sems.at[0]),
        pltpu.make_async_copy(shard_hbm.at[mine], half_ref.at[:half_rows], sems.at[1]),
        pltpu.make_async_copy(shard_hbm, full_ref.at[:shard_rows], sems.at[2]),
        pltpu.make_async_copy(draft_hbm, draft_ref, sems.at[3]),
    ]
    for copy in copies:
        copy.start()
    width, count = half_ref.shape[1], target_ref.shape[1]
    copies[0].wait()
    hit = lax.broadcasted_iota(jnp.int32, (width, count), 0) == target_ref[...]
    hit = jnp.where(hit, 1.0, 0.0).astype(jnp.bfloat16)
    block = lax.dot_general(jnp.ones((16, count), jnp.bfloat16), hit, NT, preferred_element_type=jnp.float32)
    half_ref[half_rows:, :] = block.astype(jnp.bfloat16)
    full_ref[shard_rows:, :] = block.astype(jnp.bfloat16)
    copies[3].wait()
    rows = [draft_ref[b].astype(jnp.float32) for b in range(draft_ref.shape[0])]
    target = jnp.broadcast_to(target_ref[...].astype(jnp.float32), (8, count))
    rows.append(jnp.concatenate([target, jnp.zeros((8, rows_ref.shape[1] - count), jnp.float32)], 1))
    rows_ref[...] = jnp.concatenate(rows, 0).astype(jnp.bfloat16)
    for copy in copies[1:3]:
        copy.wait()


def join_kernel(one_ref, two_ref, *refs):
    rows, (out_ref, bare_ref) = one_ref.shape[0], refs[-2:]
    out_ref[:rows, :] = one_ref[...]
    out_ref[rows:, :] = two_ref[...]
    bare_ref[: rows - 16, :] = one_ref[: rows - 16, :]
    bare_ref[rows - 16 :, :] = two_ref[: rows - 16, :]


def append_kernel(one_ref, two_ref, out_ref):
    rows = one_ref.shape[0]
    out_ref[:rows, :] = one_ref[...]
    out_ref[rows:, :] = two_ref[: out_ref.shape[0] - rows, :]


def copy_kernel(spans, one_ref, *refs):
    done = 0
    for first, count in spans:
        refs[-1][done : done + count, :] = one_ref[first : first + count, :]
        done += count


def other_half_kernel(shard_ref, out_ref):
    rows = out_ref.shape[0]
    first = pl.multiple_of((1 - lax.axis_index("rep")) * rows, rows)
    out_ref[...] = shard_ref[pl.ds(first, rows), :]


def pack_kernel(spans, *refs):
    out_ref, width = refs[-1], refs[0].shape[1]
    for m, (n, first) in enumerate(spans):
        out_ref[:, m * width : (m + 1) * width] = refs[n][first : first + 16, :]


def count_kernel(most_rows, context_ref, mine_ref, other_ref, limit_ref, column_slot_ref):
    f32 = jnp.float32
    width = mine_ref.shape[1] // 8
    wide = lax.axis_index("wide")
    core = wide % 2
    mine, other = mine_ref[...].astype(f32), other_ref[...].astype(f32)
    low = jnp.where(core == 0, mine[:1], other[:1])
    high = jnp.where(core == 0, other[:1], mine[:1])
    counts = []
    for n in range(8):
        counts += [low[:, n * width : (n + 1) * width], high[:, n * width : (n + 1) * width]]
    counts = jnp.concatenate(counts, 0)
    lane = lax.broadcasted_iota(jnp.int32, counts.shape, 1)
    row = lax.broadcasted_iota(jnp.int32, counts.shape, 0)
    z, y = wide // 4, wide // 2 % 2
    chip = lane // (2 * most_rows)
    near, far, side = (chip // 2 + z) % 2, (chip // 4 + z // 2) % 2, (chip + y) % 2
    source = (near * 4 + far * 2 + side) * 2 + lane // most_rows % 2
    spread = []
    for b in range(2):
        number = jnp.sum(jnp.where(lane == wide * 2 + b, counts, 0.0), 1, keepdims=True)
        limit = context_ref[b] - jnp.sum(number, 0, keepdims=True).astype(jnp.int32)
        limit_ref[b : b + 1, :] = jnp.broadcast_to(limit, (1, limit_ref.shape[1]))
        spread.append(jnp.sum(jnp.where(source == row, number, 0.0), 0, keepdims=True).astype(jnp.int32))
    spot = lax.broadcasted_iota(jnp.int32, column_slot_ref.shape, 1) % most_rows
    column_slot_ref[...] = jnp.where(spot < spread[0], 0, jnp.where(spot >= most_rows - spread[1], 1, -1))


def place_kernel(most_rows, mine_ref, other_ref, place_ref):
    f32, bf16 = jnp.float32, jnp.bfloat16
    count = place_ref.shape[1] // 2
    core = lax.axis_index("wide") % 2
    earlier = lax.broadcasted_iota(jnp.int32, (count, count), 0) < lax.broadcasted_iota(jnp.int32, (count, count), 1)
    earlier = jnp.where(earlier, 1.0, 0.0).astype(bf16)
    for n, (ref, owner) in enumerate(((mine_ref, core), (other_ref, 1 - core))):
        target = ref[:, :count].astype(f32)[8:9].astype(jnp.int32)
        hit = jnp.where(lax.broadcasted_iota(jnp.int32, (64, count), 0) == target, 1.0, 0.0)
        before = jnp.dot(hit.astype(bf16), earlier, preferred_element_type=f32)
        rank = jnp.sum(hit * before, 0, keepdims=True).astype(jnp.int32)
        spot = jnp.where(target % 2 == 0, rank, most_rows - 1 - rank)
        chip, side = target // 4, target // 2 % 2
        place_ref[:, n * count : (n + 1) * count] = side * 2 * count + (chip * 2 + owner) * most_rows + spot


def plain_down_kernel(place_ref, prompt_ref, draft_ref, weight_ref, outgoing_ref, draft_latent_ref):
    count = prompt_ref.shape[0]
    rows = jnp.concatenate([prompt_ref[...], draft_ref[...]], 0)
    total = jnp.dot(rows, weight_ref[...], preferred_element_type=jnp.float32)
    draft_latent_ref[...] = total[count : count + 8].astype(jnp.bfloat16).astype(jnp.float32)
    spot = lax.broadcasted_iota(jnp.int32, (outgoing_ref.shape[0], count), 0)
    chosen = jnp.where(spot == place_ref[...], 1.0, 0.0).astype(jnp.bfloat16)
    latent = total[:count].astype(jnp.bfloat16)
    outgoing_ref[...] = jnp.dot(chosen, latent, preferred_element_type=jnp.float32).astype(jnp.bfloat16)


def late_kernel(column_slot_ref, turned_ref, peak_ref, total_ref, mixed_ref, value_up_ref, *refs):
    incoming_refs, (out_ref, rows_ref, parted_ref) = refs[:-3], refs[-3:]
    slot_count, draft_count, _ = out_ref.shape
    heads_kv = value_up_ref.shape[1] // HEAD_SIZE
    group_size = QUERY_HEADS // heads_kv
    head_rows = group_size * draft_count
    rows = peak_ref.shape[1]
    block = incoming_refs[0].shape[0]
    for n, ref in enumerate(incoming_refs):
        rows_ref[n * block : (n + 1) * block, :] = ref[...]
    ones = jnp.ones((rows_ref.shape[0], HEAD_SIZE), jnp.bfloat16)
    for b in range(slot_count):
        scores = join_rows(lax.dot_general(turned_ref[b], rows_ref[...], NT, preferred_element_type=jnp.float32))
        scores = jnp.where(column_slot_ref[...] == b, scores, FAR)
        peak = jnp.maximum(jnp.max(scores, 1, keepdims=True), peak_ref[b])
        weights = split_rows(jnp.exp2(scores - peak))
        fade = jnp.exp2(peak_ref[b] - peak)
        added = join_rows(jnp.dot(weights, ones, preferred_element_type=jnp.float32))
        total = total_ref[b] * fade + added[:, :1]
        mixed = join_rows(jnp.dot(weights, rows_ref[...], preferred_element_type=jnp.float32))
        parted_ref[b] = split_rows((mixed_ref[b] * fade + mixed) * (1.0 / total))
    for k in range(heads_kv):
        part = []
        for b in range(slot_count):
            part.append(parted_ref[b, k * head_rows : (k + 1) * head_rows, :])
            part.append(parted_ref[b, rows + k * head_rows : rows + (k + 1) * head_rows, :])
        value_up = value_up_ref[:, k * HEAD_SIZE : (k + 1) * HEAD_SIZE]
        both = jnp.dot(jnp.concatenate(part, 0), value_up, preferred_element_type=jnp.float32)
        for b in range(slot_count):
            result = join_rows(both[b * 2 * head_rows : (b + 1) * 2 * head_rows])
            wide = jnp.concatenate(
                [result[g * draft_count : (g + 1) * draft_count] for g in range(group_size)], 1
            )
            out_ref[b, :, k * group_size * HEAD_SIZE : (k + 1) * group_size * HEAD_SIZE] = wide.astype(jnp.bfloat16)


def deliver(prompt_hidden, draft_hidden, shard, row_target, context_len, held):
    shard_rows, width = shard.shape
    count = prompt_hidden.shape[0]
    spots = [(r, z, y, c) for r in range(2) for z in range(4) for y in range(2) for c in range(2)]
    most_rows = count // 8
    f32, bf16 = jnp.float32, jnp.bfloat16

    def flat(spot):
        return ((spot[0] * 4 + spot[1]) * 2 + spot[2]) * 2 + spot[3]

    def swap(x, r=0, z=0, y=0, c=0):
        pairs = [(flat(spot), flat([a ^ b for a, b in zip(spot, (r, z, y, c))])) for spot in spots]
        return lax.ppermute(x, ("rep", "wide"), pairs)

    def array(rows, dtype=bf16):
        return jax.ShapeDtypeStruct((rows, width), dtype)

    def call(kernel, out_shape, name, *operands, specs=None, flops=2**20, **more):
        return pl.pallas_call(
            kernel,
            out_shape=out_shape,
            in_specs=specs or [WHOLE] * len(operands),
            out_specs=[WHOLE] * len(out_shape) if isinstance(out_shape, list) else WHOLE,
            compiler_params=params(16),
            cost_estimate=pl.CostEstimate(flops=flops, bytes_accessed=2**16, transcendentals=0),
            name=name,
            **more,
        )(*operands)

    hbm = pl.BlockSpec(memory_space=pltpu.HBM)
    half_rows = shard_rows // 2
    ext = half_rows + 16
    half, full, draft_rows = call(
        start_kernel,
        [
            array(ext),
            array(shard_rows + 16),
            jax.ShapeDtypeStruct((16, draft_hidden.shape[2]), bf16),
        ],
        "start_rows",
        *(pltpu.with_memory_space_constraint(x, pltpu.HBM) for x in (row_target.reshape(1, count), shard, draft_hidden)),
        specs=[hbm] * 3,
        scratch_shapes=[
            pltpu.VMEM((1, count), jnp.int32), pltpu.VMEM(draft_hidden.shape, bf16), pltpu.SemaphoreType.DMA((4,))
        ],
    )
    za, zb = swap(half, z=1), swap(half, z=2)
    y0 = swap(full, y=1)
    other_prompt, other_drafts = swap(prompt_hidden, c=1), swap(draft_rows, c=1)

    def copy(x, spans, *ties):
        return call(
            functools.partial(copy_kernel, spans), array(sum(rows for _, rows in spans)), "copy_piece", x, *ties,
            specs=[WHOLE] + [UNREAD] * len(ties),
        )

    rest = call(other_half_kernel, array(half_rows), "other_half", y0)
    db = swap(rest, z=2)
    zab, bare = call(
        join_kernel, [array(2 * ext), array(2 * half_rows)], "join_pieces", za, zb, other_drafts, held,
        specs=[WHOLE] * 2 + [UNREAD] * 2,
    )
    yab, xab = swap(zab, y=1), swap(bare, r=1)
    quarter = half_rows // 2
    zc = swap(call(append_kernel, array(ext + quarter), "append_piece", zb, rest), z=1)
    dc = swap(db, z=1)
    xc = swap(copy(zc, [(0, half_rows)]), r=1)
    xya = swap(copy(yab, [(quarter, quarter)]), r=1)
    yc = swap(copy(zc, [(0, ext)], yab), y=1)

    order = [
        (half, half_rows), (y0, shard_rows), (zab, ext + half_rows), (yab, ext + half_rows),
        (zab, half_rows), (yab, half_rows), (zc, half_rows), (yc, half_rows),
    ]
    pack = call(
        functools.partial(pack_kernel, [(n, first) for n, (_, first) in enumerate(order)]),
        jax.ShapeDtypeStruct((16, len(order) * width), bf16), "pack_rows", *(x for x, _ in order),
    )
    other_pack = swap(pack, c=1)
    limit, column_slot = call(
        functools.partial(count_kernel, most_rows),
        [jax.ShapeDtypeStruct((2, 128), jnp.int32), jax.ShapeDtypeStruct((1, 2 * count), jnp.int32)],
        "count_rows", context_len, pack, other_pack,
        specs=[SCALARS, WHOLE, WHOLE],
    )
    place = call(
        functools.partial(place_kernel, most_rows), jax.ShapeDtypeStruct((1, 2 * count), jnp.int32), "place_rows",
        draft_rows, other_drafts,
    )

    def starts_of(uses):
        def starts():
            rep, wide = lax.axis_index("rep"), lax.axis_index("wide")
            z, y, c = wide // 4, wide // 2 % 2, wide % 2
            found = []
            for _, _, _, (x_step, z_step, y_step), *further in uses:
                owner_z = (z // 2 + z_step // 2) % 2 * 2 + (z + z_step) % 2
                owner = (owner_z * 2 + (y + y_step) % 2) * 2 + c
                start = owner * shard_rows + (0 if x_step is None else (rep + x_step) % 2 * half_rows)
                found.append(start + sum(further))
            return found

        return starts

    rows = [prompt_hidden, other_prompt, draft_rows, other_drafts]
    stages = [
        ([full, y0], [(0, 0, shard_rows, (None, 0, 0)), (1, 0, shard_rows, (None, 0, 1))]),
        (
            [zab, yab],
            [(0, 0, half_rows, (0, 1, 0)), (0, ext, half_rows, (0, 2, 0)),
             (1, 0, half_rows, (0, 1, 1)), (1, ext, half_rows, (0, 2, 1))],
        ),
        (
            [xab, zc, xc],
            [(0, 0, half_rows, (1, 1, 0)), (0, half_rows, half_rows, (1, 2, 0)), (1, 0, half_rows, (0, 3, 0)),
             (1, ext, quarter, (1, 1, 1)), (2, 0, half_rows, (1, 3, 0))],
        ),
        (
            [yc, xya, db, dc],
            [(0, 0, half_rows, (0, 3, 1)), (1, 0, quarter, (1, 1, 1), quarter), (2, 0, half_rows, (1, 2, 1)),
             (3, 0, half_rows, (1, 3, 1))],
        ),
    ]
    sums = []
    total_rows = 2 * count + 32
    for n, (pieces, uses) in enumerate(stages[:-1]):
        sums = [
            call(
                functools.partial(down_kernel, starts_of(uses), [use[:3] for use in uses], n == 0),
                array(total_rows, f32), "down_rows", *rows, *pieces, *sums, flops=2**26,
            )
        ]

    def finish():
        pieces, uses = stages[-1]
        keep, send = call(
            functools.partial(down_place_kernel, starts_of(uses), [use[:3] for use in uses]),
            [array(2 * count + 8, f32)] * 2, "down_place_rows", *rows, place, *sums, *pieces, flops=2**26,
        )
        came = swap(send, c=1)
        draft_latent, outgoing = call(route_kernel, [array(8, f32), array(2 * count)], "route_rows", keep, came)
        incoming = lax.all_to_all(
            outgoing.reshape(8, 2 * most_rows, width), "wide", split_axis=0, concat_axis=0, tiled=True,
            axis_index_groups=[list(range(c, 16, 2)) for c in range(2)],
        )
        return draft_latent, [incoming.reshape(2 * count, width)]

    return limit, column_slot, finish


def deliver_plain(prompt_hidden, draft_hidden, shard, row_target, context_len, held):
    wide_size = lax.axis_size("wide")
    row_count = prompt_hidden.shape[0]
    slot_count, draft_count, _ = draft_hidden.shape
    latent_width = shard.shape[1]
    most_rows = 2 * ((row_count + wide_size - 1) // wide_size)
    arrived = wide_size * most_rows
    weight = lax.all_gather(shard, "wide", axis=0, tiled=True)
    index = jnp.arange(row_count, dtype=jnp.int32)
    same = (row_target[:, None] == row_target[None, :]) & (index[None, :] < index[:, None])
    rank = jnp.sum(same.astype(jnp.int32), 1)
    front = row_target % slot_count == 0
    place = row_target // slot_count * most_rows + jnp.where(front, rank, most_rows - 1 - rank)
    request = jnp.arange(wide_size * slot_count, dtype=jnp.int32)
    counts = jnp.sum((row_target[None, :] == request[:, None]).astype(jnp.int32), 1)
    counts = lax.all_to_all(counts.reshape(wide_size, slot_count), "wide", split_axis=0, concat_axis=0, tiled=True)
    limit = jnp.broadcast_to((context_len - jnp.sum(counts, 0))[:, None], (slot_count, 128))
    spot = jnp.arange(most_rows, dtype=jnp.int32)[None, :]
    column_slot = jnp.where(
        spot < counts[:, 0:1], 0, jnp.where(spot >= most_rows - counts[:, 1:2], 1, -1)
    ).reshape(1, arrived)

    tile = slot_count * draft_count
    draft_flat = jnp.pad(draft_hidden.reshape(tile, draft_hidden.shape[2]), ((0, 16 - tile), (0, 0)))

    def finish():
        outgoing, draft_latent = pl.pallas_call(
            plain_down_kernel,
            out_shape=[
                jax.ShapeDtypeStruct((arrived, latent_width), jnp.bfloat16),
                jax.ShapeDtypeStruct((slot_count * draft_count, latent_width), jnp.float32),
            ],
            in_specs=[WHOLE] * 4,
            out_specs=[WHOLE] * 2,
            compiler_params=params(24),
            name="down_rows",
        )(place.reshape(1, row_count), prompt_hidden, draft_flat, weight)
        incoming = lax.all_to_all(
            outgoing.reshape(wide_size, most_rows, latent_width), "wide", split_axis=0, concat_axis=0, tiled=True
        )
        return draft_latent, [incoming.reshape(arrived, latent_width)]

    return limit, column_slot, finish


def local(
    prompt_hidden,
    resident_latent,
    row_target,
    row_offset,
    context_len,
    draft_hidden,
    draft_query_heads,
    down_weight,
    key_up_weight,
    value_up_weight,
):
    f32, bf16 = jnp.float32, jnp.bfloat16
    slot_count, span_rows, latent_width = resident_latent.shape
    draft_count = draft_hidden.shape[1]
    rows = QUERY_HEADS * draft_count
    wide_size, row_count = lax.axis_size("wide"), prompt_hidden.shape[0]
    arrived = 2 * ((row_count + wide_size - 1) // wide_size) * wide_size
    window = min(arrived + 128, span_rows)
    hbm = pl.BlockSpec(memory_space=pltpu.HBM)
    stats = [
        jax.ShapeDtypeStruct((slot_count, rows, 1), f32),
        jax.ShapeDtypeStruct((slot_count, rows, 1), f32),
        jax.ShapeDtypeStruct((slot_count, rows, latent_width), f32),
    ]
    turned, peak, total, mixed, edge = pl.pallas_call(
        functools.partial(held_kernel, arrived),
        out_shape=[
            jax.ShapeDtypeStruct((slot_count, 2 * rows, latent_width), bf16),
            *stats,
            jax.ShapeDtypeStruct((slot_count, window, latent_width), bf16),
        ],
        in_specs=[SCALARS, hbm, hbm, hbm],
        out_specs=[WHOLE] * 5,
        scratch_shapes=[
            pltpu.VMEM(draft_query_heads.shape, bf16),
            pltpu.VMEM(key_up_weight.shape, bf16),
            pltpu.VMEM(resident_latent.shape, bf16),
            pltpu.VMEM((slot_count, rows, latent_width), f32),
            pltpu.VMEM((rows, span_rows), f32),
            pltpu.SemaphoreType.DMA((3,)),
        ],
        compiler_params=params(16),
        cost_estimate=pl.CostEstimate(flops=2**31, bytes_accessed=2**21, transcendentals=0),
        name="held_rows",
    )(context_len, *(pltpu.with_memory_space_constraint(x, pltpu.HBM) for x in (draft_query_heads, key_up_weight, resident_latent)))
    known = wide_size == 16 and lax.axis_size("rep") == 2
    limit, column_slot, finish = (deliver if known else deliver_plain)(
        prompt_hidden, draft_hidden, down_weight, row_target, context_len, peak
    )
    draft_latent, incoming = finish()
    peak, total, mixed = pl.pallas_call(
        functools.partial(window_kernel, arrived, span_rows, draft_count),
        out_shape=stats,
        in_specs=[SCALARS] + [WHOLE] * 7,
        out_specs=[WHOLE] * 3,
        compiler_params=params(16),
        cost_estimate=pl.CostEstimate(flops=2**30, bytes_accessed=2**16, transcendentals=0),
        name="window_rows",
    )(context_len, limit, turned, peak, total, mixed, edge, draft_latent)
    return pl.pallas_call(
        late_kernel,
        out_shape=jax.ShapeDtypeStruct((slot_count, draft_count, QUERY_HEADS * HEAD_SIZE), bf16),
        in_specs=[WHOLE] * (6 + len(incoming)),
        out_specs=WHOLE,
        scratch_shapes=[
            pltpu.VMEM((arrived, latent_width), bf16),
            pltpu.VMEM((slot_count, 2 * rows, latent_width), bf16),
        ],
        compiler_params=params(16),
        name="late_rows",
    )(column_slot, turned, peak, total, mixed, value_up_weight, *incoming)


def solution(mesh):
    placed = (
        P(("rep", "wide"), None),
        P(("rep", "wide"), None, None),
        P(("rep", "wide")),
        P(("rep", "wide")),
        P(("rep", "wide")),
        P(("rep", "wide"), None, None),
        P(("rep", "wide"), None, None),
        P("wide", None),
        P(),
        P(),
    )
    return jax.shard_map(
        local, mesh=mesh, in_specs=placed, out_specs=P(("rep", "wide"), None, None), check_vma=False
    )
```

```python
import functools
import math

import jax
import jax.numpy as jnp
from jax import lax
from jax.experimental import pallas as pl
from jax.experimental.pallas import tpu as pltpu
from jax.sharding import PartitionSpec as P

QUERY_HEADS = 64
HEAD_SIZE = 128
FAR = -1e30
NT = (((1,), (1,)), ((), ()))
WHOLE = pl.BlockSpec(memory_space=pltpu.VMEM)
SCALARS = pl.BlockSpec(memory_space=pltpu.SMEM)
UNREAD = pl.BlockSpec(memory_space=pl.ANY)


def params(mib):
    return pltpu.CompilerParams(vmem_limit_bytes=mib * 1024 * 1024)


def split_rows(x):
    top = x.astype(jnp.bfloat16)
    rest = (x - top.astype(jnp.float32)).astype(jnp.bfloat16)
    return jnp.concatenate([top, rest], 0)


def join_rows(x):
    half = x.shape[0] // 2
    return x[:half] + x[half:]


def held_kernel(
    arrived, context_ref, query_hbm, key_up_hbm, cache_hbm, turned_ref, peak_ref, total_ref, mixed_ref, window_ref,
    query_ref, key_up_ref, cache_ref, float_ref, scores_ref, sems,
):
    copies = [
        pltpu.make_async_copy(source, target, sems.at[n])
        for n, (source, target) in enumerate(
            [(query_hbm, query_ref), (key_up_hbm, key_up_ref), (cache_hbm, cache_ref)]
        )
    ]
    for copy in copies:
        copy.start()
    slot_count, span_rows, _ = cache_ref.shape
    draft_count = query_ref.shape[1]
    heads_kv = key_up_ref.shape[1] // HEAD_SIZE
    group_size = QUERY_HEADS // heads_kv
    rows = group_size * draft_count
    scale = math.log2(math.e) / math.sqrt(HEAD_SIZE)
    step = 256
    copies[0].wait()
    copies[1].wait()
    for k in range(heads_kv):
        pieces = []
        for b in range(slot_count):
            for g in range(group_size):
                lane = (k * group_size + g) * HEAD_SIZE
                pieces.append(query_ref[b, :, lane : lane + HEAD_SIZE].astype(jnp.float32))
        query = jnp.concatenate(pieces, 0).astype(jnp.bfloat16)
        key_up = key_up_ref[:, k * HEAD_SIZE : (k + 1) * HEAD_SIZE]
        turned = lax.dot_general(query, key_up, NT, preferred_element_type=jnp.float32) * scale
        for b in range(slot_count):
            float_ref[b, k * rows : (k + 1) * rows, :] = turned[b * rows : (b + 1) * rows]
    copies[2].wait()
    for b in range(slot_count):
        first = pl.multiple_of(window_start(context_ref[b], arrived, window_ref.shape[1], span_rows), 128)
        window_ref[b] = cache_ref[b, pl.ds(first, window_ref.shape[1]), :]
        turned_ref[b] = split_rows(float_ref[b])
        peak = None
        for c in range(0, span_rows, step):
            scores = join_rows(
                lax.dot_general(turned_ref[b], cache_ref[b, c : c + step], NT, preferred_element_type=jnp.float32)
            )
            column = lax.broadcasted_iota(jnp.int32, (1, step), 1) + c
            scores = jnp.where(column < context_ref[b] - arrived, scores, FAR)
            scores_ref[:, c : c + step] = scores
            top = jnp.max(scores, 1, keepdims=True)
            peak = top if peak is None else jnp.maximum(peak, top)
        peak_ref[b] = peak
        total = jnp.zeros_like(peak)
        mixed = jnp.zeros(mixed_ref.shape[1:], jnp.float32)
        for c in range(0, span_rows, step):
            weights = jnp.exp2(scores_ref[:, c : c + step] - peak)
            total += jnp.sum(weights, 1, keepdims=True)
            mixed += join_rows(
                jnp.dot(split_rows(weights), cache_ref[b, c : c + step], preferred_element_type=jnp.float32)
            )
        total_ref[b] = total
        mixed_ref[b] = mixed


def window_start(context, arrived, size, span_rows):
    return jnp.clip((context - arrived) // 128 * 128, 0, span_rows - size)


def window_kernel(
    arrived, span_rows, draft_count, context_ref, limit_ref, turned_ref, peak_ref, total_ref, mixed_ref, window_ref,
    draft_latent_ref, new_peak_ref, new_total_ref, new_mixed_ref,
):
    slot_count, size, width = window_ref.shape
    rows = peak_ref.shape[1]
    drafts = draft_latent_ref[...]
    drafts = jnp.concatenate([drafts, jnp.zeros((128 - drafts.shape[0], width), jnp.float32)], 0).astype(jnp.bfloat16)
    token = lax.broadcasted_iota(jnp.int32, (rows, 1), 0) % draft_count
    spot = lax.broadcasted_iota(jnp.int32, (rows, 128), 1)
    for b in range(slot_count):
        first = window_start(context_ref[b], arrived, size, span_rows)
        scores = join_rows(lax.dot_general(turned_ref[b], window_ref[b], NT, preferred_element_type=jnp.float32))
        column = lax.broadcasted_iota(jnp.int32, (1, size), 1) + first
        seen = (column >= context_ref[b] - arrived) & (column < limit_ref[b : b + 1, 0:1])
        scores = jnp.where(seen, scores, FAR)
        draft_scores = join_rows(lax.dot_general(turned_ref[b], drafts, NT, preferred_element_type=jnp.float32))
        draft_seen = (spot >= b * draft_count) & (spot <= b * draft_count + token)
        draft_scores = jnp.where(draft_seen, draft_scores, FAR)
        peak = jnp.maximum(jnp.max(scores, 1, keepdims=True), jnp.max(draft_scores, 1, keepdims=True))
        peak = jnp.maximum(peak, peak_ref[b])
        weights, draft_weights = jnp.exp2(scores - peak), jnp.exp2(draft_scores - peak)
        fade = jnp.exp2(peak_ref[b] - peak)
        new_peak_ref[b] = peak
        total = jnp.sum(weights, 1, keepdims=True) + jnp.sum(draft_weights, 1, keepdims=True)
        new_total_ref[b] = total_ref[b] * fade + total
        mixed = jnp.dot(split_rows(weights), window_ref[b], preferred_element_type=jnp.float32)
        mixed += jnp.dot(split_rows(draft_weights), drafts, preferred_element_type=jnp.float32)
        new_mixed_ref[b] = mixed_ref[b] * fade + join_rows(mixed)


def piece_sums(starts, spans, row_refs, refs):
    total = None
    for start, (n, first, depth) in zip(starts, spans):
        lanes = pl.ds(pl.multiple_of(start, HEAD_SIZE), depth)
        rows = [ref[:, lanes] for ref in row_refs]
        piece = refs[n][first : first + depth, :]
        product = jnp.dot(jnp.concatenate(rows, 0), piece, preferred_element_type=jnp.float32)
        total = product if total is None else total + product
    return total


def down_kernel(starts_of, spans, first, *refs):
    row_refs, refs, out_ref = refs[:4], refs[4:-1], refs[-1]
    total = piece_sums(starts_of(), spans, row_refs, refs)
    out_ref[...] = total if first else total + refs[-1][...]


def down_place_kernel(starts_of, spans, *refs):
    row_refs, refs, (keep_ref, send_ref) = refs[:4], refs[4:-2], refs[-2:]
    place_ref, sum_ref, refs = refs[0], refs[1], refs[2:]
    total = piece_sums(starts_of(), spans, row_refs, refs) + sum_ref[...]
    slots, width = keep_ref.shape[0] - 8, keep_ref.shape[1]
    count = place_ref.shape[1]
    parts = []
    left = total[:count]
    for _ in range(2):
        part = left.astype(jnp.bfloat16)
        parts.append(part)
        left = left - part.astype(jnp.float32)
    parts = jnp.concatenate(parts, 1)
    core = lax.axis_index("wide") % 2
    spot = lax.broadcasted_iota(jnp.int32, (slots, count), 0)
    for ref, target, draft in ((keep_ref, core, count), (send_ref, 1 - core, count + 16)):
        chosen = jnp.where(spot + target * slots == place_ref[...], 1.0, 0.0).astype(jnp.bfloat16)
        moved = jnp.dot(chosen, parts, preferred_element_type=jnp.float32)
        ref[:slots, :] = moved[:, :width] + moved[:, width:]
        ref[slots:, :] = total[draft : draft + 8]


def route_kernel(keep_ref, came_ref, draft_latent_ref, out_ref):
    slots = out_ref.shape[0]
    out_ref[...] = (keep_ref[:slots, :] + came_ref[:slots, :]).astype(jnp.bfloat16)
    drafts = keep_ref[slots:, :] + came_ref[slots:, :]
    draft_latent_ref[...] = drafts.astype(jnp.bfloat16).astype(jnp.float32)


def start_kernel(target_hbm, shard_hbm, draft_hbm, half_ref, full_ref, rows_ref, target_ref, draft_ref, sems):
    half_rows, shard_rows = half_ref.shape[0] - 16, full_ref.shape[0] - 16
    mine = pl.ds(pl.multiple_of(lax.axis_index("rep") * half_rows, half_rows), half_rows)
    copies = [
        pltpu.make_async_copy(target_hbm, target_ref, sems.at[0]),
        pltpu.make_async_copy(shard_hbm.at[mine], half_ref.at[:half_rows], sems.at[1]),
        pltpu.make_async_copy(shard_hbm, full_ref.at[:shard_rows], sems.at[2]),
        pltpu.make_async_copy(draft_hbm, draft_ref, sems.at[3]),
    ]
    for copy in copies:
        copy.start()
    width, count = half_ref.shape[1], target_ref.shape[1]
    copies[0].wait()
    hit = lax.broadcasted_iota(jnp.int32, (width, count), 0) == target_ref[...]
    hit = jnp.where(hit, 1.0, 0.0).astype(jnp.bfloat16)
    block = lax.dot_general(jnp.ones((16, count), jnp.bfloat16), hit, NT, preferred_element_type=jnp.float32)
    half_ref[half_rows:, :] = block.astype(jnp.bfloat16)
    full_ref[shard_rows:, :] = block.astype(jnp.bfloat16)
    copies[3].wait()
    rows = [draft_ref[b].astype(jnp.float32) for b in range(draft_ref.shape[0])]
    target = jnp.broadcast_to(target_ref[...].astype(jnp.float32), (8, count))
    rows.append(jnp.concatenate([target, jnp.zeros((8, rows_ref.shape[1] - count), jnp.float32)], 1))
    rows_ref[...] = jnp.concatenate(rows, 0).astype(jnp.bfloat16)
    for copy in copies[1:3]:
        copy.wait()


def join_kernel(one_ref, two_ref, *refs):
    rows, (out_ref, bare_ref) = one_ref.shape[0], refs[-2:]
    out_ref[:rows, :] = one_ref[...]
    out_ref[rows:, :] = two_ref[...]
    bare_ref[: rows - 16, :] = one_ref[: rows - 16, :]
    bare_ref[rows - 16 :, :] = two_ref[: rows - 16, :]


def copy_kernel(spans, one_ref, *refs):
    done = 0
    for first, count in spans:
        refs[-1][done : done + count, :] = one_ref[first : first + count, :]
        done += count


def other_half_kernel(shard_ref, out_ref):
    rows = out_ref.shape[0]
    first = pl.multiple_of((1 - lax.axis_index("rep")) * rows, rows)
    out_ref[...] = shard_ref[pl.ds(first, rows), :]


def pack_kernel(spans, *refs):
    out_ref, width = refs[-1], refs[0].shape[1]
    for m, (n, first) in enumerate(spans):
        out_ref[:, m * width : (m + 1) * width] = refs[n][first : first + 16, :]


def count_kernel(most_rows, context_ref, mine_ref, other_ref, limit_ref, column_slot_ref):
    f32 = jnp.float32
    width = mine_ref.shape[1] // 8
    wide = lax.axis_index("wide")
    core = wide % 2
    mine, other = mine_ref[...].astype(f32), other_ref[...].astype(f32)
    low = jnp.where(core == 0, mine[:1], other[:1])
    high = jnp.where(core == 0, other[:1], mine[:1])
    counts = []
    for n in range(8):
        counts += [low[:, n * width : (n + 1) * width], high[:, n * width : (n + 1) * width]]
    counts = jnp.concatenate(counts, 0)
    lane = lax.broadcasted_iota(jnp.int32, counts.shape, 1)
    row = lax.broadcasted_iota(jnp.int32, counts.shape, 0)
    z, y = wide // 4, wide // 2 % 2
    chip = lane // (2 * most_rows)
    near, far, side = (chip // 2 + z) % 2, (chip // 4 + z // 2) % 2, (chip + y) % 2
    source = (near * 4 + far * 2 + side) * 2 + lane // most_rows % 2
    spread = []
    for b in range(2):
        number = jnp.sum(jnp.where(lane == wide * 2 + b, counts, 0.0), 1, keepdims=True)
        limit = context_ref[b] - jnp.sum(number, 0, keepdims=True).astype(jnp.int32)
        limit_ref[b : b + 1, :] = jnp.broadcast_to(limit, (1, limit_ref.shape[1]))
        spread.append(jnp.sum(jnp.where(source == row, number, 0.0), 0, keepdims=True).astype(jnp.int32))
    spot = lax.broadcasted_iota(jnp.int32, column_slot_ref.shape, 1) % most_rows
    column_slot_ref[...] = jnp.where(spot < spread[0], 0, jnp.where(spot >= most_rows - spread[1], 1, -1))


def place_kernel(most_rows, mine_ref, other_ref, place_ref):
    f32, bf16 = jnp.float32, jnp.bfloat16
    count = place_ref.shape[1] // 2
    core = lax.axis_index("wide") % 2
    earlier = lax.broadcasted_iota(jnp.int32, (count, count), 0) < lax.broadcasted_iota(jnp.int32, (count, count), 1)
    earlier = jnp.where(earlier, 1.0, 0.0).astype(bf16)
    for n, (ref, owner) in enumerate(((mine_ref, core), (other_ref, 1 - core))):
        target = ref[:, :count].astype(f32)[8:9].astype(jnp.int32)
        hit = jnp.where(lax.broadcasted_iota(jnp.int32, (64, count), 0) == target, 1.0, 0.0)
        before = jnp.dot(hit.astype(bf16), earlier, preferred_element_type=f32)
        rank = jnp.sum(hit * before, 0, keepdims=True).astype(jnp.int32)
        spot = jnp.where(target % 2 == 0, rank, most_rows - 1 - rank)
        chip, side = target // 4, target // 2 % 2
        place_ref[:, n * count : (n + 1) * count] = side * 2 * count + (chip * 2 + owner) * most_rows + spot


def plain_down_kernel(place_ref, prompt_ref, draft_ref, weight_ref, outgoing_ref, draft_latent_ref):
    count = prompt_ref.shape[0]
    rows = jnp.concatenate([prompt_ref[...], draft_ref[...]], 0)
    total = jnp.dot(rows, weight_ref[...], preferred_element_type=jnp.float32)
    draft_latent_ref[...] = total[count : count + 8].astype(jnp.bfloat16).astype(jnp.float32)
    spot = lax.broadcasted_iota(jnp.int32, (outgoing_ref.shape[0], count), 0)
    chosen = jnp.where(spot == place_ref[...], 1.0, 0.0).astype(jnp.bfloat16)
    latent = total[:count].astype(jnp.bfloat16)
    outgoing_ref[...] = jnp.dot(chosen, latent, preferred_element_type=jnp.float32).astype(jnp.bfloat16)


def late_kernel(column_slot_ref, turned_ref, peak_ref, total_ref, mixed_ref, value_up_ref, *refs):
    incoming_refs, (out_ref, rows_ref, mixed_latent_ref) = refs[:-3], refs[-3:]
    slot_count, draft_count, _ = out_ref.shape
    heads_kv = value_up_ref.shape[1] // HEAD_SIZE
    group_size = QUERY_HEADS // heads_kv
    head_rows = group_size * draft_count
    rows = peak_ref.shape[1]
    block = incoming_refs[0].shape[0]
    for n, ref in enumerate(incoming_refs):
        rows_ref[n * block : (n + 1) * block, :] = ref[...]
    ones = jnp.ones((rows_ref.shape[0], HEAD_SIZE), jnp.bfloat16)
    for b in range(slot_count):
        scores = join_rows(lax.dot_general(turned_ref[b], rows_ref[...], NT, preferred_element_type=jnp.float32))
        scores = jnp.where(column_slot_ref[...] == b, scores, FAR)
        peak = jnp.maximum(jnp.max(scores, 1, keepdims=True), peak_ref[b])
        weights = jnp.exp2(scores - peak).astype(jnp.bfloat16)
        fade = jnp.exp2(peak_ref[b] - peak)
        added = jnp.dot(weights, ones, preferred_element_type=jnp.float32)
        total = total_ref[b] * fade + added[:, :1]
        mixed = jnp.dot(weights, rows_ref[...], preferred_element_type=jnp.float32)
        mixed_latent_ref[b] = ((mixed_ref[b] * fade + mixed) * (1.0 / total)).astype(jnp.bfloat16)
    for k in range(heads_kv):
        part = [mixed_latent_ref[b, k * head_rows : (k + 1) * head_rows, :] for b in range(slot_count)]
        value_up = value_up_ref[:, k * HEAD_SIZE : (k + 1) * HEAD_SIZE]
        both = jnp.dot(jnp.concatenate(part, 0), value_up, preferred_element_type=jnp.float32)
        for b in range(slot_count):
            result = both[b * head_rows : (b + 1) * head_rows]
            wide = jnp.concatenate(
                [result[g * draft_count : (g + 1) * draft_count] for g in range(group_size)], 1
            )
            out_ref[b, :, k * group_size * HEAD_SIZE : (k + 1) * group_size * HEAD_SIZE] = wide.astype(jnp.bfloat16)


def deliver(prompt_hidden, draft_hidden, shard, row_target, context_len, held):
    shard_rows, width = shard.shape
    count = prompt_hidden.shape[0]
    spots = [(r, z, y, c) for r in range(2) for z in range(4) for y in range(2) for c in range(2)]
    most_rows = count // 8
    f32, bf16 = jnp.float32, jnp.bfloat16

    def flat(spot):
        return ((spot[0] * 4 + spot[1]) * 2 + spot[2]) * 2 + spot[3]

    def swap(x, r=0, z=0, y=0, c=0):
        pairs = [(flat(spot), flat([a ^ b for a, b in zip(spot, (r, z, y, c))])) for spot in spots]
        return lax.ppermute(x, ("rep", "wide"), pairs)

    def array(rows, dtype=bf16):
        return jax.ShapeDtypeStruct((rows, width), dtype)

    def call(kernel, out_shape, name, *operands, specs=None, flops=2**20, **more):
        return pl.pallas_call(
            kernel,
            out_shape=out_shape,
            in_specs=specs or [WHOLE] * len(operands),
            out_specs=[WHOLE] * len(out_shape) if isinstance(out_shape, list) else WHOLE,
            compiler_params=params(16),
            cost_estimate=pl.CostEstimate(flops=flops, bytes_accessed=2**16, transcendentals=0),
            name=name,
            **more,
        )(*operands)

    hbm = pl.BlockSpec(memory_space=pltpu.HBM)
    half_rows = shard_rows // 2
    ext = half_rows + 16
    half, full, draft_rows = call(
        start_kernel,
        [
            array(ext),
            array(shard_rows + 16),
            jax.ShapeDtypeStruct((16, draft_hidden.shape[2]), bf16),
        ],
        "start_rows",
        *(pltpu.with_memory_space_constraint(x, pltpu.HBM) for x in (row_target.reshape(1, count), shard, draft_hidden)),
        specs=[hbm] * 3,
        scratch_shapes=[
            pltpu.VMEM((1, count), jnp.int32), pltpu.VMEM(draft_hidden.shape, bf16), pltpu.SemaphoreType.DMA((4,))
        ],
    )
    za, zb = swap(half, z=1), swap(half, z=2)
    y0 = swap(full, y=1)
    other_prompt, other_drafts = swap(prompt_hidden, c=1), swap(draft_rows, c=1)

    def copy(x, spans, *ties):
        return call(
            functools.partial(copy_kernel, spans), array(sum(rows for _, rows in spans)), "copy_piece", x, *ties,
            specs=[WHOLE] + [UNREAD] * len(ties),
        )

    rest = call(other_half_kernel, array(half_rows), "other_half", y0)
    db = swap(rest, z=2)
    zab, bare = call(
        join_kernel, [array(2 * ext), array(2 * half_rows)], "join_pieces", za, zb, other_drafts, held,
        specs=[WHOLE] * 2 + [UNREAD] * 2,
    )
    yab, xab = swap(zab, y=1), swap(bare, r=1)
    zc, dc = swap(zb, z=1), swap(db, z=1)
    xc = swap(copy(zc, [(0, half_rows)]), r=1)
    xya = swap(copy(yab, [(0, half_rows)]), r=1)
    yc = swap(copy(zc, [(0, ext)], yab), y=1)

    order = [
        (half, half_rows), (y0, shard_rows), (zab, ext + half_rows), (yab, ext + half_rows),
        (zab, half_rows), (yab, half_rows), (zc, half_rows), (yc, half_rows),
    ]
    pack = call(
        functools.partial(pack_kernel, [(n, first) for n, (_, first) in enumerate(order)]),
        jax.ShapeDtypeStruct((16, len(order) * width), bf16), "pack_rows", *(x for x, _ in order),
    )
    other_pack = swap(pack, c=1)
    limit, column_slot = call(
        functools.partial(count_kernel, most_rows),
        [jax.ShapeDtypeStruct((2, 128), jnp.int32), jax.ShapeDtypeStruct((1, 2 * count), jnp.int32)],
        "count_rows", context_len, pack, other_pack,
        specs=[SCALARS, WHOLE, WHOLE],
    )
    place = call(
        functools.partial(place_kernel, most_rows), jax.ShapeDtypeStruct((1, 2 * count), jnp.int32), "place_rows",
        draft_rows, other_drafts,
    )

    def starts_of(uses):
        def starts():
            rep, wide = lax.axis_index("rep"), lax.axis_index("wide")
            z, y, c = wide // 4, wide // 2 % 2, wide % 2
            found = []
            for _, _, _, (x_step, z_step, y_step), *further in uses:
                owner_z = (z // 2 + z_step // 2) % 2 * 2 + (z + z_step) % 2
                owner = (owner_z * 2 + (y + y_step) % 2) * 2 + c
                start = owner * shard_rows + (0 if x_step is None else (rep + x_step) % 2 * half_rows)
                found.append(start + sum(further))
            return found

        return starts

    rows = [prompt_hidden, other_prompt, draft_rows, other_drafts]
    stages = [
        ([full, y0], [(0, 0, shard_rows, (None, 0, 0)), (1, 0, shard_rows, (None, 0, 1))]),
        (
            [zab, yab],
            [(0, 0, half_rows, (0, 1, 0)), (0, ext, half_rows, (0, 2, 0)),
             (1, 0, half_rows, (0, 1, 1)), (1, ext, half_rows, (0, 2, 1))],
        ),
        (
            [xab, zc],
            [(0, 0, half_rows, (1, 1, 0)), (0, half_rows, half_rows, (1, 2, 0)), (1, 0, half_rows, (0, 3, 0))],
        ),
        (
            [xc, yc, xya, db, dc],
            [(0, 0, half_rows, (1, 3, 0)), (1, 0, half_rows, (0, 3, 1)), (2, 0, half_rows, (1, 1, 1)),
             (3, 0, half_rows, (1, 2, 1)), (4, 0, half_rows, (1, 3, 1))],
        ),
    ]
    sums = []
    total_rows = 2 * count + 32
    for n, (pieces, uses) in enumerate(stages[:-1]):
        sums = [
            call(
                functools.partial(down_kernel, starts_of(uses), [use[:3] for use in uses], n == 0),
                array(total_rows, f32), "down_rows", *rows, *pieces, *sums, flops=2**26,
            )
        ]

    def finish():
        pieces, uses = stages[-1]
        keep, send = call(
            functools.partial(down_place_kernel, starts_of(uses), [use[:3] for use in uses]),
            [array(2 * count + 8, f32)] * 2, "down_place_rows", *rows, place, *sums, *pieces, flops=2**26,
        )
        came = swap(send, c=1)
        draft_latent, outgoing = call(route_kernel, [array(8, f32), array(2 * count)], "route_rows", keep, came)
        incoming = lax.all_to_all(
            outgoing.reshape(8, 2 * most_rows, width), "wide", split_axis=0, concat_axis=0, tiled=True,
            axis_index_groups=[list(range(c, 16, 2)) for c in range(2)],
        )
        return draft_latent, [incoming.reshape(2 * count, width)]

    return limit, column_slot, finish


def deliver_plain(prompt_hidden, draft_hidden, shard, row_target, context_len, held):
    wide_size = lax.axis_size("wide")
    row_count = prompt_hidden.shape[0]
    slot_count, draft_count, _ = draft_hidden.shape
    latent_width = shard.shape[1]
    most_rows = 2 * ((row_count + wide_size - 1) // wide_size)
    arrived = wide_size * most_rows
    weight = lax.all_gather(shard, "wide", axis=0, tiled=True)
    index = jnp.arange(row_count, dtype=jnp.int32)
    same = (row_target[:, None] == row_target[None, :]) & (index[None, :] < index[:, None])
    rank = jnp.sum(same.astype(jnp.int32), 1)
    front = row_target % slot_count == 0
    place = row_target // slot_count * most_rows + jnp.where(front, rank, most_rows - 1 - rank)
    request = jnp.arange(wide_size * slot_count, dtype=jnp.int32)
    counts = jnp.sum((row_target[None, :] == request[:, None]).astype(jnp.int32), 1)
    counts = lax.all_to_all(counts.reshape(wide_size, slot_count), "wide", split_axis=0, concat_axis=0, tiled=True)
    limit = jnp.broadcast_to((context_len - jnp.sum(counts, 0))[:, None], (slot_count, 128))
    spot = jnp.arange(most_rows, dtype=jnp.int32)[None, :]
    column_slot = jnp.where(
        spot < counts[:, 0:1], 0, jnp.where(spot >= most_rows - counts[:, 1:2], 1, -1)
    ).reshape(1, arrived)

    tile = slot_count * draft_count
    draft_flat = jnp.pad(draft_hidden.reshape(tile, draft_hidden.shape[2]), ((0, 16 - tile), (0, 0)))

    def finish():
        outgoing, draft_latent = pl.pallas_call(
            plain_down_kernel,
            out_shape=[
                jax.ShapeDtypeStruct((arrived, latent_width), jnp.bfloat16),
                jax.ShapeDtypeStruct((slot_count * draft_count, latent_width), jnp.float32),
            ],
            in_specs=[WHOLE] * 4,
            out_specs=[WHOLE] * 2,
            compiler_params=params(24),
            name="down_rows",
        )(place.reshape(1, row_count), prompt_hidden, draft_flat, weight)
        incoming = lax.all_to_all(
            outgoing.reshape(wide_size, most_rows, latent_width), "wide", split_axis=0, concat_axis=0, tiled=True
        )
        return draft_latent, [incoming.reshape(arrived, latent_width)]

    return limit, column_slot, finish


def local(
    prompt_hidden,
    resident_latent,
    row_target,
    row_offset,
    context_len,
    draft_hidden,
    draft_query_heads,
    down_weight,
    key_up_weight,
    value_up_weight,
):
    f32, bf16 = jnp.float32, jnp.bfloat16
    slot_count, span_rows, latent_width = resident_latent.shape
    draft_count = draft_hidden.shape[1]
    rows = QUERY_HEADS * draft_count
    wide_size, row_count = lax.axis_size("wide"), prompt_hidden.shape[0]
    arrived = 2 * ((row_count + wide_size - 1) // wide_size) * wide_size
    window = min(arrived + 128, span_rows)
    hbm = pl.BlockSpec(memory_space=pltpu.HBM)
    stats = [
        jax.ShapeDtypeStruct((slot_count, rows, 1), f32),
        jax.ShapeDtypeStruct((slot_count, rows, 1), f32),
        jax.ShapeDtypeStruct((slot_count, rows, latent_width), f32),
    ]
    turned, peak, total, mixed, edge = pl.pallas_call(
        functools.partial(held_kernel, arrived),
        out_shape=[
            jax.ShapeDtypeStruct((slot_count, 2 * rows, latent_width), bf16),
            *stats,
            jax.ShapeDtypeStruct((slot_count, window, latent_width), bf16),
        ],
        in_specs=[SCALARS, hbm, hbm, hbm],
        out_specs=[WHOLE] * 5,
        scratch_shapes=[
            pltpu.VMEM(draft_query_heads.shape, bf16),
            pltpu.VMEM(key_up_weight.shape, bf16),
            pltpu.VMEM(resident_latent.shape, bf16),
            pltpu.VMEM((slot_count, rows, latent_width), f32),
            pltpu.VMEM((rows, span_rows), f32),
            pltpu.SemaphoreType.DMA((3,)),
        ],
        compiler_params=params(16),
        cost_estimate=pl.CostEstimate(flops=2**31, bytes_accessed=2**21, transcendentals=0),
        name="held_rows",
    )(context_len, *(pltpu.with_memory_space_constraint(x, pltpu.HBM) for x in (draft_query_heads, key_up_weight, resident_latent)))
    known = wide_size == 16 and lax.axis_size("rep") == 2
    limit, column_slot, finish = (deliver if known else deliver_plain)(
        prompt_hidden, draft_hidden, down_weight, row_target, context_len, peak
    )
    draft_latent, incoming = finish()
    peak, total, mixed = pl.pallas_call(
        functools.partial(window_kernel, arrived, span_rows, draft_count),
        out_shape=stats,
        in_specs=[SCALARS] + [WHOLE] * 7,
        out_specs=[WHOLE] * 3,
        compiler_params=params(16),
        cost_estimate=pl.CostEstimate(flops=2**30, bytes_accessed=2**16, transcendentals=0),
        name="window_rows",
    )(context_len, limit, turned, peak, total, mixed, edge, draft_latent)
    return pl.pallas_call(
        late_kernel,
        out_shape=jax.ShapeDtypeStruct((slot_count, draft_count, QUERY_HEADS * HEAD_SIZE), bf16),
        in_specs=[WHOLE] * (6 + len(incoming)),
        out_specs=WHOLE,
        scratch_shapes=[
            pltpu.VMEM((arrived, latent_width), bf16),
            pltpu.VMEM((slot_count, rows, latent_width), bf16),
        ],
        compiler_params=params(16),
        name="late_rows",
    )(column_slot, turned, peak, total, mixed, value_up_weight, *incoming)


def solution(mesh):
    placed = (
        P(("rep", "wide"), None),
        P(("rep", "wide"), None, None),
        P(("rep", "wide")),
        P(("rep", "wide")),
        P(("rep", "wide")),
        P(("rep", "wide"), None, None),
        P(("rep", "wide"), None, None),
        P("wide", None),
        P(),
        P(),
    )
    return jax.shard_map(
        local, mesh=mesh, in_specs=placed, out_specs=P(("rep", "wide"), None, None), check_vma=False
    )
```
